128 devices in a mesh: dp: 16 (over y, x), tensor: 8 (over z, core).
Axes of the slice: x: 4, y: 4, z: 4, core: 2. Of those that a mesh axis runs over, the one named last changes fastest.
Arguments:
- tokens: bfloat16 [16384, 1536], P('dp'), may hold values from -6 to 6
- norm_gain: float32 [1536], replicated, may hold values from 0.5 to 1.5
- in_gate: bfloat16 [1536, 3072], P(None, 'tensor'), may hold values from -0.15625 to 0.15625
- in_value: bfloat16 [1536, 3072], P(None, 'tensor'), may hold values from -0.15625 to 0.15625
- in_state: bfloat16 [1536, 256], replicated, may hold values from -0.15625 to 0.15625
- in_step: bfloat16 [1536, 48], P(None, 'tensor'), may hold values from -0.15625 to 0.15625
- step_bias: float32 [48], P('tensor'), may hold values from -6.5 to -3
- decay_log: float32 [48], P('tensor'), may hold values from 0 to 2.5
- skip_gain: float32 [48], P('tensor'), may hold values from 0.5 to 2
- conv_value_kernel: float32 [4, 3072], P(None, 'tensor'), may hold values from -3 to 3
- conv_value_bias: float32 [3072], P('tensor'), may hold values from -0.5 to 0.5
- conv_state_kernel: float32 [4, 256], replicated, may hold values from -3 to 3
- conv_state_bias: float32 [256], replicated, may hold values from -0.5 to 0.5
- gate_gain: float32 [3072], P('tensor'), may hold values from 0.5 to 1.5
- out_weight: bfloat16 [3072, 1536], P('tensor'), may hold values from -0.109375 to 0.109375
- cotangent: bfloat16 [16384, 1536], P('dp'), may hold values from -6 to 6
Outputs:
- block_output: bfloat16 [16384, 1536], P('dp')
- grad_tokens: bfloat16 [16384, 1536], P('dp')
- grad_norm_gain: float32 [1536], replicated
- grad_in_gate: float32 [1536, 3072], P(None, 'tensor')
- grad_in_value: float32 [1536, 3072], P(None, 'tensor')
- grad_in_state: float32 [1536, 256], replicated
- grad_in_step: float32 [1536, 48], P(None, 'tensor')
- grad_step_bias: float32 [48], P('tensor')
- grad_decay_log: float32 [48], P('tensor')
- grad_skip_gain: float32 [48], P('tensor')
- grad_conv_value_kernel: float32 [4, 3072], P(None, 'tensor')
- grad_conv_value_bias: float32 [3072], P('tensor')
- grad_conv_state_kernel: float32 [4, 256], replicated
- grad_conv_state_bias: float32 [256], replicated
- grad_gate_gain: float32 [3072], P('tensor')
- grad_out_weight: float32 [3072, 1536], P('tensor')
The draws below stay inside these ranges and needn't reach their ends.
All inputs are finite; a program needn't handle non-finite values.
Results may differ from the reference program's by a relative error of at most 0.012.
The reference program's roundings to bfloat16 on the way (of `normed`, `values`, `states` and `outgoing`) count: a program that leaves them out, or rounds other values in their place, can miss the bound.
Values may be sent and summed in bfloat16 or wider, within the bound.
No kernel may reach another device: no remote copies, remote signals or barrier semaphores. Data moves between devices by JAX's collectives and lax.ppermute only.
A program may use at most 128 MiB of HBM per device.

```python
import math
import jax
import jax.numpy as jnp
from jax import lax

D = 1536
HEADS = 48
STATE = 128
CONV = 4
BLOCK = 256
LEN = 1024
INNER = 3072
TOKENS = 16384


def steps_of(own_key, shape, cuts, least, largest):
    def one(axis_at, shards_of):
        draws = jax.random.uniform(jax.random.fold_in(jax.random.fold_in(own_key, 6), axis_at), (shards_of,), jnp.float32, least / len(cuts), largest / len(cuts))
        return jnp.repeat(jnp.exp(draws), shape[axis_at] // shards_of).reshape((-1,) + (1,) * (len(shape) - axis_at - 1))

    loudness = one(*cuts[0])
    for cut in cuts[1:]:
        loudness = loudness * one(*cut)
    return loudness


def bell_draw(rng, extent, scale, limit, cuts=(), dtype=jnp.bfloat16):
    array = scale * jax.random.normal(rng, extent, jnp.float32)
    if cuts:
        array = array * steps_of(rng, extent, cuts, -0.22, 0.18)
    return jnp.clip(array, -limit, limit).astype(dtype)


def setup_inputs(seed: int = 0) -> dict:
    key_list = jax.random.split(jax.random.key(seed), 17)
    tokens = bell_draw(key_list[0], (TOKENS, D), 1.0, 6.0, ((0, 16),))
    norm_gain = jnp.clip(1.0 + 0.1 * jax.random.normal(key_list[1], (D,), jnp.float32), 0.5, 1.5)
    in_gate = bell_draw(key_list[2], (D, INNER), D ** -0.5, 0.15625, ((1, 8),))
    in_value = bell_draw(key_list[3], (D, INNER), D ** -0.5, 0.15625, ((1, 8),))
    in_state = bell_draw(key_list[4], (D, 2 * STATE), D ** -0.5, 0.15625)
    in_step = bell_draw(key_list[5], (D, HEADS), D ** -0.5, 0.15625, ((1, 8),))
    step_bias = jnp.clip(-6.5 + 3.5 * jax.random.uniform(key_list[6], (HEADS,), jnp.float32) ** steps_of(key_list[6], (HEADS,), ((0, 8),), -0.2, 0.2), -6.5, -3.0)
    decay_log = jnp.clip(2.5 * jax.random.uniform(key_list[7], (HEADS,), jnp.float32) ** steps_of(key_list[7], (HEADS,), ((0, 8),), -0.2, 0.2), 0.0, 2.5)
    skip_gain = jnp.clip(0.5 + 1.5 * jax.random.uniform(key_list[8], (HEADS,), jnp.float32) ** steps_of(key_list[8], (HEADS,), ((0, 8),), -0.2, 0.2), 0.5, 2.0)
    conv_value_kernel = bell_draw(key_list[9], (CONV, INNER), CONV ** -0.5, 3.0, ((1, 8),), jnp.float32)
    conv_value_bias = jnp.clip(jax.random.uniform(key_list[10], (INNER,), jnp.float32, -0.5, 0.5) * steps_of(key_list[10], (INNER,), ((0, 8),), -0.4, 0.0), -0.5, 0.5)
    conv_state_kernel = bell_draw(key_list[11], (CONV, 2 * STATE), CONV ** -0.5, 3.0, (), jnp.float32)
    conv_state_bias = jnp.clip(jax.random.uniform(key_list[12], (2 * STATE,), jnp.float32, -0.5, 0.5), -0.5, 0.5)
    gate_gain = jnp.clip(1.0 + 0.1 * jax.random.normal(key_list[13], (INNER,), jnp.float32), 0.5, 1.5)
    out_weight = bell_draw(key_list[14], (INNER, D), INNER ** -0.5, 0.109375, ((0, 8),))
    cotangent = bell_draw(key_list[15], (TOKENS, D), 1.0, 6.0, ((0, 16),))
    return dict(tokens=tokens, norm_gain=norm_gain, in_gate=in_gate, in_value=in_value, in_state=in_state, in_step=in_step, step_bias=step_bias, decay_log=decay_log, skip_gain=skip_gain, conv_value_kernel=conv_value_kernel, conv_value_bias=conv_value_bias, conv_state_kernel=conv_state_kernel, conv_state_bias=conv_state_bias, gate_gain=gate_gain, out_weight=out_weight, cotangent=cotangent)


epsilon = 1e-05
highest = lax.Precision.HIGHEST

@jax.custom_vjp
def low(v):
    return lax.optimization_barrier(v.astype(jnp.bfloat16)).astype(jnp.float32)

@jax.custom_vjp
def low_back(v):
    return v

def low_keep(v):
    return (low(v), None)

def low_pass(kept, grad):
    return (grad,)

def back_keep(v):
    return (v, None)

def back_low(kept, grad):
    return (low(grad),)
low.defvjp(low_keep, low_pass)
low_back.defvjp(back_keep, back_low)

def causal_conv(inputs, kernel, offset_bias):
    padded = jnp.pad(inputs, ((0, 0), (CONV - 1, 0), (0, 0)))
    result = offset_bias + padded[:, 0:LEN, :] * kernel[0]
    for position in range(1, CONV):
        result = result + padded[:, position:position + LEN, :] * kernel[position]
    return result

def conv_silu(seq_count, inputs, kernel, offset_bias):
    shaped = inputs.reshape(seq_count, LEN, inputs.shape[1])
    return jax.nn.silu(causal_conv(shaped, kernel, offset_bias)).reshape(inputs.shape)

def scan_sequence(values, step_sizes, keys_in, reads_in, decay_rates):
    blocks = LEN // BLOCK
    head_count = step_sizes.shape[1]
    causal = jnp.arange(BLOCK)[:, None] >= jnp.arange(BLOCK)[None, :]

    def advance(carried, pieces):
        block_values, block_steps, block_keys, block_reads = pieces
        log_decay = jnp.cumsum(block_steps * decay_rates, axis=0)
        spread = log_decay[:, None, :] - log_decay[None, :, :]
        decays = jnp.where(causal[:, :, None], jnp.exp(jnp.where(causal[:, :, None], spread, 0.0)), 0.0)
        intersections = jnp.dot(block_reads, block_keys.T, precision=highest)
        mixing = intersections[:, :, None] * decays * block_steps[None, :, :]
        inside = jnp.einsum('ijh,jhp->ihp', mixing, block_values, precision=highest)
        carried_in = jnp.einsum('in,hnp->ihp', block_reads, carried, precision=highest) * jnp.exp(log_decay)[:, :, None]
        weights_end = jnp.exp(log_decay[-1][None, :] - log_decay) * block_steps
        updated = carried * jnp.exp(log_decay[-1])[:, None, None] + jnp.einsum('jn,jh,jhp->hnp', block_keys, weights_end, block_values, precision=highest)
        return (updated, inside + carried_in)
    start_state = jnp.zeros((head_count, keys_in.shape[1], values.shape[2]), jnp.float32)
    shaped = (values.reshape(blocks, BLOCK, head_count, values.shape[2]), step_sizes.reshape(blocks, BLOCK, head_count), keys_in.reshape(blocks, BLOCK, keys_in.shape[1]), reads_in.reshape(blocks, BLOCK, reads_in.shape[1]))
    final_state, outputs = lax.scan(jax.checkpoint(advance), start_state, shaped)
    return outputs.reshape(LEN, head_count, values.shape[2])

def mixer_rows(seq_count, values, states, step_pre, gate_pre, step_bias, decay_log, skip_gain):
    head_count = step_bias.shape[0]
    head_width = values.shape[1] // head_count
    step_sizes = jax.nn.softplus(step_pre + step_bias)
    decay_rates = -jnp.exp(decay_log)
    per_head = values.reshape(seq_count, LEN, head_count, head_width)
    keys_in = states[:, :STATE].reshape(seq_count, LEN, STATE)
    reads_in = states[:, STATE:].reshape(seq_count, LEN, STATE)
    scanned = jax.vmap(scan_sequence, in_axes=(0, 0, 0, 0, None))(per_head, step_sizes.reshape(seq_count, LEN, head_count), keys_in, reads_in, decay_rates)
    scanned = scanned + skip_gain[:, None] * per_head
    return scanned.reshape(values.shape) * jax.nn.silu(gate_pre)

def layer_forward(params, token_rows):
    norm_gain, in_gate, in_value, in_state, in_step, step_bias, decay_log, skip_gain, conv_value_kernel, conv_value_bias, conv_state_kernel, conv_state_bias, gate_gain, out_weight = params
    seq_count = token_rows.shape[0] // LEN
    inverse = lax.rsqrt(lax.optimization_barrier(jnp.mean(token_rows * token_rows, axis=1, keepdims=True)) + epsilon)
    normed = low(token_rows * inverse * norm_gain)
    gate_pre = low_back(jnp.dot(normed, in_gate, precision=highest))
    value_pre = low_back(jnp.dot(normed, in_value, precision=highest))
    state_pre = low_back(jnp.dot(normed, in_state, precision=highest))
    step_pre = low_back(jnp.dot(normed, in_step, precision=highest))
    values = low(conv_silu(seq_count, value_pre, conv_value_kernel, conv_value_bias))
    states = low(conv_silu(seq_count, state_pre, conv_state_kernel, conv_state_bias))
    gated_rows = mixer_rows(seq_count, values, states, step_pre, gate_pre, step_bias, decay_log, skip_gain)
    gate_scale = lax.rsqrt(lax.optimization_barrier(jnp.mean(gated_rows * gated_rows, axis=1, keepdims=True)) + epsilon)
    outgoing = low(gated_rows * gate_scale * gate_gain)
    return token_rows + jnp.dot(outgoing, out_weight, precision=highest)

def reference(tokens, norm_gain, in_gate, in_value, in_state, in_step, step_bias, decay_log, skip_gain, conv_value_kernel, conv_value_bias, conv_state_kernel, conv_state_bias, gate_gain, out_weight, cotangent):
    params = tuple((item.astype(jnp.float32) for item in (norm_gain, in_gate, in_value, in_state, in_step, step_bias, decay_log, skip_gain, conv_value_kernel, conv_value_bias, conv_state_kernel, conv_state_bias, gate_gain, out_weight)))
    group_rows = math.gcd(TOKENS // LEN, max(1, 4096 // LEN)) * LEN
    group_count = TOKENS // group_rows
    token_blocks = tokens.astype(jnp.float32).reshape(group_count, group_rows, D)
    cot_blocks = cotangent.astype(jnp.float32).reshape(group_count, group_rows, D)

    def visit_group(running, pieces):
        token_block, cot_block = pieces
        produced, pullback = jax.vjp(layer_forward, params, token_block)
        grad_params, grad_rows = pullback(cot_block)
        running = jax.tree.map(jnp.add, running, grad_params)
        return (running, (produced.astype(jnp.bfloat16), grad_rows.astype(jnp.bfloat16)))
    grad_zeros = jax.tree.map(jnp.zeros_like, params)
    grad_totals, (produced_all, grad_all) = lax.scan(visit_group, grad_zeros, (token_blocks, cot_blocks))
    return (produced_all.reshape(TOKENS, D), grad_all.reshape(TOKENS, D), grad_totals[0], grad_totals[1], grad_totals[2], grad_totals[3], grad_totals[4], grad_totals[5], grad_totals[6], grad_totals[7], grad_totals[8], grad_totals[9], grad_totals[10], grad_totals[11], grad_totals[12], grad_totals[13])
```

```python
from functools import partial

import jax
import jax.numpy as jnp
from jax import lax
from jax.experimental import pallas as pl
from jax.experimental.pallas import tpu as pltpu
from jax.sharding import PartitionSpec as P

STATE = 128
CONV = 4
LEN = 1024
HEAD = 64
Q = 128
ROWS = 256
LANES = 128
HALO = 8

epsilon = 1e-05
f32 = jnp.float32
bf16 = jnp.bfloat16
exact = lax.Precision.HIGHEST
VMEM = 56 * 1024 * 1024


def mm(a, b, precision=None):
    return lax.dot_general(
        a, b, (((1,), (0,)), ((), ())), precision=precision, preferred_element_type=f32
    )


def mm_nt(a, b):
    return lax.dot_general(a, b, (((1,), (1,)), ((), ())), preferred_element_type=f32)


def mm_tn(a, b):
    return lax.dot_general(a, b, (((0,), (0,)), ((), ())), preferred_element_type=f32)


def sigmoid(v):
    return 1.0 / (1.0 + jnp.exp(-v))


def softplus(v):
    return jnp.maximum(v, 0.0) + jnp.log1p(jnp.exp(-jnp.abs(v)))


def iota(shape, axis):
    return lax.broadcasted_iota(jnp.int32, shape, axis)


def column(m, at):
    return jnp.broadcast_to(m[:, at : at + 1], (m.shape[0], LANES))


def low_half(rows):
    return iota((rows, LANES), 1) < HEAD


def expand(m, heads):
    half = low_half(m.shape[0])
    return jnp.concatenate(
        [jnp.where(half, column(m, h), column(m, h + 1)) for h in range(0, heads, 2)], axis=1
    )


def split_heads(pair):
    half = low_half(pair.shape[0])
    zero = jnp.zeros_like(pair)
    return jnp.concatenate([jnp.where(half, pair, zero), jnp.where(half, zero, pair)], axis=0)


def head_sum(m, channels_to_heads):
    high = m.astype(bf16)
    low = (m - high.astype(f32)).astype(bf16)
    return mm(high, channels_to_heads) + mm(low, channels_to_heads)


def forward_kernel(
    heads,
    tokens,
    norm_gain,
    in_gate,
    in_value,
    in_state,
    in_step,
    step_bias,
    rate,
    skip,
    value_kernel,
    value_bias,
    state_kernel,
    state_bias,
    gate_gain,
    out_weight,
    cotangent,
    normed_out,
    gate_out,
    value_out,
    value_conv_out,
    state_out,
    state_conv_out,
    step_out,
    mixed_out,
    back_out,
    memory_out,
    stats_out,
    value_buf,
    state_buf,
    memory,
):
    @pl.when(pl.program_id(0) == 0)
    def _():
        value_buf[0:HALO, :] = jnp.zeros((HALO, value_buf.shape[1]), f32)
        state_buf[0:HALO, :] = jnp.zeros((HALO, state_buf.shape[1]), f32)
        memory[...] = jnp.zeros_like(memory)

    x = tokens[...].astype(f32)
    inverse = lax.rsqrt(jnp.mean(x * x, axis=1, keepdims=True) + epsilon)
    normed = (x * inverse * norm_gain[...]).astype(bf16)
    normed_out[...] = normed
    state_pre = mm(normed, in_state[...])
    value_pre = mm(normed, in_value[...])
    step_pre = mm(normed, in_step[...]) + step_bias[...]
    gate_pre = mm(normed, in_gate[...])
    gate_out[...] = gate_pre
    value_out[...] = value_pre
    state_out[...] = state_pre
    step_out[...] = step_pre

    def conv(buf, pre, kernel, bias):
        buf[HALO:, :] = pre
        result = bias[...] + buf[HALO - 3 : HALO - 3 + ROWS, :] * kernel[0:1, :]
        for k in range(1, CONV):
            result = result + buf[HALO - 3 + k : HALO - 3 + k + ROWS, :] * kernel[k : k + 1, :]
        buf[0:HALO, :] = buf[ROWS : ROWS + HALO, :]
        return result

    value_conv = conv(value_buf, value_pre, value_kernel, value_bias)
    value_conv_out[...] = value_conv
    values = (value_conv * sigmoid(value_conv)).astype(bf16)
    state_conv = conv(state_buf, state_pre, state_kernel, state_bias)
    state_conv_out[...] = state_conv
    states = (state_conv * sigmoid(state_conv)).astype(bf16)
    step = softplus(step_pre)
    log_step = step * rate[...]

    causal = iota((Q, Q), 0) >= iota((Q, Q), 1)
    tri = jnp.where(causal, 1.0, 0.0).astype(f32)
    mixed_parts = []
    for part in range(ROWS // Q):
        rows = slice(part * Q, (part + 1) * Q)
        b = states[rows, :STATE]
        c = states[rows, STATE:]
        v = values[rows, :].astype(f32)
        dt = step[rows, :]
        decay = mm(tri, log_step[rows, :], precision=exact)
        decay_t = decay.T
        wide = expand(decay, heads)
        dt_wide = expand(dt, heads)
        grown = jnp.exp(wide)
        scaled = v * dt_wide
        scaled_low = scaled.astype(bf16)
        cb = mm_nt(c, b)
        held = memory[...]
        held_low = held.astype(bf16)
        memory_out[part] = held_low
        y = mm(c, held_low) * grown + skip[...] * v
        inside = []
        for h in range(0, heads, 2):
            blocks = []
            for at in (h, h + 1):
                gap = column(decay, at) - decay_t[at : at + 1, :]
                blocks.append((cb * jnp.exp(jnp.where(causal, gap, -1e30))).astype(bf16))
            pair = scaled_low[:, h * HEAD : (h + 2) * HEAD]
            inside.append(mm(jnp.concatenate(blocks, axis=1), split_heads(pair)))
        mixed_parts.append(y + jnp.concatenate(inside, axis=1))
        ended = (scaled * jnp.exp(wide[Q - 1 : Q, :] - wide)).astype(bf16)
        memory[...] = held * grown[Q - 1 : Q, :] + mm_tn(b, ended)

    mixed = jnp.concatenate(mixed_parts, axis=0)
    mixed_out[...] = mixed
    gated = mixed * gate_pre * sigmoid(gate_pre)
    back = mm_nt(cotangent[...], out_weight[...])
    back_out[...] = back
    squares = jnp.sum(gated * gated, axis=1, keepdims=True)
    moment = jnp.sum(back * gate_gain[...] * gated, axis=1, keepdims=True)
    lane = iota((ROWS, LANES), 1)
    both = jnp.where(lane == 0, squares, jnp.where(lane == 1, moment, 0.0))
    stats_out[...] = both.T[0:8, :]


def stats_columns(stats, inner):
    padded = jnp.concatenate([stats, jnp.zeros((LANES - 8, stats.shape[1]), f32)], axis=0).T
    scale = lax.rsqrt(padded[:, 0:1] / inner + epsilon)
    return scale, padded[:, 1:2] / inner


def out_kernel(inner, stats, gate_pre, mixed, gate_gain, out_weight, outgoing_out, part_out):
    scale, _ = stats_columns(stats[...], inner)
    pre = gate_pre[...]
    gated = mixed[...] * pre * sigmoid(pre)
    outgoing = (gated * scale * gate_gain[...]).astype(bf16)
    outgoing_out[...] = outgoing
    part_out[...] = mm(outgoing, out_weight[...]).astype(bf16)


def backward_kernel(
    heads,
    inner,
    stats,
    tokens,
    gate,
    value,
    value_conv,
    state,
    state_conv,
    step_in,
    mixed_in,
    back_in,
    memory_in,
    rate,
    skip,
    value_kernel,
    state_kernel,
    gate_gain,
    in_gate,
    in_value,
    in_state,
    in_step,
    channels_to_heads,
    part_out,
    gate_out,
    value_out,
    state_out,
    step_out,
    norm_gain_out,
    gate_gain_out,
    value_taps_out,
    state_taps_out,
    skip_out,
    steps_out,
    value_buf,
    state_buf,
    adjoint,
):
    @pl.when(pl.program_id(0) == 0)
    def _():
        value_buf[ROWS:, :] = jnp.zeros((HALO, value_buf.shape[1]), f32)
        state_buf[ROWS:, :] = jnp.zeros((HALO, state_buf.shape[1]), f32)
        adjoint[...] = jnp.zeros_like(adjoint)
        for ref in (norm_gain_out, gate_gain_out, value_taps_out, state_taps_out, skip_out, steps_out):
            ref[...] = jnp.zeros_like(ref)

    def add_row(ref, at, rows):
        ref[at : at + 1, :] += jnp.sum(rows, axis=0, keepdims=True)

    scale, moment = stats_columns(stats[...], inner)
    mixed = mixed_in[...]
    back = back_in[...]
    pre = gate[...]
    bent = sigmoid(pre)
    silu = pre * bent
    gated = mixed * silu
    add_row(gate_gain_out, 0, back * gated * scale)
    grad_gated = scale * (back * gate_gain[...]) - gated * (scale * scale * scale * moment)
    grad_mixed = grad_gated * silu
    round_gate = (grad_gated * mixed * (bent * (1.0 + pre * (1.0 - bent)))).astype(bf16)
    gate_out[...] = round_gate

    value_at = value_conv[...]
    value_bent = sigmoid(value_at)
    values = (value_at * value_bent).astype(bf16)
    state_at = state_conv[...]
    state_bent = sigmoid(state_at)
    states = (state_at * state_bent).astype(bf16)
    step_pre = step_in[...]
    step = softplus(step_pre)
    log_step = step * rate[...]

    ahead = iota((Q, Q), 1) >= iota((Q, Q), 0)
    tri = jnp.where(iota((Q, Q), 0) >= iota((Q, Q), 1), 1.0, 0.0).astype(f32)
    tri_up = jnp.where(ahead, 1.0, 0.0).astype(f32)
    tri_strict = jnp.where(iota((Q, Q), 0) > iota((Q, Q), 1), 1.0, 0.0).astype(f32)
    lane = iota((Q, LANES), 1)
    row8 = iota((8, Q), 0)
    parts = ROWS // Q
    grad_value_parts = [None] * parts
    grad_state_parts = [None] * parts
    grad_step_parts = [None] * parts
    for part in reversed(range(parts)):
        rows = slice(part * Q, (part + 1) * Q)
        b = states[rows, :STATE]
        c = states[rows, STATE:]
        v_low = values[rows, :]
        v = v_low.astype(f32)
        dt = step[rows, :]
        dy = grad_mixed[rows, :]
        dy_low = dy.astype(bf16)
        decay = mm(tri, log_step[rows, :], precision=exact)
        decay_t = decay.T
        wide = expand(decay, heads)
        dt_wide = expand(dt, heads)
        grown = jnp.exp(wide)
        to_end = jnp.exp(wide[Q - 1 : Q, :] - wide)
        held = memory_in[part]
        later = adjoint[...]
        later_low = later.astype(bf16)
        bd = mm(b, later_low)
        cs = mm(c, held)
        bc = mm_nt(b, c)
        dy_grown = dy * grown
        dy_grown_low = dy_grown.astype(bf16)
        at_end = bd * to_end
        inside = []
        grad_bc = jnp.zeros((Q, Q), f32)
        direct = jnp.zeros((Q, LANES), f32)
        row_sums = jnp.zeros((8, Q), f32)
        for h in range(0, heads, 2):
            lanes = slice(h * HEAD, (h + 2) * HEAD)
            v_split = split_heads(v_low[:, lanes])
            grad_pair = mm_nt(v_split, dy_low[:, lanes])
            blocks = []
            for at in (h, h + 1):
                gap = decay_t[at : at + 1, :] - column(decay, at)
                fall = jnp.exp(jnp.where(ahead, gap, -1e30))
                grad_fall = grad_pair[(at - h) * Q : (at - h + 1) * Q, :] * fall
                direct += jnp.where(lane == at, jnp.sum(grad_fall * bc, axis=1, keepdims=True), 0.0)
                grad_one = grad_fall * column(dt, at)
                grad_bc += grad_one
                row_sums += jnp.where(
                    row8 == at, jnp.sum(grad_one * bc, axis=0, keepdims=True), 0.0
                )
                blocks.append((bc * fall).astype(bf16))
            inside.append(mm(jnp.concatenate(blocks, axis=1), split_heads(dy_low[:, lanes])))
        grad_value_parts[part] = (
            dt_wide * (jnp.concatenate(inside, axis=1) + at_end) + skip[...] * dy
        )
        add_row(skip_out, 0, dy * v)
        grown_sum = head_sum(dy_grown * cs, channels_to_heads[...])
        end_sum = head_sum(at_end * v, channels_to_heads[...])
        constant = head_sum(
            grown[Q - 1 : Q, :] * jnp.sum(held.astype(f32) * later, axis=0, keepdims=True),
            channels_to_heads[...],
        )
        row_t = jnp.concatenate([row_sums, jnp.zeros((LANES - 8, Q), f32)], axis=0).T
        grad_log = (
            mm(tri_up, row_t - direct * dt + grown_sum, precision=exact)
            + mm(tri_strict, end_sum * dt, precision=exact)
            + constant
        )
        grad_step = direct + end_sum + rate[...] * grad_log
        grad_step = grad_step * sigmoid(step_pre[rows, :])
        grad_step_parts[part] = grad_step
        add_row(steps_out, 0, grad_step)
        add_row(steps_out, 1, dt * grad_log * rate[...])
        grad_bc_low = grad_bc.astype(bf16)
        grad_b = mm(grad_bc_low, c) + mm_nt((v * dt_wide * to_end).astype(bf16), later_low)
        grad_c = mm_tn(grad_bc_low, b) + mm_nt(dy_grown_low, held)
        grad_state_parts[part] = jnp.concatenate([grad_b, grad_c], axis=1)
        adjoint[...] = later * grown[Q - 1 : Q, :] + mm_tn(c, dy_grown_low)

    def conv_back(buf, grad, at, bent, pre, kernel, taps_out):
        buf[0:ROWS, :] = grad * (bent * (1.0 + at * (1.0 - bent)))
        result = None
        for k in range(CONV):
            moved = buf[3 - k : 3 - k + ROWS, :]
            term = moved * kernel[k : k + 1, :]
            result = term if result is None else result + term
            add_row(taps_out, k, pre * moved)
        add_row(taps_out, CONV, buf[0:ROWS, :])
        buf[ROWS:, :] = buf[0:HALO, :]
        return result.astype(bf16)

    round_value = conv_back(
        value_buf,
        jnp.concatenate(grad_value_parts, axis=0),
        value_at,
        value_bent,
        value[...],
        value_kernel,
        value_taps_out,
    )
    round_state = conv_back(
        state_buf,
        jnp.concatenate(grad_state_parts, axis=0),
        state_at,
        state_bent,
        state[...],
        state_kernel,
        state_taps_out,
    )
    round_step = jnp.concatenate(grad_step_parts, axis=0).astype(bf16)
    value_out[...] = round_value
    state_out[...] = round_state
    step_out[...] = round_step
    total = (
        mm_nt(round_gate, in_gate[...])
        + mm_nt(round_value, in_value[...])
        + mm_nt(round_state, in_state[...])
        + mm_nt(round_step, in_step[...])
    )
    part_out[...] = total.astype(bf16)
    x = tokens[...].astype(f32)
    inverse = lax.rsqrt(jnp.mean(x * x, axis=1, keepdims=True) + epsilon)
    add_row(norm_gain_out, 0, total * (x * inverse))


def whole(array):
    zeros = (0,) * array.ndim
    return pl.BlockSpec(array.shape, lambda i: zeros)


def by_rows(width, steps=None, rows=ROWS):
    if steps is None:
        return pl.BlockSpec((rows, width), lambda i: (i, 0))
    return pl.BlockSpec((rows, width), lambda i: (steps - 1 - i, 0))


def swap_core(x):
    return lax.ppermute(x, "tensor", [(i, i ^ 1) for i in range(8)])


def move_z(x, k):
    return lax.ppermute(x, "tensor", [(i, (i + 2 * k) % 8) for i in range(8)])


def pick(x, at):
    return lax.dynamic_index_in_dim(x, at, 0, keepdims=False)


def add_over_tensor(x):
    for bit in (1, 2, 4):
        x = x + lax.ppermute(x, "tensor", [(i, i ^ bit) for i in range(8)])
    return x


def scatter_over_tensor(x):
    me = lax.axis_index("tensor")
    z, core = me // 2, me % 2
    blocks = x.reshape((4, 2) + (x.shape[0] // 8,) + x.shape[1:])
    mine = lax.dynamic_index_in_dim(blocks, core, 1, keepdims=False)
    other = lax.dynamic_index_in_dim(blocks, 1 - core, 1, keepdims=False)
    both = (mine.astype(f32) + swap_core(other).astype(f32)).astype(bf16)
    total = pick(both, z).astype(f32)
    for k in (1, 2, 3):
        total = total + move_z(pick(both, (z + k) % 4), k).astype(f32)
    return total


def scatter_over_dp(x):
    got = lax.all_to_all(x, "dp", 0, 0, tiled=True)
    return jnp.sum(got.astype(f32), axis=0)


def gather_over_dp(x):
    return lax.all_to_all(jnp.broadcast_to(x[None], (lax.axis_size("dp"),) + x.shape), "dp", 0, 0, tiled=True)


def two_parts(x):
    high = x.astype(bf16)
    return high, (x - high.astype(f32)).astype(bf16)


def on_device(
    tokens,
    norm_gain,
    in_gate,
    in_value,
    in_state,
    in_step,
    step_bias,
    decay_log,
    skip_gain,
    conv_value_kernel,
    conv_value_bias,
    conv_state_kernel,
    conv_state_bias,
    gate_gain,
    out_weight,
    cotangent,
):
    features = tokens.shape[1]
    channels = in_gate.shape[1]
    heads = step_bias.shape[0]
    inner = channels * lax.axis_size("tensor")
    steps = LEN // ROWS
    parts = ROWS // Q
    dp = lax.axis_size("dp")
    me = lax.axis_index("tensor")

    pad_heads = lambda a: jnp.pad(a[None, :], ((0, 0), (0, LANES - heads)))
    step_weight = jnp.pad(in_step, ((0, 0), (0, LANES - heads)))
    rate = pad_heads(-jnp.exp(decay_log))
    skip = jnp.repeat(skip_gain, HEAD)[None, :]
    gain_row = gate_gain[None, :]
    sds = jax.ShapeDtypeStruct
    params = pltpu.CompilerParams(
        dimension_semantics=("arbitrary",), vmem_limit_bytes=VMEM
    )

    operands = (
        tokens,
        norm_gain[None, :],
        in_gate,
        in_value,
        in_state,
        step_weight,
        pad_heads(step_bias),
        rate,
        skip,
        conv_value_kernel,
        conv_value_bias[None, :],
        conv_state_kernel,
        conv_state_bias[None, :],
        gain_row,
        out_weight,
        cotangent,
    )
    (
        normed,
        gate_pre,
        value_pre,
        value_conv,
        state_pre,
        state_conv,
        step_pre,
        mixed,
        back,
        memories,
        stats,
    ) = pl.pallas_call(
        partial(forward_kernel, heads),
        grid=(steps,),
        in_specs=[by_rows(features)]
        + [whole(a) for a in operands[1:-1]]
        + [by_rows(features)],
        out_specs=[
            by_rows(features),
            by_rows(channels),
            by_rows(channels),
            by_rows(channels),
            by_rows(2 * STATE),
            by_rows(2 * STATE),
            by_rows(LANES),
            by_rows(channels),
            by_rows(channels),
            pl.BlockSpec((parts, STATE, channels), lambda i: (i, 0, 0)),
            pl.BlockSpec((8, ROWS), lambda i: (0, i)),
        ],
        out_shape=[
            sds((LEN, features), bf16),
            sds((LEN, channels), f32),
            sds((LEN, channels), f32),
            sds((LEN, channels), f32),
            sds((LEN, 2 * STATE), f32),
            sds((LEN, 2 * STATE), f32),
            sds((LEN, LANES), f32),
            sds((LEN, channels), f32),
            sds((LEN, channels), f32),
            sds((LEN // Q, STATE, channels), bf16),
            sds((8, LEN), f32),
        ],
        scratch_shapes=[
            pltpu.VMEM((ROWS + HALO, channels), f32),
            pltpu.VMEM((ROWS + HALO, 2 * STATE), f32),
            pltpu.VMEM((STATE, channels), f32),
        ],
        compiler_params=params,
        cost_estimate=pl.CostEstimate(
            flops=5_000_000_000, bytes_accessed=30_000_000, transcendentals=4_000_000
        ),
    )(*operands)

    stats = add_over_tensor(stats)

    outgoing, part = pl.pallas_call(
        partial(out_kernel, inner),
        grid=(steps,),
        in_specs=[
            pl.BlockSpec((8, ROWS), lambda i: (0, i)),
            by_rows(channels),
            by_rows(channels),
            whole(gain_row),
            whole(out_weight),
        ],
        out_specs=[by_rows(channels), by_rows(features)],
        out_shape=[sds((LEN, channels), bf16), sds((LEN, features), bf16)],
        compiler_params=params,
        cost_estimate=pl.CostEstimate(
            flops=1_200_000_000, bytes_accessed=9_000_000, transcendentals=400_000
        ),
    )(stats, gate_pre, mixed, gain_row, out_weight)

    own = lambda a: lax.dynamic_slice_in_dim(a, me * (LEN // 8), LEN // 8, 0)
    own_tokens = own(tokens).astype(f32)
    own_output = (own_tokens + scatter_over_tensor(part)).astype(bf16)
    block_output = lax.all_gather(own_output, "tensor", tiled=True)
    grad_out_weight = mm_tn(outgoing, cotangent)

    channels_to_heads = (
        jnp.arange(channels)[:, None] // HEAD == jnp.arange(LANES)[None, :]
    ).astype(bf16)
    operands = (
        stats,
        tokens,
        gate_pre,
        value_pre,
        value_conv,
        state_pre,
        state_conv,
        step_pre,
        mixed,
        back,
        memories,
        rate,
        skip,
        conv_value_kernel,
        conv_state_kernel,
        gain_row,
        in_gate,
        in_value,
        in_state,
        step_weight,
        channels_to_heads,
    )
    back_rows = partial(by_rows, steps=steps)
    row_sum = lambda rows, width: pl.BlockSpec((rows, width), lambda i: (0, 0))
    (
        grad_part,
        round_gate,
        round_value,
        round_state,
        round_step,
        norm_gain_part,
        gate_gain_part,
        value_taps,
        state_taps,
        skip_part,
        step_parts,
    ) = pl.pallas_call(
        partial(backward_kernel, heads, inner),
        grid=(steps,),
        in_specs=[
            pl.BlockSpec((8, ROWS), lambda i: (0, steps - 1 - i)),
            back_rows(features),
            back_rows(channels),
            back_rows(channels),
            back_rows(channels),
            back_rows(2 * STATE),
            back_rows(2 * STATE),
            back_rows(LANES),
            back_rows(channels),
            back_rows(channels),
            pl.BlockSpec((parts, STATE, channels), lambda i: (steps - 1 - i, 0, 0)),
        ]
        + [whole(a) for a in operands[11:]],
        out_specs=[
            back_rows(features),
            back_rows(channels),
            back_rows(channels),
            back_rows(2 * STATE),
            back_rows(LANES),
            row_sum(8, features),
            row_sum(8, channels),
            row_sum(8, channels),
            row_sum(8, 2 * STATE),
            row_sum(8, channels),
            row_sum(8, LANES),
        ],
        out_shape=[
            sds((LEN, features), bf16),
            sds((LEN, channels), bf16),
            sds((LEN, channels), bf16),
            sds((LEN, 2 * STATE), bf16),
            sds((LEN, LANES), bf16),
            sds((8, features), f32),
            sds((8, channels), f32),
            sds((8, channels), f32),
            sds((8, 2 * STATE), f32),
            sds((8, channels), f32),
            sds((8, LANES), f32),
        ],
        scratch_shapes=[
            pltpu.VMEM((ROWS + HALO, channels), f32),
            pltpu.VMEM((ROWS + HALO, 2 * STATE), f32),
            pltpu.VMEM((STATE, channels), f32),
        ],
        compiler_params=params,
        cost_estimate=pl.CostEstimate(
            flops=6_000_000_000, bytes_accessed=30_000_000, transcendentals=4_000_000
        ),
    )(*operands)

    grad_normed = scatter_over_tensor(grad_part)
    inverse = lax.rsqrt(jnp.mean(own_tokens * own_tokens, axis=1, keepdims=True) + epsilon)
    scaled = grad_normed * norm_gain
    moment = jnp.mean(scaled * own_tokens, axis=1, keepdims=True)
    own_grad = own(cotangent).astype(f32) + inverse * scaled - own_tokens * inverse**3 * moment
    grad_tokens = lax.all_gather(own_grad.astype(bf16), "tensor", tiled=True)

    grad_in_gate = mm_tn(normed, round_gate)
    grad_in_value = mm_tn(normed, round_value)
    grad_in_state = mm_tn(normed, round_state)
    grad_in_step = mm_tn(normed, round_step)[:, :heads]

    first = scatter_over_dp(
        jnp.concatenate(
            [
                grad_out_weight.astype(bf16).reshape(dp, -1, channels),
                grad_in_gate.astype(bf16).reshape(dp, -1, channels),
            ],
            axis=1,
        )
    )
    first = gather_over_dp(first.astype(bf16)).astype(f32)
    grad_out_weight, grad_in_gate = jnp.split(first, 2, axis=1)
    grad_out_weight = grad_out_weight.reshape(channels, features)
    grad_in_gate = grad_in_gate.reshape(features, channels)

    state_share = scatter_over_tensor(grad_in_state.astype(bf16))
    state_share = state_share.reshape(dp, -1, channels).astype(bf16)

    def as_rows(*arrays):
        flat = jnp.concatenate([a.reshape(-1) for a in arrays])
        return jnp.pad(flat, (0, -flat.shape[0] % channels)).reshape(-1, channels)

    head_rows = as_rows(step_parts[0, :heads], step_parts[1, :heads], skip_part[0])
    small = jnp.concatenate(
        [
            as_rows(grad_in_step),
            head_rows,
            value_taps[: CONV + 1],
            gate_gain_part[:1],
            as_rows(norm_gain_part[0], state_taps[: CONV + 1]),
        ],
        axis=0,
    )
    step_rows = features * heads // channels
    small = jnp.pad(small, ((0, 64 - small.shape[0]), (0, 0)))
    small = small.reshape(dp, -1, channels)
    small_rows = small.shape[1]
    second = scatter_over_dp(
        jnp.concatenate(
            (grad_in_value.astype(bf16).reshape(dp, -1, channels),)
            + two_parts(small)
            + (state_share,),
            axis=1,
        )
    )
    value_rows = features // dp
    state_at = value_rows + 2 * small_rows
    small = second[value_rows : value_rows + small_rows] + second[value_rows + small_rows : state_at]
    second = gather_over_dp(
        jnp.concatenate(
            (second[:value_rows].astype(bf16),)
            + two_parts(small)
            + (second[state_at:].astype(bf16),),
            axis=0,
        )
    )
    grad_in_value = second[:, :value_rows].reshape(features, channels).astype(f32)
    small = second[:, value_rows : value_rows + small_rows].astype(f32)
    small = small + second[:, value_rows + small_rows : state_at].astype(f32)
    small = small.reshape(64, channels)
    state_share = second[:, state_at:].reshape(features // 8, 2 * STATE)
    grad_in_state = lax.all_gather(state_share, "tensor", tiled=True).astype(f32)

    grad_in_step = small[:step_rows].reshape(features, heads)
    at = step_rows
    head_flat = small[at : at + 2].reshape(-1)
    grad_step_bias = head_flat[:heads]
    grad_decay_log = head_flat[heads : 2 * heads]
    grad_skip_gain = head_flat[2 * heads : 2 * heads + channels].reshape(heads, HEAD).sum(axis=1)
    at += 2
    grad_conv_value_kernel = small[at : at + CONV]
    grad_conv_value_bias = small[at + CONV]
    grad_gate_gain = small[at + CONV + 1]
    at += CONV + 2
    shared = add_over_tensor(small[at : at + 8]).reshape(-1)
    grad_norm_gain = shared[:features]
    state_flat = shared[features : features + (CONV + 1) * 2 * STATE].reshape(CONV + 1, 2 * STATE)
    return (
        block_output,
        grad_tokens,
        grad_norm_gain,
        grad_in_gate,
        grad_in_value,
        grad_in_state,
        grad_in_step,
        grad_step_bias,
        grad_decay_log,
        grad_skip_gain,
        grad_conv_value_kernel,
        grad_conv_value_bias,
        state_flat[:CONV],
        state_flat[CONV],
        grad_gate_gain,
        grad_out_weight,
    )


def solution(mesh):
    placed = (
        P("dp", None),
        P(),
        P(None, "tensor"),
        P(None, "tensor"),
        P(),
        P(None, "tensor"),
        P("tensor"),
        P("tensor"),
        P("tensor"),
        P(None, "tensor"),
        P("tensor"),
        P(),
        P(),
        P("tensor"),
        P("tensor", None),
        P("dp", None),
    )
    return jax.shard_map(
        on_device,
        mesh=mesh,
        in_specs=placed,
        out_specs=(
            P("dp", None),
            P("dp", None),
            P(),
            P(None, "tensor"),
            P(None, "tensor"),
            P(),
            P(None, "tensor"),
            P("tensor"),
            P("tensor"),
            P("tensor"),
            P(None, "tensor"),
            P("tensor"),
            P(),
            P(),
            P("tensor"),
            P("tensor", None),
        ),
        check_vma=False,
    )
```

```python
import math
from functools import partial

import jax
import jax.numpy as jnp
from jax import lax
from jax.experimental import pallas as pl
from jax.experimental.pallas import tpu as pltpu
from jax.sharding import PartitionSpec as P

STATE = 128
CONV = 4
LEN = 1024
HEAD = 64
Q = 128
ROWS = 256
LANES = 128
HALO = 8
LOCAL = 32
SHARED = 16

epsilon = 1e-05
f32 = jnp.float32
bf16 = jnp.bfloat16
exact = lax.Precision.HIGHEST
VMEM = 60 * 1024 * 1024


def mm(a, b, precision=None):
    return lax.dot_general(
        a, b, (((1,), (0,)), ((), ())), precision=precision, preferred_element_type=f32
    )


def mm_nt(a, b):
    return lax.dot_general(a, b, (((1,), (1,)), ((), ())), preferred_element_type=f32)


def mm_tn(a, b):
    return lax.dot_general(a, b, (((0,), (0,)), ((), ())), preferred_element_type=f32)


def sigmoid(v):
    return 1.0 / (1.0 + jnp.exp(-v))


def softplus(v):
    return jnp.maximum(v, 0.0) + jnp.log1p(jnp.exp(-jnp.abs(v)))


def iota(shape, axis):
    return lax.broadcasted_iota(jnp.int32, shape, axis)


def column(m, at):
    return jnp.broadcast_to(m[:, at : at + 1], (m.shape[0], LANES))


def low_half(rows):
    return iota((rows, LANES), 1) < HEAD


def expand(m, heads):
    half = low_half(m.shape[0])
    return jnp.concatenate(
        [jnp.where(half, column(m, h), column(m, h + 1)) for h in range(0, heads, 2)], axis=1
    )


def split_heads(pair):
    half = low_half(pair.shape[0])
    zero = jnp.zeros_like(pair)
    return jnp.concatenate([jnp.where(half, pair, zero), jnp.where(half, zero, pair)], axis=0)


def head_sum(m, channels_to_heads):
    high = m.astype(bf16)
    low = (m - high.astype(f32)).astype(bf16)
    return mm(high, channels_to_heads) + mm(low, channels_to_heads)


def head_row(scalars, heads):
    lane = iota((1, LANES), 1)
    row = jnp.zeros((1, LANES), f32)
    for h in range(heads):
        row = jnp.where(lane == h, scalars[h], row)
    return row


def rate_row(decay_log, heads):
    return jnp.where(iota((1, LANES), 1) < heads, -jnp.exp(head_row(decay_log, heads)), 0.0)


def channel_row(scalars, heads):
    half = low_half(1)
    return jnp.concatenate(
        [jnp.where(half, scalars[h], scalars[h + 1]) for h in range(0, heads, 2)], axis=1
    )


def all_lanes(rows):
    below = jnp.zeros((LANES - rows.shape[0], rows.shape[1]), rows.dtype)
    return jnp.concatenate([rows, below], axis=0)


def row_of(ref):
    return ref[...].reshape(1, ref.shape[0])


def forward_kernel(
    heads,
    tokens,
    norm_gain,
    in_gate,
    in_value,
    in_state,
    in_step,
    step_bias,
    decay_log,
    skip_gain,
    value_kernel,
    value_bias,
    state_kernel,
    state_bias,
    gate_gain,
    out_weight,
    cotangent,
    normed_out,
    gate_out,
    value_out,
    value_conv_out,
    state_out,
    state_conv_out,
    step_out,
    mixed_out,
    back_out,
    part_out,
    memory_out,
    stats_out,
    value_buf,
    state_buf,
    memory,
):
    @pl.when(pl.program_id(0) == 0)
    def _():
        value_buf[0:HALO, :] = jnp.zeros((HALO, value_buf.shape[1]), f32)
        state_buf[0:HALO, :] = jnp.zeros((HALO, state_buf.shape[1]), f32)
        memory[...] = jnp.zeros_like(memory)

    x = tokens[...].astype(f32)
    inverse = lax.rsqrt(jnp.mean(x * x, axis=1, keepdims=True) + epsilon)
    normed = (x * inverse * row_of(norm_gain)).astype(bf16)
    normed_out[...] = normed
    state_pre = mm(normed, in_state[...])
    value_pre = mm(normed, in_value[...])
    step_pre = mm_nt(normed, all_lanes(in_step[...])) + head_row(step_bias, heads)
    gate_pre = mm(normed, in_gate[...])
    gate_out[...] = gate_pre
    value_out[...] = value_pre
    state_out[...] = state_pre
    step_out[...] = step_pre

    def conv(buf, pre, kernel, bias):
        buf[HALO:, :] = pre
        result = row_of(bias) + buf[HALO - 3 : HALO - 3 + ROWS, :] * kernel[0:1, :]
        for k in range(1, CONV):
            result = result + buf[HALO - 3 + k : HALO - 3 + k + ROWS, :] * kernel[k : k + 1, :]
        buf[0:HALO, :] = buf[ROWS : ROWS + HALO, :]
        return result

    value_conv = conv(value_buf, value_pre, value_kernel, value_bias)
    value_conv_out[...] = value_conv
    values = (value_conv * sigmoid(value_conv)).astype(bf16)
    state_conv = conv(state_buf, state_pre, state_kernel, state_bias)
    state_conv_out[...] = state_conv
    states = (state_conv * sigmoid(state_conv)).astype(bf16)
    step = softplus(step_pre)
    log_step = step * rate_row(decay_log, heads)
    skip = channel_row(skip_gain, heads)

    causal = iota((Q, Q), 0) >= iota((Q, Q), 1)
    tri = jnp.where(causal, 1.0, 0.0).astype(f32)
    mixed_parts = []
    for part in range(ROWS // Q):
        rows = slice(part * Q, (part + 1) * Q)
        b = states[rows, :STATE]
        c = states[rows, STATE:]
        v = values[rows, :].astype(f32)
        dt = step[rows, :]
        decay = mm(tri, log_step[rows, :], precision=exact)
        decay_t = decay.T
        wide = expand(decay, heads)
        dt_wide = expand(dt, heads)
        grown = jnp.exp(wide)
        scaled = v * dt_wide
        scaled_low = scaled.astype(bf16)
        cb = mm_nt(c, b)
        held = memory[...]
        held_low = held.astype(bf16)
        memory_out[part] = held_low
        y = mm(c, held_low) * grown + skip * v
        inside = []
        for h in range(0, heads, 2):
            blocks = []
            for at in (h, h + 1):
                gap = column(decay, at) - decay_t[at : at + 1, :]
                blocks.append((cb * jnp.exp(jnp.where(causal, gap, -1e30))).astype(bf16))
            pair = scaled_low[:, h * HEAD : (h + 2) * HEAD]
            inside.append(mm(jnp.concatenate(blocks, axis=1), split_heads(pair)))
        mixed_parts.append(y + jnp.concatenate(inside, axis=1))
        ended = (scaled * jnp.exp(wide[Q - 1 : Q, :] - wide)).astype(bf16)
        memory[...] = held * grown[Q - 1 : Q, :] + mm_tn(b, ended)

    mixed = jnp.concatenate(mixed_parts, axis=0)
    mixed_out[...] = mixed
    gated = mixed * gate_pre * sigmoid(gate_pre)
    back = mm_nt(cotangent[...], out_weight[...])
    back_out[...] = back
    gained = gated * row_of(gate_gain)
    part_out[...] = mm(gained.astype(bf16), out_weight[...]).astype(bf16)
    squares = jnp.sum(gated * gated, axis=1, keepdims=True)
    moment = jnp.sum(back * gained, axis=1, keepdims=True)
    lane = iota((ROWS, LANES), 1)
    both = jnp.where(lane == 0, squares, jnp.where(lane == 1, moment, 0.0))
    stats_out[...] = both.T[0:8, :]


def stats_columns(stats, inner):
    padded = jnp.concatenate([stats, jnp.zeros((LANES - 8, stats.shape[1]), f32)], axis=0).T
    scale = lax.rsqrt(padded[:, 0:1] / inner + epsilon)
    return scale, padded[:, 1:2] / inner


def add_row(ref, at, rows):
    ref[at : at + 1, :] += jnp.sum(rows, axis=0, keepdims=True)


def backward_kernel(
    heads,
    inner,
    steps,
    side,
    place,
    stats,
    normed,
    cotangent,
    gate,
    mixed_in,
    back_in,
    value,
    value_conv,
    state,
    state_conv,
    step_in,
    memory_in,
    gate_gain,
    decay_log,
    skip_gain,
    value_kernel,
    state_kernel,
    gate_out,
    value_out,
    state_out,
    step_out,
    *refs,
):
    pieces_out = refs[:side]
    (
        value_buf,
        state_buf,
        adjoint,
        weight_total,
        out_total,
        step_total,
        gate_gain_out,
        value_taps_out,
        state_taps_out,
        skip_out,
        steps_out,
        local_rows,
        shared_rows,
        slabs,
    ) = refs[side:]

    @pl.when(pl.program_id(0) == 0)
    def _():
        value_buf[ROWS:, :] = jnp.zeros((HALO, value_buf.shape[1]), f32)
        state_buf[ROWS:, :] = jnp.zeros((HALO, state_buf.shape[1]), f32)
        adjoint[...] = jnp.zeros_like(adjoint)
        for ref in (
            weight_total,
            out_total,
            step_total,
            gate_gain_out,
            value_taps_out,
            state_taps_out,
            skip_out,
            steps_out,
        ):
            ref[...] = jnp.zeros_like(ref)

    scale, moment = stats_columns(stats[...], inner)
    mixed = mixed_in[...]
    back = back_in[...]
    pre = gate[...]
    bent = sigmoid(pre)
    silu = pre * bent
    gated = mixed * silu
    scaled = gated * scale
    gain = row_of(gate_gain)
    add_row(gate_gain_out, 0, back * scaled)
    grad_gated = scale * (back * gain) - scaled * (scale * scale * moment)
    grad_mixed = grad_gated * silu
    round_gate = (grad_gated * mixed * (bent * (1.0 + pre * (1.0 - bent)))).astype(bf16)
    gate_out[...] = round_gate
    outgoing = (scaled * gain).astype(bf16)
    width = out_total.shape[2]
    for x in range(side):
        out_total[x] += mm_tn(outgoing, cotangent[:, x * width : (x + 1) * width])

    value_at = value_conv[...]
    value_bent = sigmoid(value_at)
    values = (value_at * value_bent).astype(bf16)
    state_at = state_conv[...]
    state_bent = sigmoid(state_at)
    states = (state_at * state_bent).astype(bf16)
    step_pre = step_in[...]
    step = softplus(step_pre)
    rate = rate_row(decay_log, heads)
    skip = channel_row(skip_gain, heads)
    log_step = step * rate

    ahead = iota((Q, Q), 1) >= iota((Q, Q), 0)
    tri = jnp.where(iota((Q, Q), 0) >= iota((Q, Q), 1), 1.0, 0.0).astype(f32)
    tri_up = jnp.where(ahead, 1.0, 0.0).astype(f32)
    tri_strict = jnp.where(iota((Q, Q), 0) > iota((Q, Q), 1), 1.0, 0.0).astype(f32)
    lane = iota((Q, LANES), 1)
    row8 = iota((8, Q), 0)
    channels = heads * HEAD
    to_heads = jnp.where(
        lax.shift_right_logical(iota((channels, LANES), 0), 6) == iota((channels, LANES), 1), 1.0, 0.0
    ).astype(bf16)
    parts = ROWS // Q
    grad_value_parts = [None] * parts
    grad_state_parts = [None] * parts
    grad_step_parts = [None] * parts
    for part in reversed(range(parts)):
        rows = slice(part * Q, (part + 1) * Q)
        b = states[rows, :STATE]
        c = states[rows, STATE:]
        v_low = values[rows, :]
        v = v_low.astype(f32)
        dt = step[rows, :]
        dy = grad_mixed[rows, :]
        dy_low = dy.astype(bf16)
        decay = mm(tri, log_step[rows, :], precision=exact)
        decay_t = decay.T
        wide = expand(decay, heads)
        dt_wide = expand(dt, heads)
        grown = jnp.exp(wide)
        to_end = jnp.exp(wide[Q - 1 : Q, :] - wide)
        held = memory_in[part]
        later = adjoint[...]
        later_low = later.astype(bf16)
        bd = mm(b, later_low)
        cs = mm(c, held)
        bc = mm_nt(b, c)
        dy_grown = dy * grown
        dy_grown_low = dy_grown.astype(bf16)
        at_end = bd * to_end
        inside = []
        grad_bc = jnp.zeros((Q, Q), f32)
        direct = jnp.zeros((Q, LANES), f32)
        row_sums = jnp.zeros((8, Q), f32)
        for h in range(0, heads, 2):
            lanes = slice(h * HEAD, (h + 2) * HEAD)
            v_split = split_heads(v_low[:, lanes])
            grad_pair = mm_nt(v_split, dy_low[:, lanes])
            blocks = []
            for at in (h, h + 1):
                gap = decay_t[at : at + 1, :] - column(decay, at)
                fall = jnp.exp(jnp.where(ahead, gap, -1e30))
                grad_fall = grad_pair[(at - h) * Q : (at - h + 1) * Q, :] * fall
                direct += jnp.where(lane == at, jnp.sum(grad_fall * bc, axis=1, keepdims=True), 0.0)
                grad_one = grad_fall * column(dt, at)
                grad_bc += grad_one
                row_sums += jnp.where(
                    row8 == at, jnp.sum(grad_one * bc, axis=0, keepdims=True), 0.0
                )
                blocks.append((bc * fall).astype(bf16))
            inside.append(mm(jnp.concatenate(blocks, axis=1), split_heads(dy_low[:, lanes])))
        grad_value_parts[part] = dt_wide * (jnp.concatenate(inside, axis=1) + at_end) + skip * dy
        add_row(skip_out, 0, dy * v)
        grown_sum = head_sum(dy_grown * cs, to_heads)
        end_sum = head_sum(at_end * v, to_heads)
        constant = head_sum(
            grown[Q - 1 : Q, :] * jnp.sum(held.astype(f32) * later, axis=0, keepdims=True), to_heads
        )
        row_t = jnp.concatenate([row_sums, jnp.zeros((LANES - 8, Q), f32)], axis=0).T
        grad_log = (
            mm(tri_up, row_t - direct * dt + grown_sum, precision=exact)
            + mm(tri_strict, end_sum * dt, precision=exact)
            + constant
        )
        grad_step = direct + end_sum + rate * grad_log
        grad_step = grad_step * sigmoid(step_pre[rows, :])
        grad_step_parts[part] = grad_step
        add_row(steps_out, 0, grad_step)
        add_row(steps_out, 1, dt * grad_log * rate)
        grad_bc_low = grad_bc.astype(bf16)
        grad_b = mm(grad_bc_low, c) + mm_nt((v * dt_wide * to_end).astype(bf16), later_low)
        grad_c = mm_tn(grad_bc_low, b) + mm_nt(dy_grown_low, held)
        grad_state_parts[part] = jnp.concatenate([grad_b, grad_c], axis=1)
        adjoint[...] = later * grown[Q - 1 : Q, :] + mm_tn(c, dy_grown_low)

    def conv_back(buf, grad, at, bent, pre, kernel, taps_out):
        buf[0:ROWS, :] = grad * (bent * (1.0 + at * (1.0 - bent)))
        result = None
        for k in range(CONV):
            moved = buf[3 - k : 3 - k + ROWS, :]
            term = moved * kernel[k : k + 1, :]
            result = term if result is None else result + term
            add_row(taps_out, k, pre * moved)
        add_row(taps_out, CONV, buf[0:ROWS, :])
        buf[ROWS:, :] = buf[0:HALO, :]
        return result.astype(bf16)

    round_value = conv_back(
        value_buf,
        jnp.concatenate(grad_value_parts, axis=0),
        value_at,
        value_bent,
        value[...],
        value_kernel,
        value_taps_out,
    )
    round_state = conv_back(
        state_buf,
        jnp.concatenate(grad_state_parts, axis=0),
        state_at,
        state_bent,
        state[...],
        state_kernel,
        state_taps_out,
    )
    round_step = jnp.concatenate(grad_step_parts, axis=0).astype(bf16)
    value_out[...] = round_value
    state_out[...] = round_state
    step_out[...] = round_step
    weight_total[...] += mm_tn(
        normed[...], jnp.concatenate([round_value, round_gate, round_state], axis=1)
    )
    step_total[...] += mm_tn(round_step, normed[...])

    @pl.when(pl.program_id(0) == steps - 1)
    def _():
        fold = step_total.shape[1] // channels
        local_rows[...] = jnp.zeros_like(local_rows)
        for h in range(heads):
            for q in range(fold):
                local_rows[h * fold + q : h * fold + q + 1, :] = step_total[
                    h : h + 1, q * channels : (q + 1) * channels
                ]
        at = heads * fold
        local_rows[at : at + CONV + 1, :] = value_taps_out[0 : CONV + 1, :]
        at += CONV + 1
        local_rows[at : at + 1, :] = gate_gain_out[0:1, :]
        local_rows[at + 1 : at + 2, :] = jnp.concatenate(
            [steps_out[0:1, :], steps_out[1:2, :], head_sum(skip_out[...], to_heads)[0:1, :]],
            axis=1,
        )
        shared_rows[...] = jnp.zeros_like(shared_rows)
        shared_rows[0 : CONV + 1, :] = state_taps_out[0 : CONV + 1, :]

        _, tall, _ = pieces_out[0].shape
        count = small_rows(side**2, channels)
        slabs[...] = jnp.zeros_like(slabs)
        for d in range(side**2):
            at = 0
            for ref in (local_rows, shared_rows):
                each = ref.shape[0] // side**2
                for j in range(d * each, (d + 1) * each):
                    for lanes in range(0, ref.shape[1], LANES):
                        mine = ref[j : j + 1, lanes : lanes + LANES]
                        high = mine.astype(bf16).astype(f32)
                        slabs[d, at : at + 1, :] = high
                        slabs[d, count + at : count + at + 1, :] = mine - high
                        at += 1
        rows = channels // side
        for k, piece in enumerate(pieces_out):
            for j in range(side):
                y, x = block_of(place, lax.rem(place[3 + place[1]] + k, side), j)
                here = pl.ds(pl.multiple_of((y * side + x) * tall, tall), tall)
                piece[j, :, 0 : 2 * channels] = weight_total[here, 0 : 2 * channels].astype(bf16)
                for c in range(width // channels):
                    piece[j, c * rows : (c + 1) * rows, 2 * channels : 3 * channels] = out_total[
                        x,
                        pl.ds(pl.multiple_of(y * rows, rows), rows),
                        c * channels : (c + 1) * channels,
                    ].astype(bf16)
                at = 3 * channels
                piece[j, :, at : at + 2 * STATE] = weight_total[here, 2 * channels :].astype(bf16)
                piece[j, :, at + 2 * STATE :] = slabs[y * side + x].astype(bf16)


def block_of(place, first, second):
    core = place[1]
    return first + core * (second - first), second + core * (first - second)


def small_rows(pieces, channels):
    return (LOCAL * channels + SHARED * 2 * STATE) // LANES // pieces


def input_kernel(
    tokens,
    round_gate,
    round_value,
    round_state,
    round_step,
    in_gate,
    in_value,
    in_state,
    in_step,
    part_out,
    norm_gain_out,
):
    @pl.when(pl.program_id(0) == 0)
    def _():
        norm_gain_out[...] = jnp.zeros_like(norm_gain_out)

    total = (
        mm_nt(round_gate[...], in_gate[...])
        + mm_nt(round_value[...], in_value[...])
        + mm_nt(round_state[...], in_state[...])
        + mm(round_step[...], all_lanes(in_step[...]))
    )
    part_out[...] = total.astype(bf16)
    x = tokens[...].astype(f32)
    x = x * lax.rsqrt(jnp.mean(x * x, axis=1, keepdims=True) + epsilon)
    add_row(norm_gain_out, 0, total * x)


def gather_kernel(index, place, *refs):
    *pieces, out, sems = refs
    copies = [
        pltpu.make_async_copy(piece, out.at[index(place, k)], sems.at[k])
        for k, piece in enumerate(pieces)
    ]
    for copy in copies:
        copy.start()
    for copy in copies:
        copy.wait()


def total_of(pieces):
    total = pieces[0][...].astype(f32)
    for piece in pieces[1:]:
        total = total + piece[...].astype(f32)
    return total


def line_sum_kernel(place, *refs):
    side = len(refs) // 2
    for k, out in enumerate(refs[side:]):
        at = lax.rem(place[4 - place[1]] + k, side)
        out[...] = total_of([ref.at[at] for ref in refs[:side]]).astype(bf16)


def block_sum_kernel(plain, count, gain_rows, *refs):
    *pieces, norm_gain, weights_out, rest_out = refs
    total = total_of(pieces)
    weights_out[...] = total[:, :plain].astype(bf16)
    rest_out[:, 0 : 2 * STATE] = total[:, plain : plain + 2 * STATE]
    small = total[:, plain + 2 * STATE :]
    rest_out[:, 2 * STATE :] = jnp.zeros_like(small)
    rest_out[0:count, 2 * STATE :] = small[:count, :] + small[count : 2 * count, :]
    for j in range(norm_gain.shape[1] // LANES):
        at = gain_rows + j
        rest_out[at : at + 1, 2 * STATE :] = norm_gain[0:1, j * LANES : (j + 1) * LANES]


def block_pack_kernel(local, count, gain_rows, gains, weights, before, own, one, two, three, out):
    total = (own[...] + two[...]) + (one[...] + three[...])
    plain = weights.shape[1]
    out[:, :plain] = weights[...]
    out[:, plain : plain + 2 * STATE] = total[:, : 2 * STATE].astype(bf16)
    small = total[:, 2 * STATE :]
    small = jnp.where(iota(small.shape, 0) < local, before[:, 2 * STATE :], small)
    high = small.astype(bf16).astype(f32)
    low = small - high
    packed = jnp.concatenate(
        [
            high[:count, :],
            low[:count, :],
            high[gain_rows : gain_rows + gains, :],
            low[gain_rows : gain_rows + gains, :],
            jnp.zeros((small.shape[0] - 2 * count - 2 * gains, LANES), f32),
        ],
        axis=0,
    )
    out[:, plain + 2 * STATE :] = packed.astype(bf16)


def unpack_kernel(heads, side, count, gains, place, *refs):
    pieces = refs[:side]
    value_out, gate_out, out_out, state_out, *small_outs = refs[side:-5]
    wide, states, small_rows_at, gain_parts, sems = refs[-5:]
    _, _, tall, channels = wide.shape
    rows, width = out_out.shape[0] // side, out_out.shape[1] // side
    copies = []

    def send(source, target):
        copies.append(pltpu.make_async_copy(source, target, sems.at[len(copies)]))
        copies[-1].start()

    for k, piece in enumerate(pieces):
        first = lax.rem(place[3 + place[1]] + side - k, side)
        for j in range(side):
            y, x = block_of(place, first, j)
            at = k * side + j
            d = y * side + x
            here = pl.ds(pl.multiple_of(d * tall, tall), tall)
            for c in range(3):
                wide[at, c] = piece[j, :, c * channels : (c + 1) * channels].astype(f32)
            send(wide.at[at, 0], value_out.at[here])
            send(wide.at[at, 1], gate_out.at[here])
            for c in range(width // channels):
                send(
                    wide.at[at, 2, pl.ds(c * rows, rows)],
                    out_out.at[
                        pl.ds(pl.multiple_of(y * rows, rows), rows),
                        pl.ds(pl.multiple_of(x * width + c * channels, channels), channels),
                    ],
                )
            plain = 3 * channels
            states[at] = piece[j, :, plain : plain + 2 * STATE].astype(f32)
            send(states.at[at], state_out.at[here])
            small = piece[j, :, plain + 2 * STATE :].astype(f32)
            small_rows_at[d] = small[:count, :] + small[count : 2 * count, :]
            low = 2 * count + gains
            gain_parts[d] = small[2 * count : low, :] + small[low : low + gains, :]
    (
        step_out,
        step_bias_out,
        decay_out,
        skip_out,
        value_taps_out,
        value_bias_out,
        gate_gain_out,
        norm_gain_out,
        state_taps_out,
        state_bias_out,
    ) = small_outs
    fold, across = step_out.shape[1] // channels, channels // LANES
    own, ours = LOCAL // side**2, SHARED // side**2

    def local(row, tile):
        at = row % own * across + tile
        return small_rows_at[row // own, at : at + 1, :]

    def shared(row, tile):
        at = own * across + row % ours * (2 * STATE // LANES) + tile
        return small_rows_at[row // ours, at : at + 1, :]

    total = gain_parts[0]
    for d in range(1, side**2):
        total = total + gain_parts[d]
    for t in range(gains):
        norm_gain_out[t * LANES : (t + 1) * LANES] = total[t, :]
    for h in range(heads):
        for q in range(fold):
            for t in range(across):
                at = q * channels + t * LANES
                step_out[h : h + 1, at : at + LANES] = local(h * fold + q, t)
    row = heads * fold
    for t in range(across):
        lanes = slice(t * LANES, (t + 1) * LANES)
        for k in range(CONV):
            value_taps_out[k : k + 1, lanes] = local(row + k, t)
        value_bias_out[lanes] = local(row + CONV, t)[0]
        gate_gain_out[lanes] = local(row + CONV + 1, t)[0]
    for t, out in enumerate((step_bias_out, decay_out, skip_out)):
        out[...] = local(row + CONV + 2, t)[:, :heads]
    for t in range(2 * STATE // LANES):
        lanes = slice(t * LANES, (t + 1) * LANES)
        for k in range(CONV):
            state_taps_out[k : k + 1, lanes] = shared(k, t)
        state_bias_out[lanes] = shared(CONV, t)[0]
    for copy in copies:
        copy.wait()


def output_kernel(inner, total, tokens, stats, out):
    scale, _ = stats_columns(stats[...], inner)
    out[...] = (tokens[...].astype(f32) + scale * total[...].astype(f32)).astype(bf16)


def grad_kernel(total, tokens, cotangent, norm_gain, out):
    x = tokens[...].astype(f32)
    inverse = lax.rsqrt(jnp.mean(x * x, axis=1, keepdims=True) + epsilon)
    scaled = total[...].astype(f32) * row_of(norm_gain)
    moment = jnp.mean(scaled * x, axis=1, keepdims=True)
    grad = inverse * scaled - x * (inverse * inverse * inverse * moment)
    out[...] = (cotangent[...].astype(f32) + grad).astype(bf16)


def whole(array):
    zeros = (0,) * array.ndim
    return pl.BlockSpec(array.shape, lambda i: zeros)


def in_scalars():
    return pl.BlockSpec(memory_space=pltpu.SMEM)


def by_rows(width, steps=None, rows=ROWS):
    if steps is None:
        return pl.BlockSpec((rows, width), lambda i: (i, 0))
    return pl.BlockSpec((rows, width), lambda i: (steps - 1 - i, 0))


def swap_core(x):
    return lax.ppermute(x, "tensor", [(i, i ^ 1) for i in range(8)])


def move_z(x, k):
    return lax.ppermute(x, "tensor", [(i, (i + 2 * k) % 8) for i in range(8)])


def move_dp(x, k, side, stage):
    pairs = []
    for y in range(side):
        for x_at in range(side):
            for t in range(8):
                if (t + stage) % 2 == 0:
                    to = (y + k) % side * side + x_at
                else:
                    to = y * side + (x_at + k) % side
                pairs.append(((y * side + x_at) * 8 + t, to * 8 + t))
    return lax.ppermute(x, ("dp", "tensor"), pairs)


def after(x, *others):
    return lax.optimization_barrier((x,) + others)[0]


free = pl.CostEstimate(flops=0, bytes_accessed=0, transcendentals=0)


def at_place(kernel, place, operands, grid, in_specs, out_specs, out_shape, scratch=()):
    return pl.pallas_call(
        kernel,
        grid_spec=pltpu.PrefetchScalarGridSpec(
            num_scalar_prefetch=1,
            grid=grid,
            in_specs=in_specs,
            out_specs=out_specs,
            scratch_shapes=scratch,
        ),
        out_shape=out_shape,
        compiler_params=pltpu.CompilerParams(
            dimension_semantics=("arbitrary",) * len(grid), vmem_limit_bytes=VMEM
        ),
        cost_estimate=free,
    )(place, *operands)


def fixed(*shape):
    return pl.BlockSpec(shape, lambda *_: (0,) * len(shape))


def gather_pieces(place, pieces, index):
    return at_place(
        partial(gather_kernel, index),
        place,
        pieces,
        (1,),
        [fixed(*pieces[0].shape)] * len(pieces),
        pl.BlockSpec(memory_space=pl.ANY),
        jax.ShapeDtypeStruct((len(pieces),) + pieces[0].shape, pieces[0].dtype),
        [pltpu.SemaphoreType.DMA((len(pieces),))],
    )


def along_second(place, pieces):
    side = len(pieces)
    return gather_pieces(
        place, pieces, lambda at, k: lax.rem(at[4 - at[1]] + side - k, side)
    )


def on_device(
    tokens,
    norm_gain,
    in_gate,
    in_value,
    in_state,
    in_step,
    step_bias,
    decay_log,
    skip_gain,
    conv_value_kernel,
    conv_value_bias,
    conv_state_kernel,
    conv_state_bias,
    gate_gain,
    out_weight,
    cotangent,
):
    features = tokens.shape[1]
    channels = in_gate.shape[1]
    heads = step_bias.shape[0]
    inner = channels * lax.axis_size("tensor")
    steps = LEN // ROWS
    parts = ROWS // Q
    dp = lax.axis_size("dp")
    side = math.isqrt(dp)
    me = lax.axis_index("tensor")
    row = lax.axis_index("dp")
    place = jnp.stack([me // 2, me % 2, me, row // side, row % side]).astype(jnp.int32)

    step_weight = in_step.T
    sds = jax.ShapeDtypeStruct
    params = pltpu.CompilerParams(
        dimension_semantics=("arbitrary",), vmem_limit_bytes=VMEM
    )
    stats_rows = pl.BlockSpec((8, ROWS), lambda i: (0, i))
    memory_rows = lambda at: pl.BlockSpec((parts, STATE, channels), lambda i: (at(i), 0, 0))

    (
        normed,
        gate_pre,
        value_pre,
        value_conv,
        state_pre,
        state_conv,
        step_pre,
        mixed,
        back,
        part,
        memories,
        stats,
    ) = pl.pallas_call(
        partial(forward_kernel, heads),
        grid=(steps,),
        in_specs=[
            by_rows(features),
            whole(norm_gain),
            whole(in_gate),
            whole(in_value),
            whole(in_state),
            whole(step_weight),
            in_scalars(),
            in_scalars(),
            in_scalars(),
            whole(conv_value_kernel),
            whole(conv_value_bias),
            whole(conv_state_kernel),
            whole(conv_state_bias),
            whole(gate_gain),
            whole(out_weight),
            by_rows(features),
        ],
        out_specs=[
            by_rows(features),
            by_rows(channels),
            by_rows(channels),
            by_rows(channels),
            by_rows(2 * STATE),
            by_rows(2 * STATE),
            by_rows(LANES),
            by_rows(channels),
            by_rows(channels),
            by_rows(features),
            memory_rows(lambda i: i),
            stats_rows,
        ],
        out_shape=[
            sds((LEN, features), bf16),
            sds((LEN, channels), f32),
            sds((LEN, channels), f32),
            sds((LEN, channels), f32),
            sds((LEN, 2 * STATE), f32),
            sds((LEN, 2 * STATE), f32),
            sds((LEN, LANES), f32),
            sds((LEN, channels), f32),
            sds((LEN, channels), f32),
            sds((LEN, features), bf16),
            sds((LEN // Q, STATE, channels), bf16),
            sds((8, LEN), f32),
        ],
        scratch_shapes=[
            pltpu.VMEM((ROWS + HALO, channels), f32),
            pltpu.VMEM((ROWS + HALO, 2 * STATE), f32),
            pltpu.VMEM((STATE, channels), f32),
        ],
        compiler_params=params,
        cost_estimate=free,
    )(
        tokens,
        norm_gain,
        in_gate,
        in_value,
        in_state,
        step_weight,
        step_bias,
        decay_log,
        skip_gain,
        conv_value_kernel,
        conv_value_bias,
        conv_state_kernel,
        conv_state_bias,
        gate_gain,
        out_weight,
        cotangent,
    )

    out_sum = lax.psum_scatter(part, "tensor", scatter_dimension=0, tiled=True)
    stats = stats + swap_core(stats)
    moved = [move_z(stats, k) for k in (1, 2, 3)]
    stats = (stats + moved[1]) + (moved[0] + moved[2])

    back_rows = partial(by_rows, steps=steps)
    lanes = 3 * channels + 2 * STATE + LANES
    tall = features // dp
    round_gate, round_value, round_state, round_step, *weights = pl.pallas_call(
        partial(backward_kernel, heads, inner, steps, side),
        grid=(steps,),
        in_specs=[
            in_scalars(),
            pl.BlockSpec((8, ROWS), lambda i: (0, steps - 1 - i)),
            back_rows(features),
            back_rows(features),
            back_rows(channels),
            back_rows(channels),
            back_rows(channels),
            back_rows(channels),
            back_rows(channels),
            back_rows(2 * STATE),
            back_rows(2 * STATE),
            back_rows(LANES),
            memory_rows(lambda i: steps - 1 - i),
            whole(gate_gain),
            in_scalars(),
            in_scalars(),
            whole(conv_value_kernel),
            whole(conv_state_kernel),
        ],
        out_specs=[
            back_rows(channels),
            back_rows(channels),
            back_rows(2 * STATE),
            back_rows(LANES),
        ]
        + [fixed(side, tall, lanes)] * side,
        out_shape=[
            sds((LEN, channels), bf16),
            sds((LEN, channels), bf16),
            sds((LEN, 2 * STATE), bf16),
            sds((LEN, LANES), bf16),
        ]
        + [sds((side, tall, lanes), bf16)] * side,
        scratch_shapes=[
            pltpu.VMEM((ROWS + HALO, channels), f32),
            pltpu.VMEM((ROWS + HALO, 2 * STATE), f32),
            pltpu.VMEM((STATE, channels), f32),
            pltpu.VMEM((features, 2 * channels + 2 * STATE), f32),
            pltpu.VMEM((side, channels, features // side), f32),
            pltpu.VMEM((LANES, features), f32),
            pltpu.VMEM((8, channels), f32),
            pltpu.VMEM((8, channels), f32),
            pltpu.VMEM((8, 2 * STATE), f32),
            pltpu.VMEM((8, channels), f32),
            pltpu.VMEM((8, LANES), f32),
            pltpu.VMEM((LOCAL, channels), f32),
            pltpu.VMEM((SHARED, 2 * STATE), f32),
            pltpu.VMEM((dp, tall, LANES), f32),
        ],
        compiler_params=params,
        cost_estimate=free,
    )(
        place,
        stats,
        normed,
        cotangent,
        gate_pre,
        mixed,
        back,
        value_pre,
        value_conv,
        state_pre,
        state_conv,
        step_pre,
        memories,
        gate_gain,
        decay_log,
        skip_gain,
        conv_value_kernel,
        conv_state_kernel,
    )
    out_sum = after(out_sum, round_gate)
    weights[0] = after(weights[0], out_sum)
    out_sum = lax.all_gather(out_sum, "tensor", tiled=True)

    weights = [weights[0]] + [
        move_dp(after(weights[k], weights[0]), k, side, 0) for k in range(1, side)
    ]

    part, norm_gain_part = pl.pallas_call(
        input_kernel,
        grid=(steps,),
        in_specs=[
            by_rows(features),
            by_rows(channels),
            by_rows(channels),
            by_rows(2 * STATE),
            by_rows(LANES),
            whole(in_gate),
            whole(in_value),
            whole(in_state),
            whole(step_weight),
        ],
        out_specs=[
            by_rows(features),
            fixed(8, features),
        ],
        out_shape=[
            sds((LEN, features), bf16),
            sds((8, features), f32),
        ],
        compiler_params=params,
        cost_estimate=free,
    )(
        tokens,
        round_gate,
        round_value,
        round_state,
        round_step,
        in_gate,
        in_value,
        in_state,
        step_weight,
    )
    weights[0] = after(weights[0], norm_gain_part)
    weights = at_place(
        line_sum_kernel,
        place,
        weights,
        (1,),
        [fixed(side, tall, lanes)] * side,
        [fixed(tall, lanes)] * side,
        [sds((tall, lanes), bf16)] * side,
    )
    grad_sum = lax.psum_scatter(
        after(part, weights[0]), "tensor", scatter_dimension=0, tiled=True
    )
    weights = [weights[0]] + [move_dp(weights[k], k, side, 1) for k in range(1, side)]

    block_output = pl.pallas_call(
        partial(output_kernel, inner),
        grid=(steps,),
        in_specs=[by_rows(features), by_rows(features), stats_rows],
        out_specs=by_rows(features),
        out_shape=sds((LEN, features), bf16),
        compiler_params=params,
        cost_estimate=free,
    )(after(out_sum, weights[0]), tokens, stats)

    weights[0] = after(weights[0], block_output)

    count = small_rows(dp, channels)
    local = LOCAL * channels // LANES // dp
    gains = features // LANES
    gain_rows = -(-count // 8) * 8
    plain = 3 * channels
    vmem = pltpu.CompilerParams(vmem_limit_bytes=VMEM)
    weights, rest = pl.pallas_call(
        partial(block_sum_kernel, plain, count, gain_rows),
        out_shape=[sds((tall, plain), bf16), sds((tall, lanes - plain), f32)],
        compiler_params=vmem,
        cost_estimate=free,
    )(*weights, norm_gain_part)
    both = rest + swap_core(rest)
    weights = pl.pallas_call(
        partial(block_pack_kernel, local, count, gain_rows, gains),
        out_shape=sds((tall, lanes), bf16),
        compiler_params=vmem,
        cost_estimate=free,
    )(weights, rest, both, *[move_z(both, k) for k in (1, 2, 3)])
    weights = [weights] + [move_dp(weights, k, side, 1) for k in range(1, side)]
    weights = along_second(place, weights)
    weights = [weights] + [move_dp(weights, k, side, 0) for k in range(1, side)]
    grad_sum = lax.all_gather(after(grad_sum, weights[0]), "tensor", tiled=True)
    grad_tokens = pl.pallas_call(
        grad_kernel,
        grid=(steps,),
        in_specs=[by_rows(features)] * 3 + [whole(norm_gain)],
        out_specs=by_rows(features),
        out_shape=sds((LEN, features), bf16),
        compiler_params=params,
        cost_estimate=free,
    )(grad_sum, tokens, cotangent, norm_gain)
    weights[0] = after(weights[0], grad_tokens)

    anywhere = pl.BlockSpec(memory_space=pl.ANY)
    smalls = [
        (heads, features),
        (1, heads),
        (1, heads),
        (1, heads),
        (CONV, channels),
        (channels,),
        (channels,),
        (features,),
        (CONV, 2 * STATE),
        (2 * STATE,),
    ]
    across = features // side // channels
    grad_in_value, grad_in_gate, grad_out_weight, grad_in_state, *smalls = at_place(
        partial(unpack_kernel, heads, side, count, gains),
        place,
        weights,
        (1,),
        [fixed(side, tall, lanes)] * side,
        [anywhere] * 4 + [fixed(*shape) for shape in smalls],
        [
            sds((features, channels), f32),
            sds((features, channels), f32),
            sds((channels, features), f32),
            sds((features, 2 * STATE), f32),
        ]
        + [sds(shape, f32) for shape in smalls],
        [
            pltpu.VMEM((dp, 3, tall, channels), f32),
            pltpu.VMEM((dp, tall, 2 * STATE), f32),
            pltpu.VMEM((dp, count, LANES), f32),
            pltpu.VMEM((dp, gains, LANES), f32),
            pltpu.SemaphoreType.DMA((dp * (3 + across),)),
        ],
    )
    grad_in_step = smalls[0].T
    (
        grad_step_bias,
        grad_decay_log,
        grad_skip_gain,
        grad_conv_value_kernel,
        grad_conv_value_bias,
        grad_gate_gain,
        grad_norm_gain,
        grad_conv_state_kernel,
        grad_conv_state_bias,
    ) = (a[0] if a.shape[0] == 1 else a for a in smalls[1:])
    return (
        block_output,
        grad_tokens,
        grad_norm_gain,
        grad_in_gate,
        grad_in_value,
        grad_in_state,
        grad_in_step,
        grad_step_bias,
        grad_decay_log,
        grad_skip_gain,
        grad_conv_value_kernel,
        grad_conv_value_bias,
        grad_conv_state_kernel,
        grad_conv_state_bias,
        grad_gate_gain,
        grad_out_weight,
    )


def solution(mesh):
    placed = (
        P("dp", None),
        P(),
        P(None, "tensor"),
        P(None, "tensor"),
        P(),
        P(None, "tensor"),
        P("tensor"),
        P("tensor"),
        P("tensor"),
        P(None, "tensor"),
        P("tensor"),
        P(),
        P(),
        P("tensor"),
        P("tensor", None),
        P("dp", None),
    )
    return jax.shard_map(
        on_device,
        mesh=mesh,
        in_specs=placed,
        out_specs=(
            P("dp", None),
            P("dp", None),
            P(),
            P(None, "tensor"),
            P(None, "tensor"),
            P(),
            P(None, "tensor"),
            P("tensor"),
            P("tensor"),
            P("tensor"),
            P(None, "tensor"),
            P("tensor"),
            P(),
            P(),
            P("tensor"),
            P("tensor", None),
        ),
        check_vma=False,
    )
```

```python
import math
from functools import partial

import jax
import jax.numpy as jnp
from jax import lax
from jax.experimental import pallas as pl
from jax.experimental.pallas import tpu as pltpu
from jax.sharding import PartitionSpec as P

STATE = 128
CONV = 4
LEN = 1024
HEAD = 64
Q = 128
ROWS = 256
LANES = 128
HALO = 8
LOCAL = 32
SHARED = 16

epsilon = 1e-05
f32 = jnp.float32
bf16 = jnp.bfloat16
VMEM = 60 * 1024 * 1024
SMALL_VMEM = 40 * 1024 * 1024


def mm(a, b):
    return lax.dot_general(a, b, (((1,), (0,)), ((), ())), preferred_element_type=f32)


def parts_of(x):
    high = x.astype(bf16)
    rest = x - high.astype(f32)
    middle = rest.astype(bf16)
    return [high, middle, (rest - middle.astype(f32)).astype(bf16)]


def sum_rows(triangle, x):
    width = x.shape[1]
    total = mm(triangle, jnp.concatenate(parts_of(x), axis=1))
    return total[:, :width] + total[:, width : 2 * width] + total[:, 2 * width :]


def mm_nt(a, b):
    return lax.dot_general(a, b, (((1,), (1,)), ((), ())), preferred_element_type=f32)


def mm_tn(a, b):
    return lax.dot_general(a, b, (((0,), (0,)), ((), ())), preferred_element_type=f32)


def sigmoid(v):
    return 1.0 / (1.0 + jnp.exp(-v))


def softplus(v):
    return jnp.maximum(v, 0.0) + jnp.log1p(jnp.exp(-jnp.abs(v)))


def iota(shape, axis):
    return lax.broadcasted_iota(jnp.int32, shape, axis)


def column(m, at):
    return jnp.broadcast_to(m[:, at : at + 1], (m.shape[0], LANES))


def low_half(rows):
    return iota((rows, LANES), 1) < HEAD


def expand(m, heads):
    half = low_half(m.shape[0])
    return jnp.concatenate(
        [jnp.where(half, column(m, h), column(m, h + 1)) for h in range(0, heads, 2)], axis=1
    )


def split_heads(pair):
    half = low_half(pair.shape[0])
    zero = jnp.zeros_like(pair)
    return jnp.concatenate([jnp.where(half, pair, zero), jnp.where(half, zero, pair)], axis=0)


def head_sum(m, channels_to_heads):
    high = m.astype(bf16)
    low = (m - high.astype(f32)).astype(bf16)
    return mm(high, channels_to_heads) + mm(low, channels_to_heads)


def head_row(scalars, heads):
    lane = iota((1, LANES), 1)
    row = jnp.zeros((1, LANES), f32)
    for h in range(heads):
        row = jnp.where(lane == h, scalars[h], row)
    return row


def rate_row(decay_log, heads):
    return jnp.where(iota((1, LANES), 1) < heads, -jnp.exp(head_row(decay_log, heads)), 0.0)


def channel_row(scalars, heads):
    half = low_half(1)
    return jnp.concatenate(
        [jnp.where(half, scalars[h], scalars[h + 1]) for h in range(0, heads, 2)], axis=1
    )


def all_lanes(rows):
    below = jnp.zeros((LANES - rows.shape[0], rows.shape[1]), rows.dtype)
    return jnp.concatenate([rows, below], axis=0)


def row_of(ref):
    return ref[...].reshape(1, ref.shape[0])


def forward_kernel(
    heads,
    tokens,
    norm_gain,
    in_gate,
    in_value,
    in_state,
    in_step,
    step_bias,
    decay_log,
    skip_gain,
    value_kernel,
    value_bias,
    state_kernel,
    state_bias,
    gate_gain,
    out_weight,
    cotangent,
    normed_out,
    gate_out,
    value_out,
    value_conv_out,
    state_out,
    state_conv_out,
    step_out,
    mixed_out,
    back_out,
    part_out,
    memory_out,
    stats_out,
    value_buf,
    state_buf,
    memory,
):
    @pl.when(pl.program_id(0) == 0)
    def _():
        value_buf[0:HALO, :] = jnp.zeros((HALO, value_buf.shape[1]), f32)
        state_buf[0:HALO, :] = jnp.zeros((HALO, state_buf.shape[1]), f32)
        memory[...] = jnp.zeros_like(memory)

    x = tokens[...].astype(f32)
    inverse = lax.rsqrt(jnp.mean(x * x, axis=1, keepdims=True) + epsilon)
    normed = (x * inverse * row_of(norm_gain)).astype(bf16)
    normed_out[...] = normed
    state_pre = mm(normed, in_state[...])
    value_pre = mm(normed, in_value[...])
    step_pre = mm_nt(normed, all_lanes(in_step[...])) + head_row(step_bias, heads)
    gate_pre = mm(normed, in_gate[...])
    gate_out[...] = gate_pre
    value_out[...] = value_pre
    state_out[...] = state_pre
    step_out[...] = step_pre

    def conv(buf, pre, kernel, bias):
        buf[HALO:, :] = pre
        result = row_of(bias) + buf[HALO - 3 : HALO - 3 + ROWS, :] * kernel[0:1, :]
        for k in range(1, CONV):
            result = result + buf[HALO - 3 + k : HALO - 3 + k + ROWS, :] * kernel[k : k + 1, :]
        buf[0:HALO, :] = buf[ROWS : ROWS + HALO, :]
        return result

    value_conv = conv(value_buf, value_pre, value_kernel, value_bias)
    value_conv_out[...] = value_conv
    values = (value_conv * sigmoid(value_conv)).astype(bf16)
    state_conv = conv(state_buf, state_pre, state_kernel, state_bias)
    state_conv_out[...] = state_conv
    states = (state_conv * sigmoid(state_conv)).astype(bf16)
    step = softplus(step_pre)
    log_step = step * rate_row(decay_log, heads)
    skip = channel_row(skip_gain, heads)

    causal = iota((Q, Q), 0) >= iota((Q, Q), 1)
    tri = jnp.where(causal, 1.0, 0.0).astype(bf16)
    mixed_parts = []
    for part in range(ROWS // Q):
        rows = slice(part * Q, (part + 1) * Q)
        b = states[rows, :STATE]
        c = states[rows, STATE:]
        v = values[rows, :].astype(f32)
        dt = step[rows, :]
        decay = sum_rows(tri, log_step[rows, :])
        decay_t = decay.T
        wide = expand(decay, heads)
        dt_wide = expand(dt, heads)
        grown = jnp.exp(wide)
        scaled = v * dt_wide
        scaled_low = scaled.astype(bf16)
        cb = mm_nt(c, b)
        held = memory[...]
        held_low = held.astype(bf16)
        memory_out[part] = held_low
        y = mm(c, held_low) * grown + skip * v
        inside = []
        for h in range(0, heads, 2):
            blocks = []
            for at in (h, h + 1):
                gap = column(decay, at) - decay_t[at : at + 1, :]
                blocks.append((cb * jnp.exp(jnp.where(causal, gap, -1e30))).astype(bf16))
            pair = scaled_low[:, h * HEAD : (h + 2) * HEAD]
            inside.append(mm(jnp.concatenate(blocks, axis=1), split_heads(pair)))
        mixed_parts.append(y + jnp.concatenate(inside, axis=1))
        ended = (scaled * jnp.exp(wide[Q - 1 : Q, :] - wide)).astype(bf16)
        memory[...] = held * grown[Q - 1 : Q, :] + mm_tn(b, ended)

    mixed = jnp.concatenate(mixed_parts, axis=0)
    mixed_out[...] = mixed
    gated = mixed * gate_pre * sigmoid(gate_pre)
    back = mm_nt(cotangent[...], out_weight[...])
    back_out[...] = back
    gained = gated * row_of(gate_gain)
    part_out[...] = mm(gained.astype(bf16), out_weight[...]).astype(bf16)
    squares = jnp.sum(gated * gated, axis=1, keepdims=True)
    moment = jnp.sum(back * gained, axis=1, keepdims=True)
    lane = iota((ROWS, LANES), 1)
    both = jnp.where(lane == 0, squares, jnp.where(lane == 1, moment, 0.0))
    stats_out[...] = both.T[0:8, :]


def stats_columns(stats, inner):
    padded = jnp.concatenate([stats, jnp.zeros((LANES - 8, stats.shape[1]), f32)], axis=0).T
    scale = lax.rsqrt(padded[:, 0:1] / inner + epsilon)
    return scale, padded[:, 1:2] / inner


def add_row(ref, at, rows):
    ref[at : at + 1, :] += jnp.sum(rows, axis=0, keepdims=True)


def backward_kernel(
    heads,
    inner,
    steps,
    side,
    place,
    stats,
    normed,
    cotangent,
    gate,
    mixed_in,
    back_in,
    value,
    value_conv,
    state,
    state_conv,
    step_in,
    memory_in,
    gate_gain,
    decay_log,
    skip_gain,
    value_kernel,
    state_kernel,
    norm_gain,
    in_gate_at,
    in_value_at,
    in_state_at,
    in_step,
    part_out,
    norm_gain_out,
    keep_out,
    send_out,
    *refs,
):
    pieces_out = refs[:side]
    (
        value_buf,
        state_buf,
        adjoint,
        weight_total,
        out_total,
        step_total,
        gate_gain_out,
        value_taps_out,
        state_taps_out,
        skip_out,
        steps_out,
        local_rows,
        shared_rows,
        slabs,
        in_gate,
        in_value,
        in_state,
        sems,
    ) = refs[side:]
    weights = [
        pltpu.make_async_copy(source, target, sems.at[i])
        for i, (source, target) in enumerate(
            ((in_gate_at, in_gate), (in_value_at, in_value), (in_state_at, in_state))
        )
    ]

    @pl.when(pl.program_id(0) == 0)
    def _():
        for copy in weights:
            copy.start()
        norm_gain_out[...] = jnp.zeros_like(norm_gain_out)
        value_buf[ROWS:, :] = jnp.zeros((HALO, value_buf.shape[1]), f32)
        state_buf[ROWS:, :] = jnp.zeros((HALO, state_buf.shape[1]), f32)
        adjoint[...] = jnp.zeros_like(adjoint)
        for ref in (
            weight_total,
            out_total,
            step_total,
            gate_gain_out,
            value_taps_out,
            state_taps_out,
            skip_out,
            steps_out,
        ):
            ref[...] = jnp.zeros_like(ref)

    scale, moment = stats_columns(stats[...], inner)
    mixed = mixed_in[...]
    back = back_in[...]
    pre = gate[...]
    bent = sigmoid(pre)
    silu = pre * bent
    gated = mixed * silu
    scaled = gated * scale
    gain = row_of(gate_gain)
    add_row(gate_gain_out, 0, back * scaled)
    grad_gated = scale * (back * gain) - scaled * (scale * scale * moment)
    grad_mixed = grad_gated * silu
    round_gate = (grad_gated * mixed * (bent * (1.0 + pre * (1.0 - bent)))).astype(bf16)
    outgoing = (scaled * gain).astype(bf16)
    width = out_total.shape[2]
    for x in range(side):
        out_total[x] += mm_tn(outgoing, cotangent[:, x * width : (x + 1) * width])

    value_at = value_conv[...]
    value_bent = sigmoid(value_at)
    values = (value_at * value_bent).astype(bf16)
    state_at = state_conv[...]
    state_bent = sigmoid(state_at)
    states = (state_at * state_bent).astype(bf16)
    step_pre = step_in[...]
    step = softplus(step_pre)
    rate = rate_row(decay_log, heads)
    skip = channel_row(skip_gain, heads)
    log_step = step * rate

    ahead = iota((Q, Q), 1) >= iota((Q, Q), 0)
    tri = jnp.where(iota((Q, Q), 0) >= iota((Q, Q), 1), 1.0, 0.0).astype(bf16)
    tri_both = jnp.concatenate(
        [
            jnp.where(ahead, 1.0, 0.0),
            jnp.where(iota((Q, Q), 0) > iota((Q, Q), 1), 1.0, 0.0),
        ],
        axis=1,
    ).astype(bf16)
    lane = iota((Q, LANES), 1)
    row8 = iota((8, Q), 0)
    channels = heads * HEAD
    to_heads = jnp.where(
        lax.shift_right_logical(iota((channels, LANES), 0), 6) == iota((channels, LANES), 1), 1.0, 0.0
    ).astype(bf16)
    parts = ROWS // Q
    grad_value_parts = [None] * parts
    grad_state_parts = [None] * parts
    grad_step_parts = [None] * parts
    for part in reversed(range(parts)):
        rows = slice(part * Q, (part + 1) * Q)
        b = states[rows, :STATE]
        c = states[rows, STATE:]
        v_low = values[rows, :]
        v = v_low.astype(f32)
        dt = step[rows, :]
        dy = grad_mixed[rows, :]
        dy_low = dy.astype(bf16)
        decay = sum_rows(tri, log_step[rows, :])
        decay_t = decay.T
        wide = expand(decay, heads)
        dt_wide = expand(dt, heads)
        grown = jnp.exp(wide)
        to_end = jnp.exp(wide[Q - 1 : Q, :] - wide)
        held = memory_in[part]
        later = adjoint[...]
        later_low = later.astype(bf16)
        bd = mm(b, later_low)
        cs = mm(c, held)
        bc = mm_nt(b, c)
        dy_grown = dy * grown
        dy_grown_low = dy_grown.astype(bf16)
        at_end = bd * to_end
        inside = []
        grad_bc = jnp.zeros((Q, Q), f32)
        direct = jnp.zeros((Q, LANES), f32)
        row_sums = jnp.zeros((8, Q), f32)
        for h in range(0, heads, 2):
            lanes = slice(h * HEAD, (h + 2) * HEAD)
            v_split = split_heads(v_low[:, lanes])
            grad_pair = mm_nt(v_split, dy_low[:, lanes])
            blocks = []
            for at in (h, h + 1):
                gap = decay_t[at : at + 1, :] - column(decay, at)
                fall = jnp.exp(jnp.where(ahead, gap, -1e30))
                grad_fall = grad_pair[(at - h) * Q : (at - h + 1) * Q, :] * fall
                direct += jnp.where(lane == at, jnp.sum(grad_fall * bc, axis=1, keepdims=True), 0.0)
                grad_one = grad_fall * column(dt, at)
                grad_bc += grad_one
                row_sums += jnp.where(
                    row8 == at, jnp.sum(grad_one * bc, axis=0, keepdims=True), 0.0
                )
                blocks.append((bc * fall).astype(bf16))
            inside.append(mm(jnp.concatenate(blocks, axis=1), split_heads(dy_low[:, lanes])))
        grad_value_parts[part] = dt_wide * (jnp.concatenate(inside, axis=1) + at_end) + skip * dy
        add_row(skip_out, 0, dy * v)
        grown_sum = head_sum(dy_grown * cs, to_heads)
        end_sum = head_sum(at_end * v, to_heads)
        constant = head_sum(
            grown[Q - 1 : Q, :] * jnp.sum(held.astype(f32) * later, axis=0, keepdims=True), to_heads
        )
        row_t = jnp.concatenate([row_sums, jnp.zeros((LANES - 8, Q), f32)], axis=0).T
        grad_log = (
            sum_rows(
                tri_both,
                jnp.concatenate([row_t - direct * dt + grown_sum, end_sum * dt], axis=0),
            )
            + constant
        )
        grad_step = direct + end_sum + rate * grad_log
        grad_step = grad_step * sigmoid(step_pre[rows, :])
        grad_step_parts[part] = grad_step
        add_row(steps_out, 0, grad_step)
        add_row(steps_out, 1, dt * grad_log * rate)
        grad_bc_low = grad_bc.astype(bf16)
        grad_b = mm(grad_bc_low, c) + mm_nt((v * dt_wide * to_end).astype(bf16), later_low)
        grad_c = mm_tn(grad_bc_low, b) + mm_nt(dy_grown_low, held)
        grad_state_parts[part] = jnp.concatenate([grad_b, grad_c], axis=1)
        adjoint[...] = later * grown[Q - 1 : Q, :] + mm_tn(c, dy_grown_low)

    def conv_back(buf, grad, at, bent, pre, kernel, taps_out):
        buf[0:ROWS, :] = grad * (bent * (1.0 + at * (1.0 - bent)))
        result = None
        for k in range(CONV):
            moved = buf[3 - k : 3 - k + ROWS, :]
            term = moved * kernel[k : k + 1, :]
            result = term if result is None else result + term
            add_row(taps_out, k, pre * moved)
        add_row(taps_out, CONV, buf[0:ROWS, :])
        buf[ROWS:, :] = buf[0:HALO, :]
        return result.astype(bf16)

    round_value = conv_back(
        value_buf,
        jnp.concatenate(grad_value_parts, axis=0),
        value_at,
        value_bent,
        value[...],
        value_kernel,
        value_taps_out,
    )
    round_state = conv_back(
        state_buf,
        jnp.concatenate(grad_state_parts, axis=0),
        state_at,
        state_bent,
        state[...],
        state_kernel,
        state_taps_out,
    )
    round_step = jnp.concatenate(grad_step_parts, axis=0).astype(bf16)

    @pl.when(pl.program_id(0) == 0)
    def _():
        for copy in weights:
            copy.wait()

    total = (
        mm_nt(round_gate, in_gate[...])
        + mm_nt(round_value, in_value[...])
        + mm_nt(round_state, in_state[...])
        + mm(round_step, all_lanes(in_step[...]))
    )
    part_out[...] = total.astype(bf16)
    add_row(norm_gain_out, 0, total * normed[...].astype(f32))
    weight_total[...] += mm_tn(
        normed[...], jnp.concatenate([round_value, round_gate, round_state], axis=1)
    )
    step_total[...] += mm_tn(round_step, normed[...])

    @pl.when(pl.program_id(0) == steps - 1)
    def _():
        norm_gain_out[...] = norm_gain_out[...] / row_of(norm_gain)
        fold = step_total.shape[1] // channels
        local_rows[...] = jnp.zeros_like(local_rows)
        for h in range(heads):
            for q in range(fold):
                local_rows[h * fold + q : h * fold + q + 1, :] = step_total[
                    h : h + 1, q * channels : (q + 1) * channels
                ]
        at = heads * fold
        local_rows[at : at + CONV + 1, :] = value_taps_out[0 : CONV + 1, :]
        at += CONV + 1
        local_rows[at : at + 1, :] = gate_gain_out[0:1, :]
        local_rows[at + 1 : at + 2, :] = jnp.concatenate(
            [steps_out[0:1, :], steps_out[1:2, :], head_sum(skip_out[...], to_heads)[0:1, :]],
            axis=1,
        )
        shared_rows[...] = jnp.zeros_like(shared_rows)
        shared_rows[0 : CONV + 1, :] = state_taps_out[0 : CONV + 1, :]

        _, tall, _ = pieces_out[0].shape
        count = small_rows(side**2, channels)
        slabs[...] = jnp.zeros_like(slabs)
        for d in range(side**2):
            at = 0
            for ref in (local_rows, shared_rows):
                each = ref.shape[0] // side**2
                for j in range(d * each, (d + 1) * each):
                    for lanes in range(0, ref.shape[1], LANES):
                        mine = ref[j : j + 1, lanes : lanes + LANES]
                        high = mine.astype(bf16).astype(f32)
                        slabs[d, at : at + 1, :] = high
                        slabs[d, count + at : count + at + 1, :] = mine - high
                        at += 1
        rows = channels // side
        for k, piece in enumerate(pieces_out):
            for j in range(side):
                y, x = block_of(place, lax.rem(place[3 + place[1]] + k, side), j)
                here = pl.ds(pl.multiple_of((y * side + x) * tall, tall), tall)
                piece[j, :, 0 : 2 * channels] = weight_total[here, 0 : 2 * channels].astype(bf16)
                for c in range(width // channels):
                    piece[j, c * rows : (c + 1) * rows, 2 * channels : 3 * channels] = out_total[
                        x,
                        pl.ds(pl.multiple_of(y * rows, rows), rows),
                        c * channels : (c + 1) * channels,
                    ].astype(bf16)
                piece[j, :, 3 * channels :] = slabs[y * side + x].astype(bf16)

        upper = place[1] == 0
        tall = keep_out.shape[1]
        for z in range(4):
            even = weight_total[2 * z * tall : (2 * z + 1) * tall, 2 * channels :].astype(bf16)
            odd = weight_total[(2 * z + 1) * tall : (2 * z + 2) * tall, 2 * channels :].astype(
                bf16
            )
            keep_out[z] = jnp.where(upper, even, odd)
            send_out[z] = jnp.where(upper, odd, even)


def block_of(place, first, second):
    core = place[1]
    return first + core * (second - first), second + core * (first - second)


def small_rows(pieces, channels):
    return (LOCAL * channels + SHARED * 2 * STATE) // LANES // pieces


def line_kernel(place, *refs):
    *pieces, out = refs
    side = len(pieces)
    for k, piece in enumerate(pieces):
        out[lax.rem(place[4 - place[1]] + side - k, side)] = piece[...]


def chip_kernel(place, keep, got, *outs):
    for k, out in enumerate(outs):
        z = lax.rem(place[0] + k, 4)
        out[...] = (keep[z].astype(f32) + got[z].astype(f32)).astype(bf16)


def tile_at(t):
    rows, lanes = 8 * (t // 2), LANES * (t % 2)
    return slice(rows, rows + 8), slice(lanes, lanes + LANES)


def share_kernel(side, place, own, one, two, three, *refs):
    outs, tiles = refs[:-1], refs[-1]
    total = total_of((own, one, two, three))
    count = tiles.shape[0]
    for t in range(count):
        tiles[t] = total[tile_at(t)]
    each = count // side**2
    for k, out in enumerate(outs):
        for j in range(side):
            y, x = block_of(place, lax.rem(place[3 + place[1]] + k, side), j)
            slab = [tiles[(y * side + x) * each + i] for i in range(each)]
            below = out.shape[1] - 8 * each
            out[j] = jnp.concatenate(slab + [jnp.zeros((below, LANES), f32)], axis=0).astype(bf16)


def total_of(pieces):
    total = pieces[0][...].astype(f32)
    for piece in pieces[1:]:
        total = total + piece[...].astype(f32)
    return total


def line_sum_kernel(plain, at, place, *refs):
    side = len(refs) // 3
    pieces, shares, outs = refs[:side], refs[side : 2 * side], refs[2 * side :]
    tall = shares[0].shape[1]
    for k, out in enumerate(outs):
        j = lax.rem(place[4 - place[1]] + k, side)
        total = total_of([ref.at[j] for ref in pieces])
        share = total_of([ref.at[j] for ref in shares])
        out[:, :plain] = total[:, :plain].astype(bf16)
        out[:, plain:] = jnp.concatenate(
            [total[:at, plain:], share, total[at + tall :, plain:]], axis=0
        ).astype(bf16)


def block_sum_kernel(plain, count, gains, *refs):
    *pieces, norm_gain, out = refs
    total = total_of(pieces)
    out[:, :plain] = total[:, :plain].astype(bf16)
    small = total[:count, plain:] + total[count : 2 * count, plain:]
    gain = jnp.concatenate(
        [norm_gain[0:1, j * LANES : (j + 1) * LANES] for j in range(gains)], axis=0
    )
    at = 2 * (count + gains)
    out[:, plain:] = jnp.concatenate(
        high_and_low(small) + high_and_low(gain) + [total[at:, plain:]], axis=0
    ).astype(bf16)


def high_and_low(rows):
    high = rows.astype(bf16).astype(f32)
    return [high, rows - high]


def unpack_kernel(side, place, *refs):
    pieces = refs[:side]
    value_out, gate_out, out_out, wide, sems = refs[side:]
    _, _, tall, channels = wide.shape
    rows, width = out_out.shape[0] // side, out_out.shape[1] // side
    copies = []

    def send(source, target):
        copies.append(pltpu.make_async_copy(source, target, sems.at[len(copies)]))
        copies[-1].start()

    for k, piece in enumerate(pieces):
        first = lax.rem(place[3 + place[1]] + side - k, side)
        for j in range(side):
            y, x = block_of(place, first, j)
            at = k * side + j
            here = pl.ds(pl.multiple_of((y * side + x) * tall, tall), tall)
            for c in range(3):
                wide[at, c] = piece[j, :, c * channels : (c + 1) * channels].astype(f32)
            send(wide.at[at, 0], value_out.at[here])
            send(wide.at[at, 1], gate_out.at[here])
            for c in range(width // channels):
                send(
                    wide.at[at, 2, pl.ds(c * rows, rows)],
                    out_out.at[
                        pl.ds(pl.multiple_of(y * rows, rows), rows),
                        pl.ds(pl.multiple_of(x * width + c * channels, channels), channels),
                    ],
                )
    for copy in copies:
        copy.wait()


def small_kernel(heads, side, count, gains, channels, place, *refs):
    pieces = refs[:side]
    (
        step_out,
        step_bias_out,
        decay_out,
        skip_out,
        value_taps_out,
        value_bias_out,
        gate_gain_out,
        share_out,
        small_at,
        gain_at,
        tiles,
    ) = refs[side:]
    each = tiles.shape[0] // side**2
    for k, piece in enumerate(pieces):
        first = lax.rem(place[3 + place[1]] + side - k, side)
        for j in range(side):
            y, x = block_of(place, first, j)
            d = y * side + x
            tile = piece[j, :, piece.shape[2] - LANES :].astype(f32)
            small_at[d] = tile[:count, :] + tile[count : 2 * count, :]
            at = 2 * count
            gain_at[d] = tile[at : at + gains, :] + tile[at + gains : at + 2 * gains, :]
            at += 2 * gains
            for i in range(each):
                tiles[d * each + i] = tile[at + 8 * i : at + 8 * (i + 1), :]
    fold, across = step_out.shape[1] // channels, channels // LANES
    own, ours = LOCAL // side**2, SHARED // side**2

    def local(row, tile):
        at = row % own * across + tile
        return small_at[row // own, at : at + 1, :]

    def shared(row, tile):
        at = own * across + row % ours * (2 * STATE // LANES) + tile
        return small_at[row // ours, at : at + 1, :]

    for h in range(heads):
        for q in range(fold):
            for t in range(across):
                at = q * channels + t * LANES
                step_out[h : h + 1, at : at + LANES] = local(h * fold + q, t)
    row = heads * fold
    for t in range(across):
        lanes = slice(t * LANES, (t + 1) * LANES)
        for k in range(CONV):
            value_taps_out[k : k + 1, lanes] = local(row + k, t)
        value_bias_out[lanes] = local(row + CONV, t)[0]
        gate_gain_out[lanes] = local(row + CONV + 1, t)[0]
    for t, out in enumerate((step_bias_out, decay_out, skip_out)):
        out[...] = local(row + CONV + 2, t)[:, :heads]

    gain = gain_at[0]
    for d in range(1, side**2):
        gain = gain + gain_at[d]
    rows = [gain[t : t + 1, :] for t in range(gains)]
    rows += [shared(k, t) for k in range(CONV + 1) for t in range(2 * STATE // LANES)]
    pairs = jnp.concatenate(
        [jnp.concatenate(rows[i : i + 2], axis=1) for i in range(0, len(rows), 2)], axis=0
    )
    below = jnp.zeros((SHARED - pairs.shape[0], 2 * STATE), f32)
    share = jnp.concatenate(
        [
            jnp.concatenate([tiles[t], tiles[t + 1]], axis=1)
            for t in range(0, tiles.shape[0], 2)
        ]
        + [jnp.concatenate([part, below], axis=0) for part in high_and_low(pairs)],
        axis=0,
    )
    share_out[...] = share.astype(bf16)


def join_kernel(gains, place, *refs):
    mine, other = refs[:4], refs[4:8]
    state_out, norm_gain_out, taps_out, bias_out = refs[8:]
    tall = state_out.shape[0] // 8
    sums = []
    for k in range(4):
        z = lax.rem(place[0] + 4 - k, 4)
        small = []
        for piece, core in ((mine[k], place[1]), (other[k], 1 - place[1])):
            here = pl.ds(pl.multiple_of((2 * z + core) * tall, tall), tall)
            state_out[here, :] = piece[:tall, :].astype(f32)
            small.append(
                piece[tall : tall + SHARED, :].astype(f32) + piece[tall + SHARED :, :].astype(f32)
            )
        sums.append(small[0] + small[1])
    total = (sums[0] + sums[2]) + (sums[1] + sums[3])
    wide = total.shape[1]
    for t in range(gains * LANES // wide):
        norm_gain_out[t * wide : (t + 1) * wide] = total[t]
    at = gains * LANES // wide
    taps_out[...] = total[at : at + CONV, :]
    bias_out[...] = total[at + CONV]


def output_kernel(inner, total, tokens, stats, out):
    scale, _ = stats_columns(stats[...], inner)
    out[...] = (tokens[...].astype(f32) + scale * total[...].astype(f32)).astype(bf16)


def grad_kernel(total, tokens, cotangent, norm_gain, out):
    x = tokens[...].astype(f32)
    inverse = lax.rsqrt(jnp.mean(x * x, axis=1, keepdims=True) + epsilon)
    scaled = total[...].astype(f32) * row_of(norm_gain)
    moment = jnp.mean(scaled * x, axis=1, keepdims=True)
    grad = inverse * scaled - x * (inverse * inverse * inverse * moment)
    out[...] = (cotangent[...].astype(f32) + grad).astype(bf16)


def whole(array):
    zeros = (0,) * array.ndim
    return pl.BlockSpec(array.shape, lambda i: zeros)


def in_scalars():
    return pl.BlockSpec(memory_space=pltpu.SMEM)


def by_rows(width, steps=None, rows=ROWS):
    if steps is None:
        return pl.BlockSpec((rows, width), lambda i: (i, 0))
    return pl.BlockSpec((rows, width), lambda i: (steps - 1 - i, 0))


def swap_core(x):
    return lax.ppermute(x, "tensor", [(i, i ^ 1) for i in range(8)])


def move_z(x, k):
    return lax.ppermute(x, "tensor", [(i, (i + 2 * k) % 8) for i in range(8)])


def move_dp(x, k, side, stage):
    pairs = []
    for y in range(side):
        for x_at in range(side):
            for t in range(8):
                if (t + stage) % 2 == 0:
                    to = (y + k) % side * side + x_at
                else:
                    to = y * side + (x_at + k) % side
                pairs.append(((y * side + x_at) * 8 + t, to * 8 + t))
    return lax.ppermute(x, ("dp", "tensor"), pairs)


def after(x, *others):
    return lax.optimization_barrier((x,) + others)[0]


free = pl.CostEstimate(flops=0, bytes_accessed=0, transcendentals=0)


def at_place(kernel, place, operands, grid, in_specs, out_specs, out_shape, scratch=()):
    return pl.pallas_call(
        kernel,
        grid_spec=pltpu.PrefetchScalarGridSpec(
            num_scalar_prefetch=1,
            grid=grid,
            in_specs=in_specs,
            out_specs=out_specs,
            scratch_shapes=scratch,
        ),
        out_shape=out_shape,
        compiler_params=pltpu.CompilerParams(
            dimension_semantics=("arbitrary",) * len(grid), vmem_limit_bytes=SMALL_VMEM
        ),
        cost_estimate=free,
    )(place, *operands)


in_vmem = pl.BlockSpec(memory_space=pltpu.VMEM)


def fixed(*shape):
    return pl.BlockSpec(shape, lambda *_: (0,) * len(shape))


def on_device(
    tokens,
    norm_gain,
    in_gate,
    in_value,
    in_state,
    in_step,
    step_bias,
    decay_log,
    skip_gain,
    conv_value_kernel,
    conv_value_bias,
    conv_state_kernel,
    conv_state_bias,
    gate_gain,
    out_weight,
    cotangent,
):
    features = tokens.shape[1]
    channels = in_gate.shape[1]
    heads = step_bias.shape[0]
    inner = channels * lax.axis_size("tensor")
    steps = LEN // ROWS
    parts = ROWS // Q
    dp = lax.axis_size("dp")
    side = math.isqrt(dp)
    me = lax.axis_index("tensor")
    row = lax.axis_index("dp")
    place = jnp.stack([me // 2, me % 2, me, row // side, row % side]).astype(jnp.int32)

    step_weight = in_step.T
    sds = jax.ShapeDtypeStruct
    params = pltpu.CompilerParams(
        dimension_semantics=("arbitrary",), vmem_limit_bytes=VMEM
    )
    stats_rows = pl.BlockSpec((8, ROWS), lambda i: (0, i))
    memory_rows = lambda at: pl.BlockSpec((parts, STATE, channels), lambda i: (at(i), 0, 0))

    (
        normed,
        gate_pre,
        value_pre,
        value_conv,
        state_pre,
        state_conv,
        step_pre,
        mixed,
        back,
        part,
        memories,
        stats,
    ) = pl.pallas_call(
        partial(forward_kernel, heads),
        grid=(steps,),
        in_specs=[
            by_rows(features),
            whole(norm_gain),
            whole(in_gate),
            whole(in_value),
            whole(in_state),
            whole(step_weight),
            in_scalars(),
            in_scalars(),
            in_scalars(),
            whole(conv_value_kernel),
            whole(conv_value_bias),
            whole(conv_state_kernel),
            whole(conv_state_bias),
            whole(gate_gain),
            whole(out_weight),
            by_rows(features),
        ],
        out_specs=[
            by_rows(features),
            by_rows(channels),
            by_rows(channels),
            by_rows(channels),
            by_rows(2 * STATE),
            by_rows(2 * STATE),
            by_rows(LANES),
            by_rows(channels),
            by_rows(channels),
            by_rows(features),
            memory_rows(lambda i: i),
            stats_rows,
        ],
        out_shape=[
            sds((LEN, features), bf16),
            sds((LEN, channels), f32),
            sds((LEN, channels), f32),
            sds((LEN, channels), f32),
            sds((LEN, 2 * STATE), f32),
            sds((LEN, 2 * STATE), f32),
            sds((LEN, LANES), f32),
            sds((LEN, channels), f32),
            sds((LEN, channels), f32),
            sds((LEN, features), bf16),
            sds((LEN // Q, STATE, channels), bf16),
            sds((8, LEN), f32),
        ],
        scratch_shapes=[
            pltpu.VMEM((ROWS + HALO, channels), f32),
            pltpu.VMEM((ROWS + HALO, 2 * STATE), f32),
            pltpu.VMEM((STATE, channels), f32),
        ],
        compiler_params=params,
        cost_estimate=free,
    )(
        tokens,
        norm_gain,
        in_gate,
        in_value,
        in_state,
        step_weight,
        step_bias,
        decay_log,
        skip_gain,
        conv_value_kernel,
        conv_value_bias,
        conv_state_kernel,
        conv_state_bias,
        gate_gain,
        out_weight,
        cotangent,
    )

    out_sum = lax.psum_scatter(part, "tensor", scatter_dimension=0, tiled=True)
    stats = stats + swap_core(stats)
    moved = [move_z(stats, k) for k in (1, 2, 3)]
    stats = (stats + moved[1]) + (moved[0] + moved[2])

    back_rows = partial(by_rows, steps=steps)
    anywhere = pl.BlockSpec(memory_space=pl.ANY)
    lanes = 3 * channels + LANES
    share = features // 8
    tall = features // dp
    part, norm_gain_part, keep, send, *weights = pl.pallas_call(
        partial(backward_kernel, heads, inner, steps, side),
        grid=(steps,),
        in_specs=[
            in_scalars(),
            pl.BlockSpec((8, ROWS), lambda i: (0, steps - 1 - i)),
            back_rows(features),
            back_rows(features),
            back_rows(channels),
            back_rows(channels),
            back_rows(channels),
            back_rows(channels),
            back_rows(channels),
            back_rows(2 * STATE),
            back_rows(2 * STATE),
            back_rows(LANES),
            memory_rows(lambda i: steps - 1 - i),
            whole(gate_gain),
            in_scalars(),
            in_scalars(),
            whole(conv_value_kernel),
            whole(conv_state_kernel),
            whole(norm_gain),
            anywhere,
            anywhere,
            anywhere,
            whole(step_weight),
        ],
        out_specs=[
            back_rows(features),
            fixed(8, features),
            fixed(4, share, 2 * STATE),
            fixed(4, share, 2 * STATE),
        ]
        + [fixed(side, tall, lanes)] * side,
        out_shape=[
            sds((LEN, features), bf16),
            sds((8, features), f32),
            sds((4, share, 2 * STATE), bf16),
            sds((4, share, 2 * STATE), bf16),
        ]
        + [sds((side, tall, lanes), bf16)] * side,
        scratch_shapes=[
            pltpu.VMEM((ROWS + HALO, channels), f32),
            pltpu.VMEM((ROWS + HALO, 2 * STATE), f32),
            pltpu.VMEM((STATE, channels), f32),
            pltpu.VMEM((features, 2 * channels + 2 * STATE), f32),
            pltpu.VMEM((side, channels, features // side), f32),
            pltpu.VMEM((LANES, features), f32),
            pltpu.VMEM((8, channels), f32),
            pltpu.VMEM((8, channels), f32),
            pltpu.VMEM((8, 2 * STATE), f32),
            pltpu.VMEM((8, channels), f32),
            pltpu.VMEM((8, LANES), f32),
            pltpu.VMEM((LOCAL, channels), f32),
            pltpu.VMEM((SHARED, 2 * STATE), f32),
            pltpu.VMEM((dp, tall, LANES), f32),
            pltpu.VMEM((features, channels), bf16),
            pltpu.VMEM((features, channels), bf16),
            pltpu.VMEM((features, 2 * STATE), bf16),
            pltpu.SemaphoreType.DMA((3,)),
        ],
        compiler_params=params,
        cost_estimate=free,
    )(
        place,
        stats,
        normed,
        cotangent,
        gate_pre,
        mixed,
        back,
        value_pre,
        value_conv,
        state_pre,
        state_conv,
        step_pre,
        memories,
        gate_gain,
        decay_log,
        skip_gain,
        conv_value_kernel,
        conv_state_kernel,
        norm_gain,
        in_gate,
        in_value,
        in_state,
        step_weight,
    )
    out_sum = after(out_sum, part)
    weights[0] = after(weights[0], out_sum)
    weights = [weights[0]] + [
        move_dp(after(weights[k], weights[0]), k, side, 0) for k in range(1, side)
    ]

    grad_sum = lax.psum_scatter(part, "tensor", scatter_dimension=0, tiled=True)

    got = swap_core(send)
    shares = at_place(
        chip_kernel,
        place,
        (keep, got),
        (1,),
        [in_vmem] * 2,
        [fixed(share, 2 * STATE)] * 4,
        [sds((share, 2 * STATE), bf16)] * 4,
    )
    tiles = share * 2 * STATE // (8 * LANES)
    share_tall = -(-tiles * 8 // dp // 16) * 16
    shares = at_place(
        partial(share_kernel, side),
        place,
        [shares[0]] + [move_z(shares[k], k) for k in (1, 2, 3)],
        (1,),
        [in_vmem] * 4,
        [fixed(side, share_tall, LANES)] * side,
        [sds((side, share_tall, LANES), bf16)] * side,
        [pltpu.VMEM((tiles, 8, LANES), f32)],
    )
    shares = [shares[0]] + [move_dp(shares[k], k, side, 0) for k in range(1, side)]

    count = small_rows(dp, channels)
    gains = features // LANES
    plain = 3 * channels
    weights = at_place(
        partial(line_sum_kernel, plain, 2 * (count + gains)),
        place,
        weights + shares,
        (1,),
        [in_vmem] * (2 * side),
        [fixed(tall, lanes)] * side,
        [sds((tall, lanes), bf16)] * side,
    )
    weights = [weights[0]] + [move_dp(weights[k], k, side, 1) for k in range(1, side)]
    grad_sum = lax.all_gather(after(grad_sum, weights[1]), "tensor", tiled=True)


    vmem = pltpu.CompilerParams(vmem_limit_bytes=SMALL_VMEM)
    weights = pl.pallas_call(
        partial(block_sum_kernel, plain, count, gains),
        in_specs=[in_vmem] * (side + 1),
        out_shape=sds((tall, lanes), bf16),
        compiler_params=vmem,
        cost_estimate=free,
    )(*weights, norm_gain_part)
    out_sum = lax.all_gather(after(out_sum, weights), "tensor", tiled=True)
    weights = [weights] + [move_dp(weights, k, side, 1) for k in range(1, side)]
    weights = at_place(
        line_kernel,
        place,
        weights,
        (1,),
        [in_vmem] * side,
        fixed(side, tall, lanes),
        sds((side, tall, lanes), bf16),
    )
    weights = [weights] + [move_dp(weights, k, side, 0) for k in range(1, side)]
    wide = LEN // 2
    wide_rows = by_rows(features, rows=wide)
    grad_tokens = pl.pallas_call(
        grad_kernel,
        grid=(LEN // wide,),
        in_specs=[wide_rows] * 3 + [whole(norm_gain)],
        out_specs=wide_rows,
        out_shape=sds((LEN, features), bf16),
        compiler_params=params,
        cost_estimate=free,
    )(grad_sum, tokens, cotangent, norm_gain)
    block_output = pl.pallas_call(
        partial(output_kernel, inner),
        grid=(LEN // wide,),
        in_specs=[wide_rows, wide_rows, pl.BlockSpec((8, wide), lambda i: (0, i))],
        out_specs=wide_rows,
        out_shape=sds((LEN, features), bf16),
        compiler_params=params,
        cost_estimate=free,
    )(after(out_sum, grad_tokens), tokens, stats)
    weights[0] = after(weights[0], grad_tokens)

    smalls = [
        (heads, features),
        (1, heads),
        (1, heads),
        (1, heads),
        (CONV, channels),
        (channels,),
        (channels,),
    ]
    share_rows = share + 2 * SHARED
    *smalls, state = at_place(
        partial(small_kernel, heads, side, count, gains, channels),
        place,
        weights,
        (1,),
        [in_vmem] * side,
        [fixed(*shape) for shape in smalls] + [fixed(share_rows, 2 * STATE)],
        [sds(shape, f32) for shape in smalls] + [sds((share_rows, 2 * STATE), bf16)],
        [
            pltpu.VMEM((dp, count, LANES), f32),
            pltpu.VMEM((dp, gains, LANES), f32),
            pltpu.VMEM((tiles, 8, LANES), f32),
        ],
    )
    grad_in_step = smalls[0].T
    (
        grad_step_bias,
        grad_decay_log,
        grad_skip_gain,
        grad_conv_value_kernel,
        grad_conv_value_bias,
        grad_gate_gain,
    ) = (a[0] if a.shape[0] == 1 else a for a in smalls[1:])
    state = [state] + [move_z(state, k) for k in (1, 2, 3)]
    across = features // side // channels
    weights[0] = after(weights[0], state[0])
    grad_in_value, grad_in_gate, grad_out_weight = at_place(
        partial(unpack_kernel, side),
        place,
        weights,
        (1,),
        [in_vmem] * side,
        [anywhere] * 3,
        [
            sds((features, channels), f32),
            sds((features, channels), f32),
            sds((channels, features), f32),
        ],
        [
            pltpu.VMEM((dp, 3, tall, channels), f32),
            pltpu.SemaphoreType.DMA((dp * (2 + across),)),
        ],
    )
    state[0] = after(state[0], grad_in_value, block_output)
    grad_in_state, grad_norm_gain, grad_conv_state_kernel, grad_conv_state_bias = at_place(
        partial(join_kernel, gains),
        place,
        state + [swap_core(piece) for piece in state],
        (1,),
        [in_vmem] * 8,
        [
            fixed(features, 2 * STATE),
            fixed(features),
            fixed(CONV, 2 * STATE),
            fixed(2 * STATE),
        ],
        [
            sds((features, 2 * STATE), f32),
            sds((features,), f32),
            sds((CONV, 2 * STATE), f32),
            sds((2 * STATE,), f32),
        ],
    )
    return (
        block_output,
        grad_tokens,
        grad_norm_gain,
        grad_in_gate,
        grad_in_value,
        grad_in_state,
        grad_in_step,
        grad_step_bias,
        grad_decay_log,
        grad_skip_gain,
        grad_conv_value_kernel,
        grad_conv_value_bias,
        grad_conv_state_kernel,
        grad_conv_state_bias,
        grad_gate_gain,
        grad_out_weight,
    )


def solution(mesh):
    placed = (
        P("dp", None),
        P(),
        P(None, "tensor"),
        P(None, "tensor"),
        P(),
        P(None, "tensor"),
        P("tensor"),
        P("tensor"),
        P("tensor"),
        P(None, "tensor"),
        P("tensor"),
        P(),
        P(),
        P("tensor"),
        P("tensor", None),
        P("dp", None),
    )
    return jax.shard_map(
        on_device,
        mesh=mesh,
        in_specs=placed,
        out_specs=(
            P("dp", None),
            P("dp", None),
            P(),
            P(None, "tensor"),
            P(None, "tensor"),
            P(),
            P(None, "tensor"),
            P("tensor"),
            P("tensor"),
            P("tensor"),
            P(None, "tensor"),
            P("tensor"),
            P(),
            P(),
            P("tensor"),
            P("tensor", None),
        ),
        check_vma=False,
    )
```

```python
import math
from functools import partial

import jax
import jax.numpy as jnp
from jax import lax
from jax.experimental import pallas as pl
from jax.experimental.pallas import tpu as pltpu
from jax.sharding import PartitionSpec as P

STATE = 128
CONV = 4
LEN = 1024
HEAD = 64
Q = 128
ROWS = 256
LANES = 128
HALO = 8
LOCAL = 32
SHARED = 16

epsilon = 1e-05
f32 = jnp.float32
bf16 = jnp.bfloat16
VMEM = 60 * 1024 * 1024
SMALL_VMEM = 40 * 1024 * 1024


def mm(a, b):
    return lax.dot_general(a, b, (((1,), (0,)), ((), ())), preferred_element_type=f32)


def parts_of(x):
    high = x.astype(bf16)
    rest = x - high.astype(f32)
    middle = rest.astype(bf16)
    return [high, middle, (rest - middle.astype(f32)).astype(bf16)]


def sum_rows(triangle, x):
    width = x.shape[1]
    total = mm(triangle, jnp.concatenate(parts_of(x), axis=1))
    return total[:, :width] + total[:, width : 2 * width] + total[:, 2 * width :]


def mm_nt(a, b):
    return lax.dot_general(a, b, (((1,), (1,)), ((), ())), preferred_element_type=f32)


def mm_tn(a, b):
    return lax.dot_general(a, b, (((0,), (0,)), ((), ())), preferred_element_type=f32)


def sigmoid(v):
    return 1.0 / (1.0 + jnp.exp(-v))


def softplus(v):
    return jnp.maximum(v, 0.0) + jnp.log1p(jnp.exp(-jnp.abs(v)))


def iota(shape, axis):
    return lax.broadcasted_iota(jnp.int32, shape, axis)


def column(m, at):
    return jnp.broadcast_to(m[:, at : at + 1], (m.shape[0], LANES))


def low_half(rows):
    return iota((rows, LANES), 1) < HEAD


def expand(m, heads):
    half = low_half(m.shape[0])
    return jnp.concatenate(
        [jnp.where(half, column(m, h), column(m, h + 1)) for h in range(0, heads, 2)], axis=1
    )


def split_heads(pair):
    half = low_half(pair.shape[0])
    zero = jnp.zeros_like(pair)
    return jnp.concatenate([jnp.where(half, pair, zero), jnp.where(half, zero, pair)], axis=0)


def head_sum(m, channels_to_heads):
    high = m.astype(bf16)
    low = (m - high.astype(f32)).astype(bf16)
    return mm(high, channels_to_heads) + mm(low, channels_to_heads)


def head_row(scalars, heads):
    lane = iota((1, LANES), 1)
    row = jnp.zeros((1, LANES), f32)
    for h in range(heads):
        row = jnp.where(lane == h, scalars[h], row)
    return row


def rate_row(decay_log, heads):
    return jnp.where(iota((1, LANES), 1) < heads, -jnp.exp(head_row(decay_log, heads)), 0.0)


def channel_row(scalars, heads):
    half = low_half(1)
    return jnp.concatenate(
        [jnp.where(half, scalars[h], scalars[h + 1]) for h in range(0, heads, 2)], axis=1
    )


def all_lanes(rows):
    below = jnp.zeros((LANES - rows.shape[0], rows.shape[1]), rows.dtype)
    return jnp.concatenate([rows, below], axis=0)


def row_of(ref):
    return ref[...].reshape(1, ref.shape[0])


def forward_kernel(
    heads,
    tokens,
    norm_gain,
    in_gate,
    in_value,
    in_state,
    in_step,
    step_bias,
    decay_log,
    skip_gain,
    value_kernel,
    value_bias,
    state_kernel,
    state_bias,
    gate_gain,
    out_weight,
    cotangent,
    normed_out,
    gate_out,
    value_out,
    value_conv_out,
    state_out,
    state_conv_out,
    step_out,
    mixed_out,
    back_out,
    part_out,
    memory_out,
    stats_out,
    value_buf,
    state_buf,
    memory,
):
    @pl.when(pl.program_id(0) == 0)
    def _():
        value_buf[0:HALO, :] = jnp.zeros((HALO, value_buf.shape[1]), f32)
        state_buf[0:HALO, :] = jnp.zeros((HALO, state_buf.shape[1]), f32)
        memory[...] = jnp.zeros_like(memory)

    x = tokens[...].astype(f32)
    inverse = lax.rsqrt(jnp.mean(x * x, axis=1, keepdims=True) + epsilon)
    normed = (x * inverse * row_of(norm_gain)).astype(bf16)
    normed_out[...] = normed
    state_pre = mm(normed, in_state[...])
    value_pre = mm(normed, in_value[...])
    step_pre = mm_nt(normed, all_lanes(in_step[...])) + head_row(step_bias, heads)
    gate_pre = mm(normed, in_gate[...])
    gate_out[...] = gate_pre
    value_out[...] = value_pre
    state_out[...] = state_pre
    step_out[...] = step_pre

    def conv(buf, pre, kernel, bias):
        buf[HALO:, :] = pre
        result = row_of(bias) + buf[HALO - 3 : HALO - 3 + ROWS, :] * kernel[0:1, :]
        for k in range(1, CONV):
            result = result + buf[HALO - 3 + k : HALO - 3 + k + ROWS, :] * kernel[k : k + 1, :]
        buf[0:HALO, :] = buf[ROWS : ROWS + HALO, :]
        return result

    value_conv = conv(value_buf, value_pre, value_kernel, value_bias)
    value_conv_out[...] = value_conv
    values = (value_conv * sigmoid(value_conv)).astype(bf16)
    state_conv = conv(state_buf, state_pre, state_kernel, state_bias)
    state_conv_out[...] = state_conv
    states = (state_conv * sigmoid(state_conv)).astype(bf16)
    step = softplus(step_pre)
    log_step = step * rate_row(decay_log, heads)
    skip = channel_row(skip_gain, heads)

    causal = iota((Q, Q), 0) >= iota((Q, Q), 1)
    tri = jnp.where(causal, 1.0, 0.0).astype(bf16)
    mixed_parts = []
    for part in range(ROWS // Q):
        rows = slice(part * Q, (part + 1) * Q)
        b = states[rows, :STATE]
        c = states[rows, STATE:]
        v = values[rows, :].astype(f32)
        dt = step[rows, :]
        decay = sum_rows(tri, log_step[rows, :])
        decay_t = decay.T
        wide = expand(decay, heads)
        dt_wide = expand(dt, heads)
        grown = jnp.exp(wide)
        scaled = v * dt_wide
        scaled_low = scaled.astype(bf16)
        cb = mm_nt(c, b)
        held = memory[...]
        held_low = held.astype(bf16)
        memory_out[part] = held_low
        y = mm(c, held_low) * grown + skip * v
        inside = []
        for h in range(0, heads, 2):
            blocks = []
            for at in (h, h + 1):
                gap = column(decay, at) - decay_t[at : at + 1, :]
                blocks.append((cb * jnp.exp(jnp.where(causal, gap, -1e30))).astype(bf16))
            pair = scaled_low[:, h * HEAD : (h + 2) * HEAD]
            inside.append(mm(jnp.concatenate(blocks, axis=1), split_heads(pair)))
        mixed_parts.append(y + jnp.concatenate(inside, axis=1))
        ended = (scaled * jnp.exp(wide[Q - 1 : Q, :] - wide)).astype(bf16)
        memory[...] = held * grown[Q - 1 : Q, :] + mm_tn(b, ended)

    mixed = jnp.concatenate(mixed_parts, axis=0)
    mixed_out[...] = mixed
    gated = mixed * gate_pre * sigmoid(gate_pre)
    back = mm_nt(cotangent[...], out_weight[...])
    back_out[...] = back
    gained = gated * row_of(gate_gain)
    part_out[...] = mm(gained.astype(bf16), out_weight[...]).astype(bf16)
    squares = jnp.sum(gated * gated, axis=1, keepdims=True)
    moment = jnp.sum(back * gained, axis=1, keepdims=True)
    lane = iota((ROWS, LANES), 1)
    both = jnp.where(lane == 0, squares, jnp.where(lane == 1, moment, 0.0))
    stats_out[...] = both.T[0:8, :]


def stats_columns(stats, inner):
    padded = jnp.concatenate([stats, jnp.zeros((LANES - 8, stats.shape[1]), f32)], axis=0).T
    scale = lax.rsqrt(padded[:, 0:1] / inner + epsilon)
    return scale, padded[:, 1:2] / inner


def add_row(ref, at, rows):
    ref[at : at + 1, :] += jnp.sum(rows, axis=0, keepdims=True)


def backward_kernel(
    heads,
    inner,
    steps,
    side,
    place,
    stats,
    normed,
    cotangent,
    gate,
    mixed_in,
    back_in,
    value,
    value_conv,
    state,
    state_conv,
    step_in,
    memory_in,
    gate_gain,
    decay_log,
    skip_gain,
    value_kernel,
    state_kernel,
    norm_gain,
    in_gate_at,
    in_value_at,
    in_state_at,
    in_step,
    part_out,
    norm_gain_out,
    keep_out,
    send_out,
    *refs,
):
    pieces_out = refs[:side]
    (
        value_buf,
        state_buf,
        adjoint,
        weight_total,
        out_total,
        step_total,
        gate_gain_out,
        value_taps_out,
        state_taps_out,
        skip_out,
        steps_out,
        local_rows,
        shared_rows,
        slabs,
        in_all,
        sems,
    ) = refs[side:]
    wide = in_gate_at.shape[1]
    weights = [
        pltpu.make_async_copy(source, target, sems.at[i])
        for i, (source, target) in enumerate(
            (
                (in_value_at, in_all.at[:, pl.ds(0, wide)]),
                (in_gate_at, in_all.at[:, pl.ds(wide, wide)]),
                (in_state_at, in_all.at[:, pl.ds(2 * wide, 2 * STATE)]),
            )
        )
    ]

    @pl.when(pl.program_id(0) == 0)
    def _():
        for copy in weights:
            copy.start()
        norm_gain_out[...] = jnp.zeros_like(norm_gain_out)
        value_buf[ROWS:, :] = jnp.zeros((HALO, value_buf.shape[1]), f32)
        state_buf[ROWS:, :] = jnp.zeros((HALO, state_buf.shape[1]), f32)
        adjoint[...] = jnp.zeros_like(adjoint)
        for ref in (
            weight_total,
            out_total,
            step_total,
            gate_gain_out,
            value_taps_out,
            state_taps_out,
            skip_out,
            steps_out,
        ):
            ref[...] = jnp.zeros_like(ref)

    scale, moment = stats_columns(stats[...], inner)
    mixed = mixed_in[...]
    back = back_in[...]
    pre = gate[...]
    bent = sigmoid(pre)
    silu = pre * bent
    gated = mixed * silu
    scaled = gated * scale
    gain = row_of(gate_gain)
    add_row(gate_gain_out, 0, back * scaled)
    grad_gated = scale * (back * gain) - scaled * (scale * scale * moment)
    grad_mixed = grad_gated * silu
    round_gate = (grad_gated * mixed * (bent * (1.0 + pre * (1.0 - bent)))).astype(bf16)
    outgoing = (scaled * gain).astype(bf16)
    width = out_total.shape[2]
    out_terms = mm_tn(outgoing, cotangent[...])
    for x in range(side):
        out_total[x] += out_terms[:, x * width : (x + 1) * width]

    value_at = value_conv[...]
    value_bent = sigmoid(value_at)
    values = (value_at * value_bent).astype(bf16)
    state_at = state_conv[...]
    state_bent = sigmoid(state_at)
    states = (state_at * state_bent).astype(bf16)
    step_pre = step_in[...]
    step = softplus(step_pre)
    rate = rate_row(decay_log, heads)
    skip = channel_row(skip_gain, heads)
    log_step = step * rate

    ahead = iota((Q, Q), 1) >= iota((Q, Q), 0)
    tri = jnp.where(iota((Q, Q), 0) >= iota((Q, Q), 1), 1.0, 0.0).astype(bf16)
    tri_both = jnp.concatenate(
        [
            jnp.where(ahead, 1.0, 0.0),
            jnp.where(iota((Q, Q), 0) > iota((Q, Q), 1), 1.0, 0.0),
        ],
        axis=1,
    ).astype(bf16)
    lane = iota((Q, LANES), 1)
    row8 = iota((8, Q), 0)
    channels = heads * HEAD
    to_heads = jnp.where(
        lax.shift_right_logical(iota((channels, LANES), 0), 6) == iota((channels, LANES), 1), 1.0, 0.0
    ).astype(bf16)
    parts = ROWS // Q
    grad_value_parts = [None] * parts
    grad_state_parts = [None] * parts
    grad_step_parts = [None] * parts
    for part in reversed(range(parts)):
        rows = slice(part * Q, (part + 1) * Q)
        b = states[rows, :STATE]
        c = states[rows, STATE:]
        v_low = values[rows, :]
        v = v_low.astype(f32)
        dt = step[rows, :]
        dy = grad_mixed[rows, :]
        dy_low = dy.astype(bf16)
        decay = sum_rows(tri, log_step[rows, :])
        decay_t = decay.T
        wide = expand(decay, heads)
        dt_wide = expand(dt, heads)
        grown = jnp.exp(wide)
        to_end = jnp.exp(wide[Q - 1 : Q, :] - wide)
        held = memory_in[part]
        later = adjoint[...]
        later_low = later.astype(bf16)
        bd = mm(b, later_low)
        cs = mm(c, held)
        bc = mm_nt(b, c)
        dy_grown = dy * grown
        dy_grown_low = dy_grown.astype(bf16)
        at_end = bd * to_end
        inside = []
        grad_bc = jnp.zeros((Q, Q), f32)
        direct = jnp.zeros((Q, LANES), f32)
        row_sums = jnp.zeros((8, Q), f32)
        for h in range(0, heads, 2):
            lanes = slice(h * HEAD, (h + 2) * HEAD)
            v_split = split_heads(v_low[:, lanes])
            grad_pair = mm_nt(v_split, dy_low[:, lanes])
            blocks = []
            for at in (h, h + 1):
                gap = decay_t[at : at + 1, :] - column(decay, at)
                fall = jnp.exp(jnp.where(ahead, gap, -1e30))
                grad_fall = grad_pair[(at - h) * Q : (at - h + 1) * Q, :] * fall
                direct += jnp.where(lane == at, jnp.sum(grad_fall * bc, axis=1, keepdims=True), 0.0)
                grad_one = grad_fall * column(dt, at)
                grad_bc += grad_one
                row_sums += jnp.where(
                    row8 == at, jnp.sum(grad_one * bc, axis=0, keepdims=True), 0.0
                )
                blocks.append((bc * fall).astype(bf16))
            inside.append(mm(jnp.concatenate(blocks, axis=1), split_heads(dy_low[:, lanes])))
        grad_value_parts[part] = dt_wide * (jnp.concatenate(inside, axis=1) + at_end) + skip * dy
        add_row(skip_out, 0, dy * v)
        grown_sum = head_sum(dy_grown * cs, to_heads)
        end_sum = head_sum(at_end * v, to_heads)
        constant = head_sum(
            grown[Q - 1 : Q, :] * jnp.sum(held.astype(f32) * later, axis=0, keepdims=True), to_heads
        )
        row_t = jnp.concatenate([row_sums, jnp.zeros((LANES - 8, Q), f32)], axis=0).T
        grad_log = (
            sum_rows(
                tri_both,
                jnp.concatenate([row_t - direct * dt + grown_sum, end_sum * dt], axis=0),
            )
            + constant
        )
        grad_step = direct + end_sum + rate * grad_log
        grad_step = grad_step * sigmoid(step_pre[rows, :])
        grad_step_parts[part] = grad_step
        add_row(steps_out, 0, grad_step)
        add_row(steps_out, 1, dt * grad_log * rate)
        grad_bc_low = grad_bc.astype(bf16)
        grad_b = mm(grad_bc_low, c) + mm_nt((v * dt_wide * to_end).astype(bf16), later_low)
        grad_c = mm_tn(grad_bc_low, b) + mm_nt(dy_grown_low, held)
        grad_state_parts[part] = jnp.concatenate([grad_b, grad_c], axis=1)
        adjoint[...] = later * grown[Q - 1 : Q, :] + mm_tn(c, dy_grown_low)

    def conv_back(buf, grad, at, bent, pre, kernel, taps_out):
        buf[0:ROWS, :] = grad * (bent * (1.0 + at * (1.0 - bent)))
        result = None
        for k in range(CONV):
            moved = buf[3 - k : 3 - k + ROWS, :]
            term = moved * kernel[k : k + 1, :]
            result = term if result is None else result + term
            add_row(taps_out, k, pre * moved)
        add_row(taps_out, CONV, buf[0:ROWS, :])
        buf[ROWS:, :] = buf[0:HALO, :]
        return result.astype(bf16)

    round_value = conv_back(
        value_buf,
        jnp.concatenate(grad_value_parts, axis=0),
        value_at,
        value_bent,
        value[...],
        value_kernel,
        value_taps_out,
    )
    round_state = conv_back(
        state_buf,
        jnp.concatenate(grad_state_parts, axis=0),
        state_at,
        state_bent,
        state[...],
        state_kernel,
        state_taps_out,
    )
    round_step = jnp.concatenate(grad_step_parts, axis=0).astype(bf16)

    @pl.when(pl.program_id(0) == 0)
    def _():
        for copy in weights:
            copy.wait()

    rounds = jnp.concatenate([round_value, round_gate, round_state], axis=1)
    total = mm_nt(rounds, in_all[...]) + mm(round_step, all_lanes(in_step[...]))
    part_out[...] = total.astype(bf16)
    add_row(norm_gain_out, 0, total * normed[...].astype(f32))
    weight_total[...] += mm_tn(normed[...], rounds)
    step_total[...] += mm_tn(round_step, normed[...])

    @pl.when(pl.program_id(0) == steps - 1)
    def _():
        norm_gain_out[...] = norm_gain_out[...] / row_of(norm_gain)
        fold = step_total.shape[1] // channels
        local_rows[...] = jnp.zeros_like(local_rows)
        for h in range(heads):
            for q in range(fold):
                local_rows[h * fold + q : h * fold + q + 1, :] = step_total[
                    h : h + 1, q * channels : (q + 1) * channels
                ]
        at = heads * fold
        local_rows[at : at + CONV + 1, :] = value_taps_out[0 : CONV + 1, :]
        at += CONV + 1
        local_rows[at : at + 1, :] = gate_gain_out[0:1, :]
        local_rows[at + 1 : at + 2, :] = jnp.concatenate(
            [steps_out[0:1, :], steps_out[1:2, :], head_sum(skip_out[...], to_heads)[0:1, :]],
            axis=1,
        )
        shared_rows[...] = jnp.zeros_like(shared_rows)
        shared_rows[0 : CONV + 1, :] = state_taps_out[0 : CONV + 1, :]

        _, tall, _ = pieces_out[0].shape
        count = small_rows(side**2, channels)
        slabs[...] = jnp.zeros_like(slabs)
        for d in range(side**2):
            at = 0
            for ref in (local_rows, shared_rows):
                each = ref.shape[0] // side**2
                for j in range(d * each, (d + 1) * each):
                    for lanes in range(0, ref.shape[1], LANES):
                        mine = ref[j : j + 1, lanes : lanes + LANES]
                        high = mine.astype(bf16).astype(f32)
                        slabs[d, at : at + 1, :] = high
                        slabs[d, count + at : count + at + 1, :] = mine - high
                        at += 1
        rows = channels // side
        for k, piece in enumerate(pieces_out):
            for j in range(side):
                y, x = block_of(place, lax.rem(place[3 + place[1]] + k, side), j)
                here = pl.ds(pl.multiple_of((y * side + x) * tall, tall), tall)
                piece[j, :, 0 : 2 * channels] = weight_total[here, 0 : 2 * channels].astype(bf16)
                for c in range(width // channels):
                    piece[j, c * rows : (c + 1) * rows, 2 * channels : 3 * channels] = out_total[
                        x,
                        pl.ds(pl.multiple_of(y * rows, rows), rows),
                        c * channels : (c + 1) * channels,
                    ].astype(bf16)
                piece[j, :, 3 * channels :] = slabs[y * side + x].astype(bf16)

        upper = place[1] == 0
        tall = keep_out.shape[1]
        for z in range(4):
            even = weight_total[2 * z * tall : (2 * z + 1) * tall, 2 * channels :].astype(bf16)
            odd = weight_total[(2 * z + 1) * tall : (2 * z + 2) * tall, 2 * channels :].astype(
                bf16
            )
            keep_out[z] = jnp.where(upper, even, odd)
            send_out[z] = jnp.where(upper, odd, even)


def block_of(place, first, second):
    core = place[1]
    return first + core * (second - first), second + core * (first - second)


def small_rows(pieces, channels):
    return (LOCAL * channels + SHARED * 2 * STATE) // LANES // pieces


def line_kernel(place, *refs):
    *pieces, out = refs
    side = len(pieces)
    for k, piece in enumerate(pieces):
        out[lax.rem(place[4 - place[1]] + side - k, side)] = piece[...]


def chip_kernel(place, keep, got, *outs):
    for k, out in enumerate(outs):
        z = lax.rem(place[0] + k, 4)
        out[...] = (keep[z].astype(f32) + got[z].astype(f32)).astype(bf16)


def tile_at(t):
    rows, lanes = 8 * (t // 2), LANES * (t % 2)
    return slice(rows, rows + 8), slice(lanes, lanes + LANES)


def share_kernel(side, place, own, one, two, three, *refs):
    outs, tiles = refs[:-1], refs[-1]
    total = total_of((own, one, two, three))
    count = tiles.shape[0]
    for t in range(count):
        tiles[t] = total[tile_at(t)]
    each = count // side**2
    for k, out in enumerate(outs):
        for j in range(side):
            y, x = block_of(place, lax.rem(place[3 + place[1]] + k, side), j)
            slab = [tiles[(y * side + x) * each + i] for i in range(each)]
            below = out.shape[1] - 8 * each
            out[j] = jnp.concatenate(slab + [jnp.zeros((below, LANES), f32)], axis=0).astype(bf16)


def total_of(pieces):
    total = pieces[0][...].astype(f32)
    for piece in pieces[1:]:
        total = total + piece[...].astype(f32)
    return total


def line_sum_kernel(plain, at, place, *refs):
    side = len(refs) // 3
    pieces, shares, outs = refs[:side], refs[side : 2 * side], refs[2 * side :]
    tall = shares[0].shape[1]
    for k, out in enumerate(outs):
        j = lax.rem(place[4 - place[1]] + k, side)
        total = total_of([ref.at[j] for ref in pieces])
        share = total_of([ref.at[j] for ref in shares])
        out[:, :plain] = total[:, :plain].astype(bf16)
        out[:, plain:] = jnp.concatenate(
            [total[:at, plain:], share, total[at + tall :, plain:]], axis=0
        ).astype(bf16)


def block_sum_kernel(plain, count, gains, *refs):
    *pieces, norm_gain, out = refs
    total = total_of(pieces)
    out[:, :plain] = total[:, :plain].astype(bf16)
    small = total[:count, plain:] + total[count : 2 * count, plain:]
    gain = jnp.concatenate(
        [norm_gain[0:1, j * LANES : (j + 1) * LANES] for j in range(gains)], axis=0
    )
    at = 2 * (count + gains)
    out[:, plain:] = jnp.concatenate(
        high_and_low(small) + high_and_low(gain) + [total[at:, plain:]], axis=0
    ).astype(bf16)


def high_and_low(rows):
    high = rows.astype(bf16).astype(f32)
    return [high, rows - high]


def unpack_kernel(side, place, *refs):
    pieces = refs[:side]
    value_out, gate_out, out_out, wide, sems = refs[side:]
    _, _, tall, channels = wide.shape
    rows, width = out_out.shape[0] // side, out_out.shape[1] // side
    copies = []

    def send(source, target):
        copies.append(pltpu.make_async_copy(source, target, sems.at[len(copies)]))
        copies[-1].start()

    for k, piece in enumerate(pieces):
        first = lax.rem(place[3 + place[1]] + side - k, side)
        for j in range(side):
            y, x = block_of(place, first, j)
            at = k * side + j
            here = pl.ds(pl.multiple_of((y * side + x) * tall, tall), tall)
            for c in range(3):
                wide[at, c] = piece[j, :, c * channels : (c + 1) * channels].astype(f32)
            send(wide.at[at, 0], value_out.at[here])
            send(wide.at[at, 1], gate_out.at[here])
            for c in range(width // channels):
                send(
                    wide.at[at, 2, pl.ds(c * rows, rows)],
                    out_out.at[
                        pl.ds(pl.multiple_of(y * rows, rows), rows),
                        pl.ds(pl.multiple_of(x * width + c * channels, channels), channels),
                    ],
                )
    for copy in copies:
        copy.wait()


def small_kernel(heads, side, count, gains, channels, place, *refs):
    pieces = refs[:side]
    (
        step_out,
        step_bias_out,
        decay_out,
        skip_out,
        value_taps_out,
        value_bias_out,
        gate_gain_out,
        share_out,
        small_at,
        gain_at,
        tiles,
    ) = refs[side:]
    each = tiles.shape[0] // side**2
    for k, piece in enumerate(pieces):
        first = lax.rem(place[3 + place[1]] + side - k, side)
        for j in range(side):
            y, x = block_of(place, first, j)
            d = y * side + x
            tile = piece[j, :, piece.shape[2] - LANES :].astype(f32)
            small_at[d] = tile[:count, :] + tile[count : 2 * count, :]
            at = 2 * count
            gain_at[d] = tile[at : at + gains, :] + tile[at + gains : at + 2 * gains, :]
            at += 2 * gains
            for i in range(each):
                tiles[d * each + i] = tile[at + 8 * i : at + 8 * (i + 1), :]
    fold, across = step_out.shape[1] // channels, channels // LANES
    own, ours = LOCAL // side**2, SHARED // side**2

    def local(row, tile):
        at = row % own * across + tile
        return small_at[row // own, at : at + 1, :]

    def shared(row, tile):
        at = own * across + row % ours * (2 * STATE // LANES) + tile
        return small_at[row // ours, at : at + 1, :]

    for h in range(heads):
        for q in range(fold):
            for t in range(across):
                at = q * channels + t * LANES
                step_out[h : h + 1, at : at + LANES] = local(h * fold + q, t)
    row = heads * fold
    for t in range(across):
        lanes = slice(t * LANES, (t + 1) * LANES)
        for k in range(CONV):
            value_taps_out[k : k + 1, lanes] = local(row + k, t)
        value_bias_out[lanes] = local(row + CONV, t)[0]
        gate_gain_out[lanes] = local(row + CONV + 1, t)[0]
    for t, out in enumerate((step_bias_out, decay_out, skip_out)):
        out[...] = local(row + CONV + 2, t)[:, :heads]

    gain = gain_at[0]
    for d in range(1, side**2):
        gain = gain + gain_at[d]
    rows = [gain[t : t + 1, :] for t in range(gains)]
    rows += [shared(k, t) for k in range(CONV + 1) for t in range(2 * STATE // LANES)]
    pairs = jnp.concatenate(
        [jnp.concatenate(rows[i : i + 2], axis=1) for i in range(0, len(rows), 2)], axis=0
    )
    below = jnp.zeros((SHARED - pairs.shape[0], 2 * STATE), f32)
    share = jnp.concatenate(
        [
            jnp.concatenate([tiles[t], tiles[t + 1]], axis=1)
            for t in range(0, tiles.shape[0], 2)
        ]
        + [jnp.concatenate([part, below], axis=0) for part in high_and_low(pairs)],
        axis=0,
    )
    share_out[...] = share.astype(bf16)


def join_kernel(gains, place, *refs):
    mine, other = refs[:4], refs[4:8]
    state_out, norm_gain_out, taps_out, bias_out = refs[8:]
    tall = state_out.shape[0] // 8
    sums = []
    for k in range(4):
        z = lax.rem(place[0] + 4 - k, 4)
        small = []
        for piece, core in ((mine[k], place[1]), (other[k], 1 - place[1])):
            here = pl.ds(pl.multiple_of((2 * z + core) * tall, tall), tall)
            state_out[here, :] = piece[:tall, :].astype(f32)
            small.append(
                piece[tall : tall + SHARED, :].astype(f32) + piece[tall + SHARED :, :].astype(f32)
            )
        sums.append(small[0] + small[1])
    total = (sums[0] + sums[2]) + (sums[1] + sums[3])
    wide = total.shape[1]
    for t in range(gains * LANES // wide):
        norm_gain_out[t * wide : (t + 1) * wide] = total[t]
    at = gains * LANES // wide
    taps_out[...] = total[at : at + CONV, :]
    bias_out[...] = total[at + CONV]


def output_kernel(inner, total, tokens, stats, out):
    scale, _ = stats_columns(stats[...], inner)
    out[...] = (tokens[...].astype(f32) + scale * total[...].astype(f32)).astype(bf16)


def grad_kernel(total, tokens, cotangent, norm_gain, out):
    x = tokens[...].astype(f32)
    inverse = lax.rsqrt(jnp.mean(x * x, axis=1, keepdims=True) + epsilon)
    scaled = total[...].astype(f32) * row_of(norm_gain)
    moment = jnp.mean(scaled * x, axis=1, keepdims=True)
    grad = inverse * scaled - x * (inverse * inverse * inverse * moment)
    out[...] = (cotangent[...].astype(f32) + grad).astype(bf16)


def whole(array):
    zeros = (0,) * array.ndim
    return pl.BlockSpec(array.shape, lambda i: zeros)


def in_scalars():
    return pl.BlockSpec(memory_space=pltpu.SMEM)


def by_rows(width, steps=None, rows=ROWS):
    if steps is None:
        return pl.BlockSpec((rows, width), lambda i: (i, 0))
    return pl.BlockSpec((rows, width), lambda i: (steps - 1 - i, 0))


def swap_core(x):
    return lax.ppermute(x, "tensor", [(i, i ^ 1) for i in range(8)])


def move_z(x, k):
    return lax.ppermute(x, "tensor", [(i, (i + 2 * k) % 8) for i in range(8)])


def move_dp(x, k, side, stage):
    pairs = []
    for y in range(side):
        for x_at in range(side):
            for t in range(8):
                if (t + stage) % 2 == 0:
                    to = (y + k) % side * side + x_at
                else:
                    to = y * side + (x_at + k) % side
                pairs.append(((y * side + x_at) * 8 + t, to * 8 + t))
    return lax.ppermute(x, ("dp", "tensor"), pairs)


def after(x, *others):
    return lax.optimization_barrier((x,) + others)[0]


free = pl.CostEstimate(flops=0, bytes_accessed=0, transcendentals=0)


def at_place(kernel, place, operands, grid, in_specs, out_specs, out_shape, scratch=()):
    return pl.pallas_call(
        kernel,
        grid_spec=pltpu.PrefetchScalarGridSpec(
            num_scalar_prefetch=1,
            grid=grid,
            in_specs=in_specs,
            out_specs=out_specs,
            scratch_shapes=scratch,
        ),
        out_shape=out_shape,
        compiler_params=pltpu.CompilerParams(
            dimension_semantics=("arbitrary",) * len(grid), vmem_limit_bytes=SMALL_VMEM
        ),
        cost_estimate=free,
    )(place, *operands)


in_vmem = pl.BlockSpec(memory_space=pltpu.VMEM)


def fixed(*shape):
    return pl.BlockSpec(shape, lambda *_: (0,) * len(shape))


def on_device(
    tokens,
    norm_gain,
    in_gate,
    in_value,
    in_state,
    in_step,
    step_bias,
    decay_log,
    skip_gain,
    conv_value_kernel,
    conv_value_bias,
    conv_state_kernel,
    conv_state_bias,
    gate_gain,
    out_weight,
    cotangent,
):
    features = tokens.shape[1]
    channels = in_gate.shape[1]
    heads = step_bias.shape[0]
    inner = channels * lax.axis_size("tensor")
    steps = LEN // ROWS
    parts = ROWS // Q
    dp = lax.axis_size("dp")
    side = math.isqrt(dp)
    me = lax.axis_index("tensor")
    row = lax.axis_index("dp")
    place = jnp.stack([me // 2, me % 2, me, row // side, row % side]).astype(jnp.int32)

    step_weight = in_step.T
    sds = jax.ShapeDtypeStruct
    params = pltpu.CompilerParams(
        dimension_semantics=("arbitrary",), vmem_limit_bytes=VMEM
    )
    stats_rows = pl.BlockSpec((8, ROWS), lambda i: (0, i))
    memory_rows = lambda at: pl.BlockSpec((parts, STATE, channels), lambda i: (at(i), 0, 0))

    (
        normed,
        gate_pre,
        value_pre,
        value_conv,
        state_pre,
        state_conv,
        step_pre,
        mixed,
        back,
        part,
        memories,
        stats,
    ) = pl.pallas_call(
        partial(forward_kernel, heads),
        grid=(steps,),
        in_specs=[
            by_rows(features),
            whole(norm_gain),
            whole(in_gate),
            whole(in_value),
            whole(in_state),
            whole(step_weight),
            in_scalars(),
            in_scalars(),
            in_scalars(),
            whole(conv_value_kernel),
            whole(conv_value_bias),
            whole(conv_state_kernel),
            whole(conv_state_bias),
            whole(gate_gain),
            whole(out_weight),
            by_rows(features),
        ],
        out_specs=[
            by_rows(features),
            by_rows(channels),
            by_rows(channels),
            by_rows(channels),
            by_rows(2 * STATE),
            by_rows(2 * STATE),
            by_rows(LANES),
            by_rows(channels),
            by_rows(channels),
            by_rows(features),
            memory_rows(lambda i: i),
            stats_rows,
        ],
        out_shape=[
            sds((LEN, features), bf16),
            sds((LEN, channels), f32),
            sds((LEN, channels), f32),
            sds((LEN, channels), f32),
            sds((LEN, 2 * STATE), f32),
            sds((LEN, 2 * STATE), f32),
            sds((LEN, LANES), f32),
            sds((LEN, channels), f32),
            sds((LEN, channels), f32),
            sds((LEN, features), bf16),
            sds((LEN // Q, STATE, channels), bf16),
            sds((8, LEN), f32),
        ],
        scratch_shapes=[
            pltpu.VMEM((ROWS + HALO, channels), f32),
            pltpu.VMEM((ROWS + HALO, 2 * STATE), f32),
            pltpu.VMEM((STATE, channels), f32),
        ],
        compiler_params=params,
        cost_estimate=free,
    )(
        tokens,
        norm_gain,
        in_gate,
        in_value,
        in_state,
        step_weight,
        step_bias,
        decay_log,
        skip_gain,
        conv_value_kernel,
        conv_value_bias,
        conv_state_kernel,
        conv_state_bias,
        gate_gain,
        out_weight,
        cotangent,
    )

    out_sum = lax.psum_scatter(part, "tensor", scatter_dimension=0, tiled=True)
    stats = stats + swap_core(stats)
    moved = [move_z(stats, k) for k in (1, 2, 3)]
    stats = (stats + moved[1]) + (moved[0] + moved[2])

    back_rows = partial(by_rows, steps=steps)
    anywhere = pl.BlockSpec(memory_space=pl.ANY)
    lanes = 3 * channels + LANES
    share = features // 8
    tall = features // dp
    part, norm_gain_part, keep, send, *weights = pl.pallas_call(
        partial(backward_kernel, heads, inner, steps, side),
        grid=(steps,),
        in_specs=[
            in_scalars(),
            pl.BlockSpec((8, ROWS), lambda i: (0, steps - 1 - i)),
            back_rows(features),
            back_rows(features),
            back_rows(channels),
            back_rows(channels),
            back_rows(channels),
            back_rows(channels),
            back_rows(channels),
            back_rows(2 * STATE),
            back_rows(2 * STATE),
            back_rows(LANES),
            memory_rows(lambda i: steps - 1 - i),
            whole(gate_gain),
            in_scalars(),
            in_scalars(),
            whole(conv_value_kernel),
            whole(conv_state_kernel),
            whole(norm_gain),
            anywhere,
            anywhere,
            anywhere,
            whole(step_weight),
        ],
        out_specs=[
            back_rows(features),
            fixed(8, features),
            fixed(4, share, 2 * STATE),
            fixed(4, share, 2 * STATE),
        ]
        + [fixed(side, tall, lanes)] * side,
        out_shape=[
            sds((LEN, features), bf16),
            sds((8, features), f32),
            sds((4, share, 2 * STATE), bf16),
            sds((4, share, 2 * STATE), bf16),
        ]
        + [sds((side, tall, lanes), bf16)] * side,
        scratch_shapes=[
            pltpu.VMEM((ROWS + HALO, channels), f32),
            pltpu.VMEM((ROWS + HALO, 2 * STATE), f32),
            pltpu.VMEM((STATE, channels), f32),
            pltpu.VMEM((features, 2 * channels + 2 * STATE), f32),
            pltpu.VMEM((side, channels, features // side), f32),
            pltpu.VMEM((LANES, features), f32),
            pltpu.VMEM((8, channels), f32),
            pltpu.VMEM((8, channels), f32),
            pltpu.VMEM((8, 2 * STATE), f32),
            pltpu.VMEM((8, channels), f32),
            pltpu.VMEM((8, LANES), f32),
            pltpu.VMEM((LOCAL, channels), f32),
            pltpu.VMEM((SHARED, 2 * STATE), f32),
            pltpu.VMEM((dp, tall, LANES), f32),
            pltpu.VMEM((features, 2 * channels + 2 * STATE), bf16),
            pltpu.SemaphoreType.DMA((3,)),
        ],
        compiler_params=params,
        cost_estimate=free,
    )(
        place,
        stats,
        normed,
        cotangent,
        gate_pre,
        mixed,
        back,
        value_pre,
        value_conv,
        state_pre,
        state_conv,
        step_pre,
        memories,
        gate_gain,
        decay_log,
        skip_gain,
        conv_value_kernel,
        conv_state_kernel,
        norm_gain,
        in_gate,
        in_value,
        in_state,
        step_weight,
    )
    out_sum = after(out_sum, part)
    weights[0] = after(weights[0], out_sum)
    weights = [weights[0]] + [
        move_dp(after(weights[k], weights[0]), k, side, 0) for k in range(1, side)
    ]

    grad_sum = lax.psum_scatter(part, "tensor", scatter_dimension=0, tiled=True)

    got = swap_core(send)
    shares = at_place(
        chip_kernel,
        place,
        (keep, got),
        (1,),
        [in_vmem] * 2,
        [fixed(share, 2 * STATE)] * 4,
        [sds((share, 2 * STATE), bf16)] * 4,
    )
    tiles = share * 2 * STATE // (8 * LANES)
    share_tall = -(-tiles * 8 // dp // 16) * 16
    shares = at_place(
        partial(share_kernel, side),
        place,
        [shares[0]] + [move_z(shares[k], k) for k in (1, 2, 3)],
        (1,),
        [in_vmem] * 4,
        [fixed(side, share_tall, LANES)] * side,
        [sds((side, share_tall, LANES), bf16)] * side,
        [pltpu.VMEM((tiles, 8, LANES), f32)],
    )
    shares = [shares[0]] + [move_dp(shares[k], k, side, 0) for k in range(1, side)]

    count = small_rows(dp, channels)
    gains = features // LANES
    plain = 3 * channels
    weights = at_place(
        partial(line_sum_kernel, plain, 2 * (count + gains)),
        place,
        weights + shares,
        (1,),
        [in_vmem] * (2 * side),
        [fixed(tall, lanes)] * side,
        [sds((tall, lanes), bf16)] * side,
    )
    weights = [weights[0]] + [move_dp(weights[k], k, side, 1) for k in range(1, side)]
    grad_sum = lax.all_gather(after(grad_sum, weights[1]), "tensor", tiled=True)


    vmem = pltpu.CompilerParams(vmem_limit_bytes=SMALL_VMEM)
    weights = pl.pallas_call(
        partial(block_sum_kernel, plain, count, gains),
        in_specs=[in_vmem] * (side + 1),
        out_shape=sds((tall, lanes), bf16),
        compiler_params=vmem,
        cost_estimate=free,
    )(*weights, norm_gain_part)
    out_sum = lax.all_gather(after(out_sum, weights), "tensor", tiled=True)
    weights = [weights] + [move_dp(weights, k, side, 1) for k in range(1, side)]
    weights = at_place(
        line_kernel,
        place,
        weights,
        (1,),
        [in_vmem] * side,
        fixed(side, tall, lanes),
        sds((side, tall, lanes), bf16),
    )
    weights = [weights] + [move_dp(weights, k, side, 0) for k in range(1, side)]
    wide = LEN // 2
    wide_rows = by_rows(features, rows=wide)
    grad_tokens = pl.pallas_call(
        grad_kernel,
        grid=(LEN // wide,),
        in_specs=[wide_rows] * 3 + [whole(norm_gain)],
        out_specs=wide_rows,
        out_shape=sds((LEN, features), bf16),
        compiler_params=params,
        cost_estimate=free,
    )(grad_sum, tokens, cotangent, norm_gain)
    block_output = pl.pallas_call(
        partial(output_kernel, inner),
        grid=(LEN // wide,),
        in_specs=[wide_rows, wide_rows, pl.BlockSpec((8, wide), lambda i: (0, i))],
        out_specs=wide_rows,
        out_shape=sds((LEN, features), bf16),
        compiler_params=params,
        cost_estimate=free,
    )(after(out_sum, grad_tokens), tokens, stats)
    weights[0] = after(weights[0], grad_tokens)

    smalls = [
        (heads, features),
        (1, heads),
        (1, heads),
        (1, heads),
        (CONV, channels),
        (channels,),
        (channels,),
    ]
    share_rows = share + 2 * SHARED
    *smalls, state = at_place(
        partial(small_kernel, heads, side, count, gains, channels),
        place,
        weights,
        (1,),
        [in_vmem] * side,
        [fixed(*shape) for shape in smalls] + [fixed(share_rows, 2 * STATE)],
        [sds(shape, f32) for shape in smalls] + [sds((share_rows, 2 * STATE), bf16)],
        [
            pltpu.VMEM((dp, count, LANES), f32),
            pltpu.VMEM((dp, gains, LANES), f32),
            pltpu.VMEM((tiles, 8, LANES), f32),
        ],
    )
    grad_in_step = smalls[0].T
    (
        grad_step_bias,
        grad_decay_log,
        grad_skip_gain,
        grad_conv_value_kernel,
        grad_conv_value_bias,
        grad_gate_gain,
    ) = (a[0] if a.shape[0] == 1 else a for a in smalls[1:])
    state = [state] + [move_z(state, k) for k in (1, 2, 3)]
    across = features // side // channels
    weights[0] = after(weights[0], state[0])
    grad_in_value, grad_in_gate, grad_out_weight = at_place(
        partial(unpack_kernel, side),
        place,
        weights,
        (1,),
        [in_vmem] * side,
        [anywhere] * 3,
        [
            sds((features, channels), f32),
            sds((features, channels), f32),
            sds((channels, features), f32),
        ],
        [
            pltpu.VMEM((dp, 3, tall, channels), f32),
            pltpu.SemaphoreType.DMA((dp * (2 + across),)),
        ],
    )
    state[0] = after(state[0], grad_in_value, block_output)
    grad_in_state, grad_norm_gain, grad_conv_state_kernel, grad_conv_state_bias = at_place(
        partial(join_kernel, gains),
        place,
        state + [swap_core(piece) for piece in state],
        (1,),
        [in_vmem] * 8,
        [
            fixed(features, 2 * STATE),
            fixed(features),
            fixed(CONV, 2 * STATE),
            fixed(2 * STATE),
        ],
        [
            sds((features, 2 * STATE), f32),
            sds((features,), f32),
            sds((CONV, 2 * STATE), f32),
            sds((2 * STATE,), f32),
        ],
    )
    return (
        block_output,
        grad_tokens,
        grad_norm_gain,
        grad_in_gate,
        grad_in_value,
        grad_in_state,
        grad_in_step,
        grad_step_bias,
        grad_decay_log,
        grad_skip_gain,
        grad_conv_value_kernel,
        grad_conv_value_bias,
        grad_conv_state_kernel,
        grad_conv_state_bias,
        grad_gate_gain,
        grad_out_weight,
    )


def solution(mesh):
    placed = (
        P("dp", None),
        P(),
        P(None, "tensor"),
        P(None, "tensor"),
        P(),
        P(None, "tensor"),
        P("tensor"),
        P("tensor"),
        P("tensor"),
        P(None, "tensor"),
        P("tensor"),
        P(),
        P(),
        P("tensor"),
        P("tensor", None),
        P("dp", None),
    )
    return jax.shard_map(
        on_device,
        mesh=mesh,
        in_specs=placed,
        out_specs=(
            P("dp", None),
            P("dp", None),
            P(),
            P(None, "tensor"),
            P(None, "tensor"),
            P(),
            P(None, "tensor"),
            P("tensor"),
            P("tensor"),
            P("tensor"),
            P(None, "tensor"),
            P("tensor"),
            P(),
            P(),
            P("tensor"),
            P("tensor", None),
        ),
        check_vma=False,
    )
```

```python
import math
from functools import partial

import jax
import jax.numpy as jnp
from jax import lax
from jax.experimental import pallas as pl
from jax.experimental.pallas import tpu as pltpu
from jax.sharding import PartitionSpec as P

STATE = 128
CONV = 4
LEN = 1024
HEAD = 64
Q = 128
ROWS = 256
LANES = 128
HALO = 8
LOCAL = 32
SHARED = 16

epsilon = 1e-05
f32 = jnp.float32
bf16 = jnp.bfloat16
VMEM = 60 * 1024 * 1024
SMALL_VMEM = 40 * 1024 * 1024


def mm(a, b):
    return lax.dot_general(a, b, (((1,), (0,)), ((), ())), preferred_element_type=f32)


def parts_of(x):
    high = x.astype(bf16)
    rest = x - high.astype(f32)
    middle = rest.astype(bf16)
    return [high, middle, (rest - middle.astype(f32)).astype(bf16)]


def sum_rows(triangle, x):
    width = x.shape[1]
    total = mm(triangle, jnp.concatenate(parts_of(x), axis=1))
    return total[:, :width] + total[:, width : 2 * width] + total[:, 2 * width :]


def mm_nt(a, b):
    return lax.dot_general(a, b, (((1,), (1,)), ((), ())), preferred_element_type=f32)


def mm_tn(a, b):
    return lax.dot_general(a, b, (((0,), (0,)), ((), ())), preferred_element_type=f32)


def sigmoid(v):
    return 1.0 / (1.0 + jnp.exp(-v))


def softplus(v):
    return jnp.maximum(v, 0.0) + jnp.log1p(jnp.exp(-jnp.abs(v)))


def iota(shape, axis):
    return lax.broadcasted_iota(jnp.int32, shape, axis)


def column(m, at):
    return jnp.broadcast_to(m[:, at : at + 1], (m.shape[0], LANES))


def low_half(rows):
    return iota((rows, LANES), 1) < HEAD


def expand(m, heads):
    half = low_half(m.shape[0])
    return jnp.concatenate(
        [jnp.where(half, column(m, h), column(m, h + 1)) for h in range(0, heads, 2)], axis=1
    )


def split_heads(pair):
    half = low_half(pair.shape[0])
    zero = jnp.zeros_like(pair)
    return jnp.concatenate([jnp.where(half, pair, zero), jnp.where(half, zero, pair)], axis=0)


def head_sum(m, channels_to_heads):
    high = m.astype(bf16)
    low = (m - high.astype(f32)).astype(bf16)
    return mm(high, channels_to_heads) + mm(low, channels_to_heads)


def head_row(scalars, heads):
    lane = iota((1, LANES), 1)
    row = jnp.zeros((1, LANES), f32)
    for h in range(heads):
        row = jnp.where(lane == h, scalars[h], row)
    return row


def rate_row(decay_log, heads):
    return jnp.where(iota((1, LANES), 1) < heads, -jnp.exp(head_row(decay_log, heads)), 0.0)


def channel_row(scalars, heads):
    half = low_half(1)
    return jnp.concatenate(
        [jnp.where(half, scalars[h], scalars[h + 1]) for h in range(0, heads, 2)], axis=1
    )


def all_lanes(rows):
    below = jnp.zeros((LANES - rows.shape[0], rows.shape[1]), rows.dtype)
    return jnp.concatenate([rows, below], axis=0)


def row_of(ref):
    return ref[...].reshape(1, ref.shape[0])


def forward_kernel(
    heads,
    tokens,
    norm_gain,
    in_gate,
    in_value,
    in_state,
    in_step,
    step_bias,
    decay_log,
    skip_gain,
    value_kernel,
    value_bias,
    state_kernel,
    state_bias,
    gate_gain,
    out_weight,
    cotangent,
    normed_out,
    gate_out,
    value_out,
    value_conv_out,
    state_out,
    state_conv_out,
    step_out,
    mixed_out,
    back_out,
    part_out,
    memory_out,
    stats_out,
    value_buf,
    state_buf,
    memory,
):
    @pl.when(pl.program_id(0) == 0)
    def _():
        value_buf[0:HALO, :] = jnp.zeros((HALO, value_buf.shape[1]), f32)
        state_buf[0:HALO, :] = jnp.zeros((HALO, state_buf.shape[1]), f32)
        memory[...] = jnp.zeros_like(memory)

    x = tokens[...].astype(f32)
    inverse = lax.rsqrt(jnp.mean(x * x, axis=1, keepdims=True) + epsilon)
    normed = (x * inverse * row_of(norm_gain)).astype(bf16)
    normed_out[...] = normed
    state_pre = mm(normed, in_state[...])
    value_pre = mm(normed, in_value[...])
    step_pre = mm_nt(normed, all_lanes(in_step[...])) + head_row(step_bias, heads)
    gate_pre = mm(normed, in_gate[...])
    gate_out[...] = gate_pre
    value_out[...] = value_pre
    state_out[...] = state_pre
    step_out[...] = step_pre

    def conv(buf, pre, kernel, bias):
        buf[HALO:, :] = pre
        result = row_of(bias) + buf[HALO - 3 : HALO - 3 + ROWS, :] * kernel[0:1, :]
        for k in range(1, CONV):
            result = result + buf[HALO - 3 + k : HALO - 3 + k + ROWS, :] * kernel[k : k + 1, :]
        buf[0:HALO, :] = buf[ROWS : ROWS + HALO, :]
        return result

    value_conv = conv(value_buf, value_pre, value_kernel, value_bias)
    value_conv_out[...] = value_conv
    values = (value_conv * sigmoid(value_conv)).astype(bf16)
    state_conv = conv(state_buf, state_pre, state_kernel, state_bias)
    state_conv_out[...] = state_conv
    states = (state_conv * sigmoid(state_conv)).astype(bf16)
    step = softplus(step_pre)
    log_step = step * rate_row(decay_log, heads)
    skip = channel_row(skip_gain, heads)

    causal = iota((Q, Q), 0) >= iota((Q, Q), 1)
    tri = jnp.where(causal, 1.0, 0.0).astype(bf16)
    mixed_parts = []
    for part in range(ROWS // Q):
        rows = slice(part * Q, (part + 1) * Q)
        b = states[rows, :STATE]
        c = states[rows, STATE:]
        v = values[rows, :].astype(f32)
        dt = step[rows, :]
        decay = sum_rows(tri, log_step[rows, :])
        decay_t = decay.T
        wide = expand(decay, heads)
        dt_wide = expand(dt, heads)
        grown = jnp.exp(wide)
        scaled = v * dt_wide
        scaled_low = scaled.astype(bf16)
        cb = mm_nt(c, b)
        held = memory[...]
        held_low = held.astype(bf16)
        memory_out[part] = held_low
        y = mm(c, held_low) * grown + skip * v
        inside = []
        for h in range(0, heads, 2):
            blocks = []
            for at in (h, h + 1):
                gap = column(decay, at) - decay_t[at : at + 1, :]
                blocks.append((cb * jnp.exp(jnp.where(causal, gap, -1e30))).astype(bf16))
            pair = scaled_low[:, h * HEAD : (h + 2) * HEAD]
            inside.append(mm(jnp.concatenate(blocks, axis=1), split_heads(pair)))
        mixed_parts.append(y + jnp.concatenate(inside, axis=1))
        ended = (scaled * jnp.exp(wide[Q - 1 : Q, :] - wide)).astype(bf16)
        memory[...] = held * grown[Q - 1 : Q, :] + mm_tn(b, ended)

    mixed = jnp.concatenate(mixed_parts, axis=0)
    mixed_out[...] = mixed
    gated = mixed * gate_pre * sigmoid(gate_pre)
    back = mm_nt(cotangent[...], out_weight[...])
    back_out[...] = back
    gained = gated * row_of(gate_gain)
    part_out[...] = mm(gained.astype(bf16), out_weight[...]).astype(bf16)
    squares = jnp.sum(gated * gated, axis=1, keepdims=True)
    moment = jnp.sum(back * gained, axis=1, keepdims=True)
    lane = iota((ROWS, LANES), 1)
    both = jnp.where(lane == 0, squares, jnp.where(lane == 1, moment, 0.0))
    stats_out[...] = both.T[0:8, :]


def stats_columns(stats, inner):
    padded = jnp.concatenate([stats, jnp.zeros((LANES - 8, stats.shape[1]), f32)], axis=0).T
    scale = lax.rsqrt(padded[:, 0:1] / inner + epsilon)
    return scale, padded[:, 1:2] / inner


def add_row(ref, at, rows):
    ref[at : at + 1, :] += jnp.sum(rows, axis=0, keepdims=True)


def backward_kernel(
    heads,
    inner,
    steps,
    side,
    place,
    stats,
    normed,
    cotangent,
    gate,
    mixed_in,
    back_in,
    value,
    value_conv,
    state,
    state_conv,
    step_in,
    memory_in,
    gate_gain,
    decay_log,
    skip_gain,
    value_kernel,
    state_kernel,
    norm_gain,
    in_gate_at,
    in_value_at,
    in_state_at,
    in_step,
    part_out,
    norm_gain_out,
    keep_out,
    send_out,
    *refs,
):
    pieces_out = refs[:side]
    (
        value_buf,
        state_buf,
        adjoint,
        weight_total,
        out_total,
        step_total,
        gate_gain_out,
        value_taps_out,
        state_taps_out,
        skip_out,
        steps_out,
        local_rows,
        shared_rows,
        slabs,
        in_all,
        sems,
    ) = refs[side:]
    wide = in_gate_at.shape[1]
    weights = [
        pltpu.make_async_copy(source, target, sems.at[i])
        for i, (source, target) in enumerate(
            (
                (in_value_at, in_all.at[:, pl.ds(0, wide)]),
                (in_gate_at, in_all.at[:, pl.ds(wide, wide)]),
                (in_state_at, in_all.at[:, pl.ds(2 * wide, 2 * STATE)]),
            )
        )
    ]

    @pl.when(pl.program_id(0) == 0)
    def _():
        for copy in weights:
            copy.start()
        norm_gain_out[...] = jnp.zeros_like(norm_gain_out)
        value_buf[ROWS:, :] = jnp.zeros((HALO, value_buf.shape[1]), f32)
        state_buf[ROWS:, :] = jnp.zeros((HALO, state_buf.shape[1]), f32)
        adjoint[...] = jnp.zeros_like(adjoint)
        for ref in (
            weight_total,
            out_total,
            step_total,
            gate_gain_out,
            value_taps_out,
            state_taps_out,
            skip_out,
            steps_out,
        ):
            ref[...] = jnp.zeros_like(ref)

    scale, moment = stats_columns(stats[...], inner)
    mixed = mixed_in[...]
    back = back_in[...]
    pre = gate[...]
    bent = sigmoid(pre)
    silu = pre * bent
    gated = mixed * silu
    scaled = gated * scale
    gain = row_of(gate_gain)
    add_row(gate_gain_out, 0, back * scaled)
    grad_gated = scale * (back * gain) - scaled * (scale * scale * moment)
    grad_mixed = grad_gated * silu
    round_gate = (grad_gated * mixed * (bent * (1.0 + pre * (1.0 - bent)))).astype(bf16)
    outgoing = (scaled * gain).astype(bf16)
    width = out_total.shape[2]
    out_terms = mm_tn(outgoing, cotangent[...])
    for x in range(side):
        out_total[x] += out_terms[:, x * width : (x + 1) * width]

    value_at = value_conv[...]
    value_bent = sigmoid(value_at)
    values = (value_at * value_bent).astype(bf16)
    state_at = state_conv[...]
    state_bent = sigmoid(state_at)
    states = (state_at * state_bent).astype(bf16)
    step_pre = step_in[...]
    step = softplus(step_pre)
    rate = rate_row(decay_log, heads)
    skip = channel_row(skip_gain, heads)
    log_step = step * rate

    ahead = iota((Q, Q), 1) >= iota((Q, Q), 0)
    tri = jnp.where(iota((Q, Q), 0) >= iota((Q, Q), 1), 1.0, 0.0).astype(bf16)
    tri_both = jnp.concatenate(
        [
            jnp.where(ahead, 1.0, 0.0),
            jnp.where(iota((Q, Q), 0) > iota((Q, Q), 1), 1.0, 0.0),
        ],
        axis=1,
    ).astype(bf16)
    lane = iota((Q, LANES), 1)
    row8 = iota((8, Q), 0)
    channels = heads * HEAD
    to_heads = jnp.where(
        lax.shift_right_logical(iota((channels, LANES), 0), 6) == iota((channels, LANES), 1), 1.0, 0.0
    ).astype(bf16)
    parts = ROWS // Q
    grad_value_parts = [None] * parts
    grad_state_parts = [None] * parts
    grad_step_parts = [None] * parts
    for part in reversed(range(parts)):
        rows = slice(part * Q, (part + 1) * Q)
        b = states[rows, :STATE]
        c = states[rows, STATE:]
        v_low = values[rows, :]
        v = v_low.astype(f32)
        dt = step[rows, :]
        dy = grad_mixed[rows, :]
        dy_low = dy.astype(bf16)
        decay = sum_rows(tri, log_step[rows, :])
        decay_t = decay.T
        wide = expand(decay, heads)
        dt_wide = expand(dt, heads)
        grown = jnp.exp(wide)
        to_end = jnp.exp(wide[Q - 1 : Q, :] - wide)
        held = memory_in[part]
        later = adjoint[...]
        later_low = later.astype(bf16)
        bd = mm(b, later_low)
        cs = mm(c, held)
        bc = mm_nt(b, c)
        dy_grown = dy * grown
        dy_grown_low = dy_grown.astype(bf16)
        at_end = bd * to_end
        inside = []
        grad_bc = jnp.zeros((Q, Q), f32)
        direct = jnp.zeros((Q, LANES), f32)
        row_sums = jnp.zeros((8, Q), f32)
        for h in range(0, heads, 2):
            lanes = slice(h * HEAD, (h + 2) * HEAD)
            v_split = split_heads(v_low[:, lanes])
            grad_pair = mm_nt(v_split, dy_low[:, lanes])
            blocks = []
            for at in (h, h + 1):
                gap = decay_t[at : at + 1, :] - column(decay, at)
                fall = jnp.exp(jnp.where(ahead, gap, -1e30))
                grad_fall = grad_pair[(at - h) * Q : (at - h + 1) * Q, :] * fall
                direct += jnp.where(lane == at, jnp.sum(grad_fall * bc, axis=1, keepdims=True), 0.0)
                grad_one = grad_fall * column(dt, at)
                grad_bc += grad_one
                row_sums += jnp.where(
                    row8 == at, jnp.sum(grad_one * bc, axis=0, keepdims=True), 0.0
                )
                blocks.append((bc * fall).astype(bf16))
            inside.append(mm(jnp.concatenate(blocks, axis=1), split_heads(dy_low[:, lanes])))
        grad_value_parts[part] = dt_wide * (jnp.concatenate(inside, axis=1) + at_end) + skip * dy
        add_row(skip_out, 0, dy * v)
        grown_sum = head_sum(dy_grown * cs, to_heads)
        end_sum = head_sum(at_end * v, to_heads)
        constant = head_sum(
            grown[Q - 1 : Q, :] * jnp.sum(held.astype(f32) * later, axis=0, keepdims=True), to_heads
        )
        row_t = jnp.concatenate([row_sums, jnp.zeros((LANES - 8, Q), f32)], axis=0).T
        grad_log = (
            sum_rows(
                tri_both,
                jnp.concatenate([row_t - direct * dt + grown_sum, end_sum * dt], axis=0),
            )
            + constant
        )
        grad_step = direct + end_sum + rate * grad_log
        grad_step = grad_step * sigmoid(step_pre[rows, :])
        grad_step_parts[part] = grad_step
        add_row(steps_out, 0, grad_step)
        add_row(steps_out, 1, dt * grad_log * rate)
        grad_bc_low = grad_bc.astype(bf16)
        grad_b = mm(grad_bc_low, c) + mm_nt((v * dt_wide * to_end).astype(bf16), later_low)
        grad_c = mm_tn(grad_bc_low, b) + mm_nt(dy_grown_low, held)
        grad_state_parts[part] = jnp.concatenate([grad_b, grad_c], axis=1)
        adjoint[...] = later * grown[Q - 1 : Q, :] + mm_tn(c, dy_grown_low)

    def conv_back(buf, grad, at, bent, pre, kernel, taps_out):
        buf[0:ROWS, :] = grad * (bent * (1.0 + at * (1.0 - bent)))
        result = None
        for k in range(CONV):
            moved = buf[3 - k : 3 - k + ROWS, :]
            term = moved * kernel[k : k + 1, :]
            result = term if result is None else result + term
            add_row(taps_out, k, pre * moved)
        add_row(taps_out, CONV, buf[0:ROWS, :])
        buf[ROWS:, :] = buf[0:HALO, :]
        return result.astype(bf16)

    round_value = conv_back(
        value_buf,
        jnp.concatenate(grad_value_parts, axis=0),
        value_at,
        value_bent,
        value[...],
        value_kernel,
        value_taps_out,
    )
    round_state = conv_back(
        state_buf,
        jnp.concatenate(grad_state_parts, axis=0),
        state_at,
        state_bent,
        state[...],
        state_kernel,
        state_taps_out,
    )
    round_step = jnp.concatenate(grad_step_parts, axis=0).astype(bf16)

    @pl.when(pl.program_id(0) == 0)
    def _():
        for copy in weights:
            copy.wait()

    rounds = jnp.concatenate([round_value, round_gate, round_state], axis=1)
    total = mm_nt(rounds, in_all[...]) + mm(round_step, all_lanes(in_step[...]))
    part_out[...] = total.astype(bf16)
    add_row(norm_gain_out, 0, total * normed[...].astype(f32))
    weight_total[...] += mm_tn(normed[...], rounds)
    step_total[...] += mm_tn(round_step, normed[...])

    @pl.when(pl.program_id(0) == steps - 1)
    def _():
        norm_gain_out[...] = norm_gain_out[...] / row_of(norm_gain)
        fold = step_total.shape[1] // channels
        local_rows[...] = jnp.zeros_like(local_rows)
        for h in range(heads):
            for q in range(fold):
                local_rows[h * fold + q : h * fold + q + 1, :] = step_total[
                    h : h + 1, q * channels : (q + 1) * channels
                ]
        at = heads * fold
        local_rows[at : at + CONV + 1, :] = value_taps_out[0 : CONV + 1, :]
        at += CONV + 1
        local_rows[at : at + 1, :] = gate_gain_out[0:1, :]
        local_rows[at + 1 : at + 2, :] = jnp.concatenate(
            [steps_out[0:1, :], steps_out[1:2, :], head_sum(skip_out[...], to_heads)[0:1, :]],
            axis=1,
        )
        shared_rows[...] = jnp.zeros_like(shared_rows)
        shared_rows[0 : CONV + 1, :] = state_taps_out[0 : CONV + 1, :]

        _, tall, _ = pieces_out[0].shape
        count = small_rows(side**2, channels)
        slabs[...] = jnp.zeros_like(slabs)
        for d in range(side**2):
            at = 0
            for ref in (local_rows, shared_rows):
                each = ref.shape[0] // side**2
                for j in range(d * each, (d + 1) * each):
                    for lanes in range(0, ref.shape[1], LANES):
                        mine = ref[j : j + 1, lanes : lanes + LANES]
                        high = mine.astype(bf16).astype(f32)
                        slabs[d, at : at + 1, :] = high
                        slabs[d, count + at : count + at + 1, :] = mine - high
                        at += 1
        rows = channels // side
        for k, piece in enumerate(pieces_out):
            for j in range(side):
                y, x = block_of(place, lax.rem(place[3 + place[1]] + k, side), j)
                here = pl.ds(pl.multiple_of((y * side + x) * tall, tall), tall)
                piece[j, :, 0 : 2 * channels] = weight_total[here, 0 : 2 * channels].astype(bf16)
                for c in range(width // channels):
                    piece[j, c * rows : (c + 1) * rows, 2 * channels : 3 * channels] = out_total[
                        x,
                        pl.ds(pl.multiple_of(y * rows, rows), rows),
                        c * channels : (c + 1) * channels,
                    ].astype(bf16)
                piece[j, :, 3 * channels :] = slabs[y * side + x].astype(bf16)

        upper = place[1] == 0
        tall = keep_out.shape[1]
        for z in range(4):
            even = weight_total[2 * z * tall : (2 * z + 1) * tall, 2 * channels :].astype(bf16)
            odd = weight_total[(2 * z + 1) * tall : (2 * z + 2) * tall, 2 * channels :].astype(
                bf16
            )
            keep_out[z] = jnp.where(upper, even, odd)
            send_out[z] = jnp.where(upper, odd, even)


def block_of(place, first, second):
    core = place[1]
    return first + core * (second - first), second + core * (first - second)


def small_rows(pieces, channels):
    return (LOCAL * channels + SHARED * 2 * STATE) // LANES // pieces


def line_kernel(place, *refs):
    *pieces, out = refs
    side = len(pieces)
    for k, piece in enumerate(pieces):
        out[lax.rem(place[4 - place[1]] + side - k, side)] = piece[...]


def chip_kernel(place, keep, got, *outs):
    for k, out in enumerate(outs):
        z = lax.rem(place[0] + k, 4)
        out[...] = (keep[z].astype(f32) + got[z].astype(f32)).astype(bf16)


def tile_at(t):
    rows, lanes = 8 * (t // 2), LANES * (t % 2)
    return slice(rows, rows + 8), slice(lanes, lanes + LANES)


def share_kernel(side, place, own, one, two, three, *refs):
    outs, tiles = refs[:-1], refs[-1]
    total = total_of((own, one, two, three))
    count = tiles.shape[0]
    for t in range(count):
        tiles[t] = total[tile_at(t)]
    each = count // side**2
    for k, out in enumerate(outs):
        for j in range(side):
            y, x = block_of(place, lax.rem(place[3 + place[1]] + k, side), j)
            slab = [tiles[(y * side + x) * each + i] for i in range(each)]
            below = out.shape[1] - 8 * each
            out[j] = jnp.concatenate(slab + [jnp.zeros((below, LANES), f32)], axis=0).astype(bf16)


def total_of(pieces):
    total = pieces[0][...].astype(f32)
    for piece in pieces[1:]:
        total = total + piece[...].astype(f32)
    return total


def line_sum_kernel(plain, at, place, *refs):
    side = len(refs) // 3
    pieces, shares, outs = refs[:side], refs[side : 2 * side], refs[2 * side :]
    tall = shares[0].shape[1]
    for k, out in enumerate(outs):
        j = lax.rem(place[4 - place[1]] + k, side)
        total = total_of([ref.at[j] for ref in pieces])
        share = total_of([ref.at[j] for ref in shares])
        out[:, :plain] = total[:, :plain].astype(bf16)
        out[:, plain:] = jnp.concatenate(
            [total[:at, plain:], share, total[at + tall :, plain:]], axis=0
        ).astype(bf16)


def block_sum_kernel(plain, count, gains, *refs):
    *pieces, norm_gain, out = refs
    total = total_of(pieces)
    out[:, :plain] = total[:, :plain].astype(bf16)
    small = total[:count, plain:] + total[count : 2 * count, plain:]
    gain = jnp.concatenate(
        [norm_gain[0:1, j * LANES : (j + 1) * LANES] for j in range(gains)], axis=0
    )
    at = 2 * (count + gains)
    out[:, plain:] = jnp.concatenate(
        high_and_low(small) + high_and_low(gain) + [total[at:, plain:]], axis=0
    ).astype(bf16)


def high_and_low(rows):
    high = rows.astype(bf16).astype(f32)
    return [high, rows - high]


def unpack_kernel(side, steps_back, place, *refs):
    pieces = refs[: len(steps_back)]
    value_out, gate_out, out_out, wide, sems = refs[-5:]
    _, _, tall, channels = wide.shape
    rows, width = out_out.shape[0] // side, out_out.shape[1] // side
    copies = []

    def send(source, target):
        copies.append(pltpu.make_async_copy(source, target, sems.at[len(copies)]))
        copies[-1].start()

    for k, piece in enumerate(pieces):
        first = lax.rem(place[3 + place[1]] + side - steps_back[k], side)
        for j in range(side):
            y, x = block_of(place, first, j)
            at = k * side + j
            here = pl.ds(pl.multiple_of((y * side + x) * tall, tall), tall)
            for c in range(3):
                wide[at, c] = piece[j, :, c * channels : (c + 1) * channels].astype(f32)
            send(wide.at[at, 0], value_out.at[here])
            send(wide.at[at, 1], gate_out.at[here])
            for c in range(width // channels):
                send(
                    wide.at[at, 2, pl.ds(c * rows, rows)],
                    out_out.at[
                        pl.ds(pl.multiple_of(y * rows, rows), rows),
                        pl.ds(pl.multiple_of(x * width + c * channels, channels), channels),
                    ],
                )
    for copy in copies:
        copy.wait()


def small_kernel(heads, side, count, gains, channels, place, *refs):
    pieces = refs[:side]
    (
        step_out,
        step_bias_out,
        decay_out,
        skip_out,
        value_taps_out,
        value_bias_out,
        gate_gain_out,
        share_out,
        small_at,
        gain_at,
        tiles,
    ) = refs[side:]
    each = tiles.shape[0] // side**2
    for k, piece in enumerate(pieces):
        first = lax.rem(place[3 + place[1]] + side - k, side)
        for j in range(side):
            y, x = block_of(place, first, j)
            d = y * side + x
            tile = piece[j, :, piece.shape[2] - LANES :].astype(f32)
            small_at[d] = tile[:count, :] + tile[count : 2 * count, :]
            at = 2 * count
            gain_at[d] = tile[at : at + gains, :] + tile[at + gains : at + 2 * gains, :]
            at += 2 * gains
            for i in range(each):
                tiles[d * each + i] = tile[at + 8 * i : at + 8 * (i + 1), :]
    fold, across = step_out.shape[1] // channels, channels // LANES
    own, ours = LOCAL // side**2, SHARED // side**2

    def local(row, tile):
        at = row % own * across + tile
        return small_at[row // own, at : at + 1, :]

    def shared(row, tile):
        at = own * across + row % ours * (2 * STATE // LANES) + tile
        return small_at[row // ours, at : at + 1, :]

    for h in range(heads):
        for q in range(fold):
            for t in range(across):
                at = q * channels + t * LANES
                step_out[h : h + 1, at : at + LANES] = local(h * fold + q, t)
    row = heads * fold
    for t in range(across):
        lanes = slice(t * LANES, (t + 1) * LANES)
        for k in range(CONV):
            value_taps_out[k : k + 1, lanes] = local(row + k, t)
        value_bias_out[lanes] = local(row + CONV, t)[0]
        gate_gain_out[lanes] = local(row + CONV + 1, t)[0]
    for t, out in enumerate((step_bias_out, decay_out, skip_out)):
        out[...] = local(row + CONV + 2, t)[:, :heads]

    gain = gain_at[0]
    for d in range(1, side**2):
        gain = gain + gain_at[d]
    rows = [gain[t : t + 1, :] for t in range(gains)]
    rows += [shared(k, t) for k in range(CONV + 1) for t in range(2 * STATE // LANES)]
    pairs = jnp.concatenate(
        [jnp.concatenate(rows[i : i + 2], axis=1) for i in range(0, len(rows), 2)], axis=0
    )
    below = jnp.zeros((SHARED - pairs.shape[0], 2 * STATE), f32)
    share = jnp.concatenate(
        [
            jnp.concatenate([tiles[t], tiles[t + 1]], axis=1)
            for t in range(0, tiles.shape[0], 2)
        ]
        + [jnp.concatenate([part, below], axis=0) for part in high_and_low(pairs)],
        axis=0,
    )
    share_out[...] = share.astype(bf16)


def join_kernel(gains, place, *refs):
    mine, other = refs[:4], refs[4:8]
    state_out, norm_gain_out, taps_out, bias_out = refs[8:]
    tall = state_out.shape[0] // 8
    sums = []
    for k in range(4):
        z = lax.rem(place[0] + 4 - k, 4)
        small = []
        for piece, core in ((mine[k], place[1]), (other[k], 1 - place[1])):
            here = pl.ds(pl.multiple_of((2 * z + core) * tall, tall), tall)
            state_out[here, :] = piece[:tall, :].astype(f32)
            small.append(
                piece[tall : tall + SHARED, :].astype(f32) + piece[tall + SHARED :, :].astype(f32)
            )
        sums.append(small[0] + small[1])
    total = (sums[0] + sums[2]) + (sums[1] + sums[3])
    wide = total.shape[1]
    for t in range(gains * LANES // wide):
        norm_gain_out[t * wide : (t + 1) * wide] = total[t]
    at = gains * LANES // wide
    taps_out[...] = total[at : at + CONV, :]
    bias_out[...] = total[at + CONV]


def output_kernel(inner, total, tokens, stats, out):
    scale, _ = stats_columns(stats[...], inner)
    out[...] = (tokens[...].astype(f32) + scale * total[...].astype(f32)).astype(bf16)


def grad_kernel(total, tokens, cotangent, norm_gain, out):
    x = tokens[...].astype(f32)
    inverse = lax.rsqrt(jnp.mean(x * x, axis=1, keepdims=True) + epsilon)
    scaled = total[...].astype(f32) * row_of(norm_gain)
    moment = jnp.mean(scaled * x, axis=1, keepdims=True)
    grad = inverse * scaled - x * (inverse * inverse * inverse * moment)
    out[...] = (cotangent[...].astype(f32) + grad).astype(bf16)


def whole(array):
    zeros = (0,) * array.ndim
    return pl.BlockSpec(array.shape, lambda i: zeros)


def in_scalars():
    return pl.BlockSpec(memory_space=pltpu.SMEM)


def by_rows(width, steps=None, rows=ROWS):
    if steps is None:
        return pl.BlockSpec((rows, width), lambda i: (i, 0))
    return pl.BlockSpec((rows, width), lambda i: (steps - 1 - i, 0))


def swap_core(x):
    return lax.ppermute(x, "tensor", [(i, i ^ 1) for i in range(8)])


def move_z(x, k):
    return lax.ppermute(x, "tensor", [(i, (i + 2 * k) % 8) for i in range(8)])


def move_dp(x, k, side, stage):
    pairs = []
    for y in range(side):
        for x_at in range(side):
            for t in range(8):
                if (t + stage) % 2 == 0:
                    to = (y + k) % side * side + x_at
                else:
                    to = y * side + (x_at + k) % side
                pairs.append(((y * side + x_at) * 8 + t, to * 8 + t))
    return lax.ppermute(x, ("dp", "tensor"), pairs)


def after(x, *others):
    return lax.optimization_barrier((x,) + others)[0]


free = pl.CostEstimate(flops=0, bytes_accessed=0, transcendentals=0)


def at_place(
    kernel, place, operands, grid, in_specs, out_specs, out_shape, scratch=(), aliases=None
):
    return pl.pallas_call(
        kernel,
        grid_spec=pltpu.PrefetchScalarGridSpec(
            num_scalar_prefetch=1,
            grid=grid,
            in_specs=in_specs,
            out_specs=out_specs,
            scratch_shapes=scratch,
        ),
        out_shape=out_shape,
        compiler_params=pltpu.CompilerParams(
            dimension_semantics=("arbitrary",) * len(grid), vmem_limit_bytes=SMALL_VMEM
        ),
        input_output_aliases=aliases or {},
        cost_estimate=free,
    )(place, *operands)


in_vmem = pl.BlockSpec(memory_space=pltpu.VMEM)


def fixed(*shape):
    return pl.BlockSpec(shape, lambda *_: (0,) * len(shape))


def on_device(
    tokens,
    norm_gain,
    in_gate,
    in_value,
    in_state,
    in_step,
    step_bias,
    decay_log,
    skip_gain,
    conv_value_kernel,
    conv_value_bias,
    conv_state_kernel,
    conv_state_bias,
    gate_gain,
    out_weight,
    cotangent,
):
    features = tokens.shape[1]
    channels = in_gate.shape[1]
    heads = step_bias.shape[0]
    inner = channels * lax.axis_size("tensor")
    steps = LEN // ROWS
    parts = ROWS // Q
    dp = lax.axis_size("dp")
    side = math.isqrt(dp)
    me = lax.axis_index("tensor")
    row = lax.axis_index("dp")
    place = jnp.stack([me // 2, me % 2, me, row // side, row % side]).astype(jnp.int32)

    step_weight = in_step.T
    sds = jax.ShapeDtypeStruct
    params = pltpu.CompilerParams(
        dimension_semantics=("arbitrary",), vmem_limit_bytes=VMEM
    )
    stats_rows = pl.BlockSpec((8, ROWS), lambda i: (0, i))
    memory_rows = lambda at: pl.BlockSpec((parts, STATE, channels), lambda i: (at(i), 0, 0))

    (
        normed,
        gate_pre,
        value_pre,
        value_conv,
        state_pre,
        state_conv,
        step_pre,
        mixed,
        back,
        part,
        memories,
        stats,
    ) = pl.pallas_call(
        partial(forward_kernel, heads),
        grid=(steps,),
        in_specs=[
            by_rows(features),
            whole(norm_gain),
            whole(in_gate),
            whole(in_value),
            whole(in_state),
            whole(step_weight),
            in_scalars(),
            in_scalars(),
            in_scalars(),
            whole(conv_value_kernel),
            whole(conv_value_bias),
            whole(conv_state_kernel),
            whole(conv_state_bias),
            whole(gate_gain),
            whole(out_weight),
            by_rows(features),
        ],
        out_specs=[
            by_rows(features),
            by_rows(channels),
            by_rows(channels),
            by_rows(channels),
            by_rows(2 * STATE),
            by_rows(2 * STATE),
            by_rows(LANES),
            by_rows(channels),
            by_rows(channels),
            by_rows(features),
            memory_rows(lambda i: i),
            stats_rows,
        ],
        out_shape=[
            sds((LEN, features), bf16),
            sds((LEN, channels), f32),
            sds((LEN, channels), f32),
            sds((LEN, channels), f32),
            sds((LEN, 2 * STATE), f32),
            sds((LEN, 2 * STATE), f32),
            sds((LEN, LANES), f32),
            sds((LEN, channels), f32),
            sds((LEN, channels), f32),
            sds((LEN, features), bf16),
            sds((LEN // Q, STATE, channels), bf16),
            sds((8, LEN), f32),
        ],
        scratch_shapes=[
            pltpu.VMEM((ROWS + HALO, channels), f32),
            pltpu.VMEM((ROWS + HALO, 2 * STATE), f32),
            pltpu.VMEM((STATE, channels), f32),
        ],
        compiler_params=params,
        cost_estimate=free,
    )(
        tokens,
        norm_gain,
        in_gate,
        in_value,
        in_state,
        step_weight,
        step_bias,
        decay_log,
        skip_gain,
        conv_value_kernel,
        conv_value_bias,
        conv_state_kernel,
        conv_state_bias,
        gate_gain,
        out_weight,
        cotangent,
    )

    out_sum = lax.psum_scatter(part, "tensor", scatter_dimension=0, tiled=True)
    stats = stats + swap_core(stats)
    moved = [move_z(stats, k) for k in (1, 2, 3)]
    stats = (stats + moved[1]) + (moved[0] + moved[2])

    back_rows = partial(by_rows, steps=steps)
    anywhere = pl.BlockSpec(memory_space=pl.ANY)
    lanes = 3 * channels + LANES
    share = features // 8
    tall = features // dp
    part, norm_gain_part, keep, send, *weights = pl.pallas_call(
        partial(backward_kernel, heads, inner, steps, side),
        grid=(steps,),
        in_specs=[
            in_scalars(),
            pl.BlockSpec((8, ROWS), lambda i: (0, steps - 1 - i)),
            back_rows(features),
            back_rows(features),
            back_rows(channels),
            back_rows(channels),
            back_rows(channels),
            back_rows(channels),
            back_rows(channels),
            back_rows(2 * STATE),
            back_rows(2 * STATE),
            back_rows(LANES),
            memory_rows(lambda i: steps - 1 - i),
            whole(gate_gain),
            in_scalars(),
            in_scalars(),
            whole(conv_value_kernel),
            whole(conv_state_kernel),
            whole(norm_gain),
            anywhere,
            anywhere,
            anywhere,
            whole(step_weight),
        ],
        out_specs=[
            back_rows(features),
            fixed(8, features),
            fixed(4, share, 2 * STATE),
            fixed(4, share, 2 * STATE),
        ]
        + [fixed(side, tall, lanes)] * side,
        out_shape=[
            sds((LEN, features), bf16),
            sds((8, features), f32),
            sds((4, share, 2 * STATE), bf16),
            sds((4, share, 2 * STATE), bf16),
        ]
        + [sds((side, tall, lanes), bf16)] * side,
        scratch_shapes=[
            pltpu.VMEM((ROWS + HALO, channels), f32),
            pltpu.VMEM((ROWS + HALO, 2 * STATE), f32),
            pltpu.VMEM((STATE, channels), f32),
            pltpu.VMEM((features, 2 * channels + 2 * STATE), f32),
            pltpu.VMEM((side, channels, features // side), f32),
            pltpu.VMEM((LANES, features), f32),
            pltpu.VMEM((8, channels), f32),
            pltpu.VMEM((8, channels), f32),
            pltpu.VMEM((8, 2 * STATE), f32),
            pltpu.VMEM((8, channels), f32),
            pltpu.VMEM((8, LANES), f32),
            pltpu.VMEM((LOCAL, channels), f32),
            pltpu.VMEM((SHARED, 2 * STATE), f32),
            pltpu.VMEM((dp, tall, LANES), f32),
            pltpu.VMEM((features, 2 * channels + 2 * STATE), bf16),
            pltpu.SemaphoreType.DMA((3,)),
        ],
        compiler_params=params,
        cost_estimate=free,
    )(
        place,
        stats,
        normed,
        cotangent,
        gate_pre,
        mixed,
        back,
        value_pre,
        value_conv,
        state_pre,
        state_conv,
        step_pre,
        memories,
        gate_gain,
        decay_log,
        skip_gain,
        conv_value_kernel,
        conv_state_kernel,
        norm_gain,
        in_gate,
        in_value,
        in_state,
        step_weight,
    )
    out_sum = after(out_sum, part)
    weights[0] = after(weights[0], out_sum)
    weights = [weights[0]] + [
        move_dp(after(weights[k], weights[0]), k, side, 0) for k in range(1, side)
    ]

    grad_sum = lax.psum_scatter(part, "tensor", scatter_dimension=0, tiled=True)

    got = swap_core(send)
    shares = at_place(
        chip_kernel,
        place,
        (keep, got),
        (1,),
        [in_vmem] * 2,
        [fixed(share, 2 * STATE)] * 4,
        [sds((share, 2 * STATE), bf16)] * 4,
    )
    tiles = share * 2 * STATE // (8 * LANES)
    share_tall = -(-tiles * 8 // dp // 16) * 16
    shares = at_place(
        partial(share_kernel, side),
        place,
        [shares[0]] + [move_z(shares[k], k) for k in (1, 2, 3)],
        (1,),
        [in_vmem] * 4,
        [fixed(side, share_tall, LANES)] * side,
        [sds((side, share_tall, LANES), bf16)] * side,
        [pltpu.VMEM((tiles, 8, LANES), f32)],
    )
    shares = [shares[0]] + [move_dp(shares[k], k, side, 0) for k in range(1, side)]

    count = small_rows(dp, channels)
    gains = features // LANES
    plain = 3 * channels
    weights = at_place(
        partial(line_sum_kernel, plain, 2 * (count + gains)),
        place,
        weights + shares,
        (1,),
        [in_vmem] * (2 * side),
        [fixed(tall, lanes)] * side,
        [sds((tall, lanes), bf16)] * side,
    )
    weights = [weights[0]] + [move_dp(weights[k], k, side, 1) for k in range(1, side)]
    grad_sum = lax.all_gather(after(grad_sum, weights[1]), "tensor", tiled=True)


    vmem = pltpu.CompilerParams(vmem_limit_bytes=SMALL_VMEM)
    weights = pl.pallas_call(
        partial(block_sum_kernel, plain, count, gains),
        in_specs=[in_vmem] * (side + 1),
        out_shape=sds((tall, lanes), bf16),
        compiler_params=vmem,
        cost_estimate=free,
    )(*weights, norm_gain_part)
    out_sum = lax.all_gather(after(out_sum, weights), "tensor", tiled=True)
    weights = [weights] + [move_dp(weights, k, side, 1) for k in range(1, side)]
    weights = at_place(
        line_kernel,
        place,
        weights,
        (1,),
        [in_vmem] * side,
        fixed(side, tall, lanes),
        sds((side, tall, lanes), bf16),
    )
    weights = [weights] + [move_dp(weights, k, side, 0) for k in range(1, side)]
    wide = LEN // 2
    wide_rows = by_rows(features, rows=wide)
    grad_tokens = pl.pallas_call(
        grad_kernel,
        grid=(LEN // wide,),
        in_specs=[wide_rows] * 3 + [whole(norm_gain)],
        out_specs=wide_rows,
        out_shape=sds((LEN, features), bf16),
        compiler_params=params,
        cost_estimate=free,
    )(grad_sum, tokens, cotangent, norm_gain)
    block_output = pl.pallas_call(
        partial(output_kernel, inner),
        grid=(LEN // wide,),
        in_specs=[wide_rows, wide_rows, pl.BlockSpec((8, wide), lambda i: (0, i))],
        out_specs=wide_rows,
        out_shape=sds((LEN, features), bf16),
        compiler_params=params,
        cost_estimate=free,
    )(after(out_sum, grad_tokens), tokens, stats)
    across = features // side // channels

    def unpack(steps_back, *operands):
        count = len(steps_back)
        shapes = [
            sds((features, channels), f32),
            sds((features, channels), f32),
            sds((channels, features), f32),
        ]
        return at_place(
            partial(unpack_kernel, side, steps_back),
            place,
            operands,
            (1,),
            [in_vmem] * count + [anywhere] * (len(operands) - count),
            [anywhere] * 3,
            shapes,
            [
                pltpu.VMEM((count * side, 3, tall, channels), f32),
                pltpu.SemaphoreType.DMA((count * side * (2 + across),)),
            ],
            {1 + count + i: i for i in range(len(operands) - count)},
        )

    unpacked = unpack([0], after(weights[0], grad_tokens))
    others = list(range(2, side))
    unpacked = unpack(others, *[weights[k] for k in others], *unpacked)
    weights[1] = after(weights[1], unpacked[0])

    smalls = [
        (heads, features),
        (1, heads),
        (1, heads),
        (1, heads),
        (CONV, channels),
        (channels,),
        (channels,),
    ]
    share_rows = share + 2 * SHARED
    *smalls, state = at_place(
        partial(small_kernel, heads, side, count, gains, channels),
        place,
        weights,
        (1,),
        [in_vmem] * side,
        [fixed(*shape) for shape in smalls] + [fixed(share_rows, 2 * STATE)],
        [sds(shape, f32) for shape in smalls] + [sds((share_rows, 2 * STATE), bf16)],
        [
            pltpu.VMEM((dp, count, LANES), f32),
            pltpu.VMEM((dp, gains, LANES), f32),
            pltpu.VMEM((tiles, 8, LANES), f32),
        ],
    )
    grad_in_step = smalls[0].T
    (
        grad_step_bias,
        grad_decay_log,
        grad_skip_gain,
        grad_conv_value_kernel,
        grad_conv_value_bias,
        grad_gate_gain,
    ) = (a[0] if a.shape[0] == 1 else a for a in smalls[1:])
    state = [state] + [move_z(state, k) for k in (1, 2, 3)]
    grad_in_value, grad_in_gate, grad_out_weight = unpack(
        [1], after(weights[1], state[0]), *unpacked
    )
    state[0] = after(state[0], grad_in_value, block_output)
    grad_in_state, grad_norm_gain, grad_conv_state_kernel, grad_conv_state_bias = at_place(
        partial(join_kernel, gains),
        place,
        state + [swap_core(piece) for piece in state],
        (1,),
        [in_vmem] * 8,
        [
            fixed(features, 2 * STATE),
            fixed(features),
            fixed(CONV, 2 * STATE),
            fixed(2 * STATE),
        ],
        [
            sds((features, 2 * STATE), f32),
            sds((features,), f32),
            sds((CONV, 2 * STATE), f32),
            sds((2 * STATE,), f32),
        ],
    )
    return (
        block_output,
        grad_tokens,
        grad_norm_gain,
        grad_in_gate,
        grad_in_value,
        grad_in_state,
        grad_in_step,
        grad_step_bias,
        grad_decay_log,
        grad_skip_gain,
        grad_conv_value_kernel,
        grad_conv_value_bias,
        grad_conv_state_kernel,
        grad_conv_state_bias,
        grad_gate_gain,
        grad_out_weight,
    )


def solution(mesh):
    placed = (
        P("dp", None),
        P(),
        P(None, "tensor"),
        P(None, "tensor"),
        P(),
        P(None, "tensor"),
        P("tensor"),
        P("tensor"),
        P("tensor"),
        P(None, "tensor"),
        P("tensor"),
        P(),
        P(),
        P("tensor"),
        P("tensor", None),
        P("dp", None),
    )
    return jax.shard_map(
        on_device,
        mesh=mesh,
        in_specs=placed,
        out_specs=(
            P("dp", None),
            P("dp", None),
            P(),
            P(None, "tensor"),
            P(None, "tensor"),
            P(),
            P(None, "tensor"),
            P("tensor"),
            P("tensor"),
            P("tensor"),
            P(None, "tensor"),
            P("tensor"),
            P(),
            P(),
            P("tensor"),
            P("tensor", None),
        ),
        check_vma=False,
    )
```

```python
import math
from functools import partial

import jax
import jax.numpy as jnp
from jax import lax
from jax.experimental import pallas as pl
from jax.experimental.pallas import tpu as pltpu
from jax.sharding import PartitionSpec as P

STATE = 128
CONV = 4
LEN = 1024
HEAD = 64
Q = 128
ROWS = 256
LANES = 128
HALO = 8
LOCAL = 32
SHARED = 16

epsilon = 1e-05
f32 = jnp.float32
bf16 = jnp.bfloat16
VMEM = 60 * 1024 * 1024
SMALL_VMEM = 40 * 1024 * 1024


def mm(a, b):
    return lax.dot_general(a, b, (((1,), (0,)), ((), ())), preferred_element_type=f32)


def parts_of(x):
    high = x.astype(bf16)
    rest = x - high.astype(f32)
    middle = rest.astype(bf16)
    return [high, middle, (rest - middle.astype(f32)).astype(bf16)]


def sum_rows(triangle, x):
    width = x.shape[1]
    total = mm(triangle, jnp.concatenate(parts_of(x), axis=1))
    return total[:, :width] + total[:, width : 2 * width] + total[:, 2 * width :]


def mm_nt(a, b):
    return lax.dot_general(a, b, (((1,), (1,)), ((), ())), preferred_element_type=f32)


def mm_tn(a, b):
    return lax.dot_general(a, b, (((0,), (0,)), ((), ())), preferred_element_type=f32)


def sigmoid(v):
    return 1.0 / (1.0 + jnp.exp(-v))


def softplus(v):
    return jnp.maximum(v, 0.0) + jnp.log1p(jnp.exp(-jnp.abs(v)))


def iota(shape, axis):
    return lax.broadcasted_iota(jnp.int32, shape, axis)


def column(m, at):
    return jnp.broadcast_to(m[:, at : at + 1], (m.shape[0], LANES))


def low_half(rows):
    return iota((rows, LANES), 1) < HEAD


def expand(m, heads):
    half = low_half(m.shape[0])
    return jnp.concatenate(
        [jnp.where(half, column(m, h), column(m, h + 1)) for h in range(0, heads, 2)], axis=1
    )


def split_heads(pair):
    half = low_half(pair.shape[0])
    zero = jnp.zeros_like(pair)
    return jnp.concatenate([jnp.where(half, pair, zero), jnp.where(half, zero, pair)], axis=0)


def head_sum(m, channels_to_heads):
    high = m.astype(bf16)
    low = (m - high.astype(f32)).astype(bf16)
    return mm(high, channels_to_heads) + mm(low, channels_to_heads)


def head_row(scalars, heads):
    lane = iota((1, LANES), 1)
    row = jnp.zeros((1, LANES), f32)
    for h in range(heads):
        row = jnp.where(lane == h, scalars[h], row)
    return row


def rate_row(decay_log, heads):
    return jnp.where(iota((1, LANES), 1) < heads, -jnp.exp(head_row(decay_log, heads)), 0.0)


def channel_row(scalars, heads):
    half = low_half(1)
    return jnp.concatenate(
        [jnp.where(half, scalars[h], scalars[h + 1]) for h in range(0, heads, 2)], axis=1
    )


def all_lanes(rows):
    below = jnp.zeros((LANES - rows.shape[0], rows.shape[1]), rows.dtype)
    return jnp.concatenate([rows, below], axis=0)


def row_of(ref):
    return ref[...].reshape(1, ref.shape[0])


def forward_kernel(
    heads,
    tokens,
    norm_gain,
    in_gate,
    in_value,
    in_state,
    in_step,
    step_bias,
    decay_log,
    skip_gain,
    value_kernel,
    value_bias,
    state_kernel,
    state_bias,
    gate_gain,
    out_weight,
    cotangent,
    normed_out,
    gate_out,
    value_out,
    value_conv_out,
    state_out,
    state_conv_out,
    step_out,
    mixed_out,
    back_out,
    part_out,
    memory_out,
    stats_out,
    value_buf,
    state_buf,
    memory,
):
    @pl.when(pl.program_id(0) == 0)
    def _():
        value_buf[0:HALO, :] = jnp.zeros((HALO, value_buf.shape[1]), f32)
        state_buf[0:HALO, :] = jnp.zeros((HALO, state_buf.shape[1]), f32)
        memory[...] = jnp.zeros_like(memory)

    x = tokens[...].astype(f32)
    inverse = lax.rsqrt(jnp.mean(x * x, axis=1, keepdims=True) + epsilon)
    normed = (x * inverse * row_of(norm_gain)).astype(bf16)
    normed_out[...] = normed
    state_pre = mm(normed, in_state[...])
    value_pre = mm(normed, in_value[...])
    step_pre = mm_nt(normed, all_lanes(in_step[...])) + head_row(step_bias, heads)
    gate_pre = mm(normed, in_gate[...])
    gate_out[...] = gate_pre
    value_out[...] = value_pre
    state_out[...] = state_pre
    step_out[...] = step_pre

    def conv(buf, pre, kernel, bias):
        buf[HALO:, :] = pre
        result = row_of(bias) + buf[HALO - 3 : HALO - 3 + ROWS, :] * kernel[0:1, :]
        for k in range(1, CONV):
            result = result + buf[HALO - 3 + k : HALO - 3 + k + ROWS, :] * kernel[k : k + 1, :]
        buf[0:HALO, :] = buf[ROWS : ROWS + HALO, :]
        return result

    value_conv = conv(value_buf, value_pre, value_kernel, value_bias)
    value_conv_out[...] = value_conv
    values = (value_conv * sigmoid(value_conv)).astype(bf16)
    state_conv = conv(state_buf, state_pre, state_kernel, state_bias)
    state_conv_out[...] = state_conv
    states = (state_conv * sigmoid(state_conv)).astype(bf16)
    step = softplus(step_pre)
    log_step = step * rate_row(decay_log, heads)
    skip = channel_row(skip_gain, heads)

    causal = iota((Q, Q), 0) >= iota((Q, Q), 1)
    tri = jnp.where(causal, 1.0, 0.0).astype(bf16)
    mixed_parts = []
    for part in range(ROWS // Q):
        rows = slice(part * Q, (part + 1) * Q)
        b = states[rows, :STATE]
        c = states[rows, STATE:]
        v = values[rows, :].astype(f32)
        dt = step[rows, :]
        decay = sum_rows(tri, log_step[rows, :])
        decay_t = decay.T
        wide = expand(decay, heads)
        dt_wide = expand(dt, heads)
        grown = jnp.exp(wide)
        scaled = v * dt_wide
        scaled_low = scaled.astype(bf16)
        cb = mm_nt(c, b)
        held = memory[...]
        held_low = held.astype(bf16)
        memory_out[part] = held_low
        y = mm(c, held_low) * grown + skip * v
        inside = []
        for h in range(0, heads, 2):
            blocks = []
            for at in (h, h + 1):
                gap = column(decay, at) - decay_t[at : at + 1, :]
                blocks.append((cb * jnp.exp(jnp.where(causal, gap, -1e30))).astype(bf16))
            pair = scaled_low[:, h * HEAD : (h + 2) * HEAD]
            inside.append(mm(jnp.concatenate(blocks, axis=1), split_heads(pair)))
        mixed_parts.append(y + jnp.concatenate(inside, axis=1))
        ended = (scaled * jnp.exp(wide[Q - 1 : Q, :] - wide)).astype(bf16)
        memory[...] = held * grown[Q - 1 : Q, :] + mm_tn(b, ended)

    mixed = jnp.concatenate(mixed_parts, axis=0)
    mixed_out[...] = mixed
    gated = mixed * gate_pre * sigmoid(gate_pre)
    back = mm_nt(cotangent[...], out_weight[...])
    back_out[...] = back
    gained = gated * row_of(gate_gain)
    part_out[...] = mm(gained.astype(bf16), out_weight[...]).astype(bf16)
    squares = jnp.sum(gated * gated, axis=1, keepdims=True)
    moment = jnp.sum(back * gained, axis=1, keepdims=True)
    lane = iota((ROWS, LANES), 1)
    both = jnp.where(lane == 0, squares, jnp.where(lane == 1, moment, 0.0))
    stats_out[...] = both.T[0:8, :]


def stats_columns(stats, inner):
    padded = jnp.concatenate([stats, jnp.zeros((LANES - 8, stats.shape[1]), f32)], axis=0).T
    scale = lax.rsqrt(padded[:, 0:1] / inner + epsilon)
    return scale, padded[:, 1:2] / inner


def add_row(ref, at, rows):
    ref[at : at + 1, :] += jnp.sum(rows, axis=0, keepdims=True)


def backward_kernel(
    heads,
    inner,
    steps,
    side,
    place,
    stats,
    normed,
    cotangent,
    gate,
    mixed_in,
    back_in,
    value,
    value_conv,
    state,
    state_conv,
    step_in,
    memory_in,
    gate_gain,
    decay_log,
    skip_gain,
    value_kernel,
    state_kernel,
    norm_gain,
    in_gate_at,
    in_value_at,
    in_state_at,
    in_step,
    part_out,
    norm_gain_out,
    keep_out,
    send_out,
    *refs,
):
    pieces_out = refs[:side]
    (
        value_buf,
        state_buf,
        adjoint,
        weight_total,
        out_total,
        step_total,
        gate_gain_out,
        value_taps_out,
        state_taps_out,
        skip_out,
        steps_out,
        local_rows,
        shared_rows,
        slabs,
        in_all,
        sems,
    ) = refs[side:]
    wide = in_gate_at.shape[1]
    weights = [
        pltpu.make_async_copy(source, target, sems.at[i])
        for i, (source, target) in enumerate(
            (
                (in_value_at, in_all.at[:, pl.ds(0, wide)]),
                (in_gate_at, in_all.at[:, pl.ds(wide, wide)]),
                (in_state_at, in_all.at[:, pl.ds(2 * wide, 2 * STATE)]),
            )
        )
    ]

    @pl.when(pl.program_id(0) == 0)
    def _():
        for copy in weights:
            copy.start()
        norm_gain_out[...] = jnp.zeros_like(norm_gain_out)
        value_buf[ROWS:, :] = jnp.zeros((HALO, value_buf.shape[1]), f32)
        state_buf[ROWS:, :] = jnp.zeros((HALO, state_buf.shape[1]), f32)
        adjoint[...] = jnp.zeros_like(adjoint)
        for ref in (
            weight_total,
            out_total,
            step_total,
            gate_gain_out,
            value_taps_out,
            state_taps_out,
            skip_out,
            steps_out,
        ):
            ref[...] = jnp.zeros_like(ref)

    scale, moment = stats_columns(stats[...], inner)
    mixed = mixed_in[...]
    back = back_in[...]
    pre = gate[...]
    bent = sigmoid(pre)
    silu = pre * bent
    gated = mixed * silu
    scaled = gated * scale
    gain = row_of(gate_gain)
    add_row(gate_gain_out, 0, back * scaled)
    grad_gated = scale * (back * gain) - scaled * (scale * scale * moment)
    grad_mixed = grad_gated * silu
    round_gate = (grad_gated * mixed * (bent * (1.0 + pre * (1.0 - bent)))).astype(bf16)
    outgoing = (scaled * gain).astype(bf16)
    width = out_total.shape[2]
    out_terms = mm_tn(outgoing, cotangent[...])
    for x in range(side):
        out_total[x] += out_terms[:, x * width : (x + 1) * width]

    value_at = value_conv[...]
    value_bent = sigmoid(value_at)
    values = (value_at * value_bent).astype(bf16)
    state_at = state_conv[...]
    state_bent = sigmoid(state_at)
    states = (state_at * state_bent).astype(bf16)
    step_pre = step_in[...]
    step = softplus(step_pre)
    rate = rate_row(decay_log, heads)
    skip = channel_row(skip_gain, heads)
    log_step = step * rate

    ahead = iota((Q, Q), 1) >= iota((Q, Q), 0)
    tri = jnp.where(iota((Q, Q), 0) >= iota((Q, Q), 1), 1.0, 0.0).astype(bf16)
    tri_both = jnp.concatenate(
        [
            jnp.where(ahead, 1.0, 0.0),
            jnp.where(iota((Q, Q), 0) > iota((Q, Q), 1), 1.0, 0.0),
        ],
        axis=1,
    ).astype(bf16)
    lane = iota((Q, LANES), 1)
    row8 = iota((8, Q), 0)
    channels = heads * HEAD
    to_heads = jnp.where(
        lax.shift_right_logical(iota((channels, LANES), 0), 6) == iota((channels, LANES), 1), 1.0, 0.0
    ).astype(bf16)
    parts = ROWS // Q
    grad_value_parts = [None] * parts
    grad_state_parts = [None] * parts
    grad_step_parts = [None] * parts
    for part in reversed(range(parts)):
        rows = slice(part * Q, (part + 1) * Q)
        b = states[rows, :STATE]
        c = states[rows, STATE:]
        v_low = values[rows, :]
        v = v_low.astype(f32)
        dt = step[rows, :]
        dy = grad_mixed[rows, :]
        dy_low = dy.astype(bf16)
        decay = sum_rows(tri, log_step[rows, :])
        decay_t = decay.T
        wide = expand(decay, heads)
        dt_wide = expand(dt, heads)
        grown = jnp.exp(wide)
        to_end = jnp.exp(wide[Q - 1 : Q, :] - wide)
        held = memory_in[part]
        later = adjoint[...]
        later_low = later.astype(bf16)
        bd = mm(b, later_low)
        cs = mm(c, held)
        bc = mm_nt(b, c)
        dy_grown = dy * grown
        dy_grown_low = dy_grown.astype(bf16)
        at_end = bd * to_end
        inside = []
        grad_bc = jnp.zeros((Q, Q), f32)
        direct = jnp.zeros((Q, LANES), f32)
        row_sums = jnp.zeros((8, Q), f32)
        for h in range(0, heads, 2):
            lanes = slice(h * HEAD, (h + 2) * HEAD)
            v_split = split_heads(v_low[:, lanes])
            grad_pair = mm_nt(v_split, dy_low[:, lanes])
            blocks = []
            for at in (h, h + 1):
                gap = decay_t[at : at + 1, :] - column(decay, at)
                fall = jnp.exp(jnp.where(ahead, gap, -1e30))
                grad_fall = grad_pair[(at - h) * Q : (at - h + 1) * Q, :] * fall
                direct += jnp.where(lane == at, jnp.sum(grad_fall * bc, axis=1, keepdims=True), 0.0)
                grad_one = grad_fall * column(dt, at)
                grad_bc += grad_one
                row_sums += jnp.where(
                    row8 == at, jnp.sum(grad_one * bc, axis=0, keepdims=True), 0.0
                )
                blocks.append((bc * fall).astype(bf16))
            inside.append(mm(jnp.concatenate(blocks, axis=1), split_heads(dy_low[:, lanes])))
        grad_value_parts[part] = dt_wide * (jnp.concatenate(inside, axis=1) + at_end) + skip * dy
        add_row(skip_out, 0, dy * v)
        grown_sum = head_sum(dy_grown * cs, to_heads)
        end_sum = head_sum(at_end * v, to_heads)
        constant = head_sum(
            grown[Q - 1 : Q, :] * jnp.sum(held.astype(f32) * later, axis=0, keepdims=True), to_heads
        )
        row_t = jnp.concatenate([row_sums, jnp.zeros((LANES - 8, Q), f32)], axis=0).T
        grad_log = (
            sum_rows(
                tri_both,
                jnp.concatenate([row_t - direct * dt + grown_sum, end_sum * dt], axis=0),
            )
            + constant
        )
        grad_step = direct + end_sum + rate * grad_log
        grad_step = grad_step * sigmoid(step_pre[rows, :])
        grad_step_parts[part] = grad_step
        add_row(steps_out, 0, grad_step)
        add_row(steps_out, 1, dt * grad_log * rate)
        grad_bc_low = grad_bc.astype(bf16)
        grad_b = mm(grad_bc_low, c) + mm_nt((v * dt_wide * to_end).astype(bf16), later_low)
        grad_c = mm_tn(grad_bc_low, b) + mm_nt(dy_grown_low, held)
        grad_state_parts[part] = jnp.concatenate([grad_b, grad_c], axis=1)
        adjoint[...] = later * grown[Q - 1 : Q, :] + mm_tn(c, dy_grown_low)

    def conv_back(buf, grad, at, bent, pre, kernel, taps_out):
        buf[0:ROWS, :] = grad * (bent * (1.0 + at * (1.0 - bent)))
        result = None
        for k in range(CONV):
            moved = buf[3 - k : 3 - k + ROWS, :]
            term = moved * kernel[k : k + 1, :]
            result = term if result is None else result + term
            add_row(taps_out, k, pre * moved)
        add_row(taps_out, CONV, buf[0:ROWS, :])
        buf[ROWS:, :] = buf[0:HALO, :]
        return result.astype(bf16)

    round_value = conv_back(
        value_buf,
        jnp.concatenate(grad_value_parts, axis=0),
        value_at,
        value_bent,
        value[...],
        value_kernel,
        value_taps_out,
    )
    round_state = conv_back(
        state_buf,
        jnp.concatenate(grad_state_parts, axis=0),
        state_at,
        state_bent,
        state[...],
        state_kernel,
        state_taps_out,
    )
    round_step = jnp.concatenate(grad_step_parts, axis=0).astype(bf16)

    @pl.when(pl.program_id(0) == 0)
    def _():
        for copy in weights:
            copy.wait()

    rounds = jnp.concatenate([round_value, round_gate, round_state], axis=1)
    total = mm_nt(rounds, in_all[...]) + mm(round_step, all_lanes(in_step[...]))
    part_out[...] = total.astype(bf16)
    add_row(norm_gain_out, 0, total * normed[...].astype(f32))
    weight_total[...] += mm_tn(normed[...], rounds)
    step_total[...] += mm_tn(round_step, normed[...])

    @pl.when(pl.program_id(0) == steps - 1)
    def _():
        norm_gain_out[...] = norm_gain_out[...] / row_of(norm_gain)
        fold = step_total.shape[1] // channels
        local_rows[...] = jnp.zeros_like(local_rows)
        for h in range(heads):
            for q in range(fold):
                local_rows[h * fold + q : h * fold + q + 1, :] = step_total[
                    h : h + 1, q * channels : (q + 1) * channels
                ]
        at = heads * fold
        local_rows[at : at + CONV + 1, :] = value_taps_out[0 : CONV + 1, :]
        at += CONV + 1
        local_rows[at : at + 1, :] = gate_gain_out[0:1, :]
        local_rows[at + 1 : at + 2, :] = jnp.concatenate(
            [steps_out[0:1, :], steps_out[1:2, :], head_sum(skip_out[...], to_heads)[0:1, :]],
            axis=1,
        )
        shared_rows[...] = jnp.zeros_like(shared_rows)
        shared_rows[0 : CONV + 1, :] = state_taps_out[0 : CONV + 1, :]

        _, tall, _ = pieces_out[0].shape
        count = small_rows(side**2, channels)
        slabs[...] = jnp.zeros_like(slabs)
        for d in range(side**2):
            at = 0
            for ref in (local_rows, shared_rows):
                each = ref.shape[0] // side**2
                for j in range(d * each, (d + 1) * each):
                    for lanes in range(0, ref.shape[1], LANES):
                        mine = ref[j : j + 1, lanes : lanes + LANES]
                        high = mine.astype(bf16).astype(f32)
                        slabs[d, at : at + 1, :] = high
                        slabs[d, count + at : count + at + 1, :] = mine - high
                        at += 1
        rows = channels // side
        for k, piece in enumerate(pieces_out):
            for j in range(side):
                y, x = block_of(place, lax.rem(place[3 + place[1]] + k, side), j)
                here = pl.ds(pl.multiple_of((y * side + x) * tall, tall), tall)
                piece[j, :, 0 : 2 * channels] = weight_total[here, 0 : 2 * channels].astype(bf16)
                for c in range(width // channels):
                    piece[j, c * rows : (c + 1) * rows, 2 * channels : 3 * channels] = out_total[
                        x,
                        pl.ds(pl.multiple_of(y * rows, rows), rows),
                        c * channels : (c + 1) * channels,
                    ].astype(bf16)
                piece[j, :, 3 * channels :] = slabs[y * side + x].astype(bf16)

        upper = place[1] == 0
        tall = keep_out.shape[1]
        for z in range(4):
            even = weight_total[2 * z * tall : (2 * z + 1) * tall, 2 * channels :].astype(bf16)
            odd = weight_total[(2 * z + 1) * tall : (2 * z + 2) * tall, 2 * channels :].astype(
                bf16
            )
            keep_out[z] = jnp.where(upper, even, odd)
            send_out[z] = jnp.where(upper, odd, even)


def block_of(place, first, second):
    core = place[1]
    return first + core * (second - first), second + core * (first - second)


def small_rows(pieces, channels):
    return (LOCAL * channels + SHARED * 2 * STATE) // LANES // pieces


def line_kernel(place, *refs):
    *pieces, out = refs
    side = len(pieces)
    for k, piece in enumerate(pieces):
        out[lax.rem(place[4 - place[1]] + side - k, side)] = piece[...]


def chip_kernel(place, keep, got, *outs):
    for k, out in enumerate(outs):
        z = lax.rem(place[0] + k, 4)
        out[...] = (keep[z].astype(f32) + got[z].astype(f32)).astype(bf16)


def tile_at(t):
    rows, lanes = 8 * (t // 2), LANES * (t % 2)
    return slice(rows, rows + 8), slice(lanes, lanes + LANES)


def share_kernel(side, place, own, one, two, three, *refs):
    outs, tiles = refs[:-1], refs[-1]
    total = total_of((own, one, two, three))
    count = tiles.shape[0]
    for t in range(count):
        tiles[t] = total[tile_at(t)]
    each = count // side**2
    for k, out in enumerate(outs):
        for j in range(side):
            y, x = block_of(place, lax.rem(place[3 + place[1]] + k, side), j)
            slab = [tiles[(y * side + x) * each + i] for i in range(each)]
            below = out.shape[1] - 8 * each
            out[j] = jnp.concatenate(slab + [jnp.zeros((below, LANES), f32)], axis=0).astype(bf16)


def total_of(pieces):
    total = pieces[0][...].astype(f32)
    for piece in pieces[1:]:
        total = total + piece[...].astype(f32)
    return total


def line_sum_kernel(plain, at, place, *refs):
    side = len(refs) // 3
    pieces, shares, outs = refs[:side], refs[side : 2 * side], refs[2 * side :]
    tall = shares[0].shape[1]
    for k, out in enumerate(outs):
        j = lax.rem(place[4 - place[1]] + k, side)
        total = total_of([ref.at[j] for ref in pieces])
        share = total_of([ref.at[j] for ref in shares])
        out[:, :plain] = total[:, :plain].astype(bf16)
        out[:, plain:] = jnp.concatenate(
            [total[:at, plain:], share, total[at + tall :, plain:]], axis=0
        ).astype(bf16)


def block_sum_kernel(plain, count, gains, *refs):
    *pieces, norm_gain, out = refs
    total = total_of(pieces)
    out[:, :plain] = total[:, :plain].astype(bf16)
    small = total[:count, plain:] + total[count : 2 * count, plain:]
    gain = jnp.concatenate(
        [norm_gain[0:1, j * LANES : (j + 1) * LANES] for j in range(gains)], axis=0
    )
    at = 2 * (count + gains)
    out[:, plain:] = jnp.concatenate(
        high_and_low(small) + high_and_low(gain) + [total[at:, plain:]], axis=0
    ).astype(bf16)


def high_and_low(rows):
    high = rows.astype(bf16).astype(f32)
    return [high, rows - high]


def unpack_kernel(side, steps_back, place, *refs):
    pieces = refs[: len(steps_back)]
    value_out, gate_out, out_out, wide, sems = refs[-5:]
    _, _, tall, channels = wide.shape
    rows, width = out_out.shape[0] // side, out_out.shape[1] // side
    copies = []

    def send(source, target):
        copies.append(pltpu.make_async_copy(source, target, sems.at[len(copies)]))
        copies[-1].start()

    for k, piece in enumerate(pieces):
        first = lax.rem(place[3 + place[1]] + side - steps_back[k], side)
        for j in range(side):
            y, x = block_of(place, first, j)
            at = k * side + j
            here = pl.ds(pl.multiple_of((y * side + x) * tall, tall), tall)
            for c in range(3):
                wide[at, c] = piece[j, :, c * channels : (c + 1) * channels].astype(f32)
            send(wide.at[at, 0], value_out.at[here])
            send(wide.at[at, 1], gate_out.at[here])
            for c in range(width // channels):
                send(
                    wide.at[at, 2, pl.ds(c * rows, rows)],
                    out_out.at[
                        pl.ds(pl.multiple_of(y * rows, rows), rows),
                        pl.ds(pl.multiple_of(x * width + c * channels, channels), channels),
                    ],
                )
    for copy in copies:
        copy.wait()


def small_kernel(heads, side, count, gains, channels, place, *refs):
    pieces = refs[:side]
    (
        step_out,
        step_bias_out,
        decay_out,
        skip_out,
        value_taps_out,
        value_bias_out,
        gate_gain_out,
        share_out,
        small_at,
        gain_at,
        tiles,
    ) = refs[side:]
    each = tiles.shape[0] // side**2
    for k, piece in enumerate(pieces):
        first = lax.rem(place[3 + place[1]] + side - k, side)
        for j in range(side):
            y, x = block_of(place, first, j)
            d = y * side + x
            tile = piece[j, :, piece.shape[2] - LANES :].astype(f32)
            small_at[d] = tile[:count, :] + tile[count : 2 * count, :]
            at = 2 * count
            gain_at[d] = tile[at : at + gains, :] + tile[at + gains : at + 2 * gains, :]
            at += 2 * gains
            for i in range(each):
                tiles[d * each + i] = tile[at + 8 * i : at + 8 * (i + 1), :]
    fold, across = step_out.shape[1] // channels, channels // LANES
    own, ours = LOCAL // side**2, SHARED // side**2

    def local(row, tile):
        at = row % own * across + tile
        return small_at[row // own, at : at + 1, :]

    def shared(row, tile):
        at = own * across + row % ours * (2 * STATE // LANES) + tile
        return small_at[row // ours, at : at + 1, :]

    for h in range(heads):
        for q in range(fold):
            for t in range(across):
                at = q * channels + t * LANES
                step_out[h : h + 1, at : at + LANES] = local(h * fold + q, t)
    row = heads * fold
    for t in range(across):
        lanes = slice(t * LANES, (t + 1) * LANES)
        for k in range(CONV):
            value_taps_out[k : k + 1, lanes] = local(row + k, t)
        value_bias_out[lanes] = local(row + CONV, t)[0]
        gate_gain_out[lanes] = local(row + CONV + 1, t)[0]
    for t, out in enumerate((step_bias_out, decay_out, skip_out)):
        out[...] = local(row + CONV + 2, t)[:, :heads]

    gain = gain_at[0]
    for d in range(1, side**2):
        gain = gain + gain_at[d]
    rows = [gain[t : t + 1, :] for t in range(gains)]
    rows += [shared(k, t) for k in range(CONV + 1) for t in range(2 * STATE // LANES)]
    pairs = jnp.concatenate(
        [jnp.concatenate(rows[i : i + 2], axis=1) for i in range(0, len(rows), 2)], axis=0
    )
    below = jnp.zeros((SHARED - pairs.shape[0], 2 * STATE), f32)
    share = jnp.concatenate(
        [
            jnp.concatenate([tiles[t], tiles[t + 1]], axis=1)
            for t in range(0, tiles.shape[0], 2)
        ]
        + [jnp.concatenate([part, below], axis=0) for part in high_and_low(pairs)],
        axis=0,
    )
    share_out[...] = share.astype(bf16)


def join_kernel(gains, place, *refs):
    mine, other = refs[:4], refs[4:8]
    state_out, norm_gain_out, taps_out, bias_out = refs[8:]
    tall = state_out.shape[0] // 8
    sums = []
    for k in range(4):
        z = lax.rem(place[0] + 4 - k, 4)
        small = []
        for piece, core in ((mine[k], place[1]), (other[k], 1 - place[1])):
            here = pl.ds(pl.multiple_of((2 * z + core) * tall, tall), tall)
            state_out[here, :] = piece[:tall, :].astype(f32)
            small.append(
                piece[tall : tall + SHARED, :].astype(f32) + piece[tall + SHARED :, :].astype(f32)
            )
        sums.append(small[0] + small[1])
    total = (sums[0] + sums[2]) + (sums[1] + sums[3])
    wide = total.shape[1]
    for t in range(gains * LANES // wide):
        norm_gain_out[t * wide : (t + 1) * wide] = total[t]
    at = gains * LANES // wide
    taps_out[...] = total[at : at + CONV, :]
    bias_out[...] = total[at + CONV]


def output_kernel(inner, total, tokens, stats, out):
    scale, _ = stats_columns(stats[...], inner)
    terms = total[...].astype(f32).reshape(tokens.shape)
    out[...] = (tokens[...].astype(f32) + scale * terms).astype(bf16)


def grad_kernel(total, tokens, cotangent, norm_gain, out):
    x = tokens[...].astype(f32)
    inverse = lax.rsqrt(jnp.mean(x * x, axis=1, keepdims=True) + epsilon)
    scaled = total[...].astype(f32).reshape(tokens.shape) * row_of(norm_gain)
    moment = jnp.mean(scaled * x, axis=1, keepdims=True)
    grad = inverse * scaled - x * (inverse * inverse * inverse * moment)
    out[...] = (cotangent[...].astype(f32) + grad).astype(bf16)


def whole(array):
    zeros = (0,) * array.ndim
    return pl.BlockSpec(array.shape, lambda i: zeros)


def in_scalars():
    return pl.BlockSpec(memory_space=pltpu.SMEM)


def by_rows(width, steps=None, rows=ROWS):
    if steps is None:
        return pl.BlockSpec((rows, width), lambda i: (i, 0))
    return pl.BlockSpec((rows, width), lambda i: (steps - 1 - i, 0))


def swap_core(x):
    return lax.ppermute(x, "tensor", [(i, i ^ 1) for i in range(8)])


def move_z(x, k):
    return lax.ppermute(x, "tensor", [(i, (i + 2 * k) % 8) for i in range(8)])


def move_dp(x, k, side, stage):
    pairs = []
    for y in range(side):
        for x_at in range(side):
            for t in range(8):
                if (t + stage) % 2 == 0:
                    to = (y + k) % side * side + x_at
                else:
                    to = y * side + (x_at + k) % side
                pairs.append(((y * side + x_at) * 8 + t, to * 8 + t))
    return lax.ppermute(x, ("dp", "tensor"), pairs)


def after(x, *others):
    return lax.optimization_barrier((x,) + others)[0]


free = pl.CostEstimate(flops=0, bytes_accessed=0, transcendentals=0)


def at_place(
    kernel, place, operands, grid, in_specs, out_specs, out_shape, scratch=(), aliases=None
):
    return pl.pallas_call(
        kernel,
        grid_spec=pltpu.PrefetchScalarGridSpec(
            num_scalar_prefetch=1,
            grid=grid,
            in_specs=in_specs,
            out_specs=out_specs,
            scratch_shapes=scratch,
        ),
        out_shape=out_shape,
        compiler_params=pltpu.CompilerParams(
            dimension_semantics=("arbitrary",) * len(grid), vmem_limit_bytes=SMALL_VMEM
        ),
        input_output_aliases=aliases or {},
        cost_estimate=free,
    )(place, *operands)


in_vmem = pl.BlockSpec(memory_space=pltpu.VMEM)


def fixed(*shape):
    return pl.BlockSpec(shape, lambda *_: (0,) * len(shape))


def on_device(
    tokens,
    norm_gain,
    in_gate,
    in_value,
    in_state,
    in_step,
    step_bias,
    decay_log,
    skip_gain,
    conv_value_kernel,
    conv_value_bias,
    conv_state_kernel,
    conv_state_bias,
    gate_gain,
    out_weight,
    cotangent,
):
    features = tokens.shape[1]
    channels = in_gate.shape[1]
    heads = step_bias.shape[0]
    inner = channels * lax.axis_size("tensor")
    steps = LEN // ROWS
    parts = ROWS // Q
    dp = lax.axis_size("dp")
    side = math.isqrt(dp)
    me = lax.axis_index("tensor")
    row = lax.axis_index("dp")
    place = jnp.stack([me // 2, me % 2, me, row // side, row % side]).astype(jnp.int32)

    step_weight = in_step.T
    sds = jax.ShapeDtypeStruct
    params = pltpu.CompilerParams(
        dimension_semantics=("arbitrary",), vmem_limit_bytes=VMEM
    )
    stats_rows = pl.BlockSpec((8, ROWS), lambda i: (0, i))
    memory_rows = lambda at: pl.BlockSpec((parts, STATE, channels), lambda i: (at(i), 0, 0))

    (
        normed,
        gate_pre,
        value_pre,
        value_conv,
        state_pre,
        state_conv,
        step_pre,
        mixed,
        back,
        part,
        memories,
        stats,
    ) = pl.pallas_call(
        partial(forward_kernel, heads),
        grid=(steps,),
        in_specs=[
            by_rows(features),
            whole(norm_gain),
            whole(in_gate),
            whole(in_value),
            whole(in_state),
            whole(step_weight),
            in_scalars(),
            in_scalars(),
            in_scalars(),
            whole(conv_value_kernel),
            whole(conv_value_bias),
            whole(conv_state_kernel),
            whole(conv_state_bias),
            whole(gate_gain),
            whole(out_weight),
            by_rows(features),
        ],
        out_specs=[
            by_rows(features),
            by_rows(channels),
            by_rows(channels),
            by_rows(channels),
            by_rows(2 * STATE),
            by_rows(2 * STATE),
            by_rows(LANES),
            by_rows(channels),
            by_rows(channels),
            by_rows(features),
            memory_rows(lambda i: i),
            stats_rows,
        ],
        out_shape=[
            sds((LEN, features), bf16),
            sds((LEN, channels), f32),
            sds((LEN, channels), f32),
            sds((LEN, channels), f32),
            sds((LEN, 2 * STATE), f32),
            sds((LEN, 2 * STATE), f32),
            sds((LEN, LANES), f32),
            sds((LEN, channels), f32),
            sds((LEN, channels), f32),
            sds((LEN, features), bf16),
            sds((LEN // Q, STATE, channels), bf16),
            sds((8, LEN), f32),
        ],
        scratch_shapes=[
            pltpu.VMEM((ROWS + HALO, channels), f32),
            pltpu.VMEM((ROWS + HALO, 2 * STATE), f32),
            pltpu.VMEM((STATE, channels), f32),
        ],
        compiler_params=params,
        cost_estimate=free,
    )(
        tokens,
        norm_gain,
        in_gate,
        in_value,
        in_state,
        step_weight,
        step_bias,
        decay_log,
        skip_gain,
        conv_value_kernel,
        conv_value_bias,
        conv_state_kernel,
        conv_state_bias,
        gate_gain,
        out_weight,
        cotangent,
    )

    out_sum = lax.psum_scatter(part, "tensor", scatter_dimension=0, tiled=True)
    stats = stats + swap_core(stats)
    moved = [move_z(stats, k) for k in (1, 2, 3)]
    stats = (stats + moved[1]) + (moved[0] + moved[2])

    back_rows = partial(by_rows, steps=steps)
    anywhere = pl.BlockSpec(memory_space=pl.ANY)
    lanes = 3 * channels + LANES
    share = features // 8
    tall = features // dp
    part, norm_gain_part, keep, send, *weights = pl.pallas_call(
        partial(backward_kernel, heads, inner, steps, side),
        grid=(steps,),
        in_specs=[
            in_scalars(),
            pl.BlockSpec((8, ROWS), lambda i: (0, steps - 1 - i)),
            back_rows(features),
            back_rows(features),
            back_rows(channels),
            back_rows(channels),
            back_rows(channels),
            back_rows(channels),
            back_rows(channels),
            back_rows(2 * STATE),
            back_rows(2 * STATE),
            back_rows(LANES),
            memory_rows(lambda i: steps - 1 - i),
            whole(gate_gain),
            in_scalars(),
            in_scalars(),
            whole(conv_value_kernel),
            whole(conv_state_kernel),
            whole(norm_gain),
            anywhere,
            anywhere,
            anywhere,
            whole(step_weight),
        ],
        out_specs=[
            back_rows(features),
            fixed(8, features),
            fixed(4, share, 2 * STATE),
            fixed(4, share, 2 * STATE),
        ]
        + [fixed(side, tall, lanes)] * side,
        out_shape=[
            sds((LEN, features), bf16),
            sds((8, features), f32),
            sds((4, share, 2 * STATE), bf16),
            sds((4, share, 2 * STATE), bf16),
        ]
        + [sds((side, tall, lanes), bf16)] * side,
        scratch_shapes=[
            pltpu.VMEM((ROWS + HALO, channels), f32),
            pltpu.VMEM((ROWS + HALO, 2 * STATE), f32),
            pltpu.VMEM((STATE, channels), f32),
            pltpu.VMEM((features, 2 * channels + 2 * STATE), f32),
            pltpu.VMEM((side, channels, features // side), f32),
            pltpu.VMEM((LANES, features), f32),
            pltpu.VMEM((8, channels), f32),
            pltpu.VMEM((8, channels), f32),
            pltpu.VMEM((8, 2 * STATE), f32),
            pltpu.VMEM((8, channels), f32),
            pltpu.VMEM((8, LANES), f32),
            pltpu.VMEM((LOCAL, channels), f32),
            pltpu.VMEM((SHARED, 2 * STATE), f32),
            pltpu.VMEM((dp, tall, LANES), f32),
            pltpu.VMEM((features, 2 * channels + 2 * STATE), bf16),
            pltpu.SemaphoreType.DMA((3,)),
        ],
        compiler_params=params,
        cost_estimate=free,
    )(
        place,
        stats,
        normed,
        cotangent,
        gate_pre,
        mixed,
        back,
        value_pre,
        value_conv,
        state_pre,
        state_conv,
        step_pre,
        memories,
        gate_gain,
        decay_log,
        skip_gain,
        conv_value_kernel,
        conv_state_kernel,
        norm_gain,
        in_gate,
        in_value,
        in_state,
        step_weight,
    )
    out_sum = after(out_sum, part)
    weights[0] = after(weights[0], out_sum)
    weights = [weights[0]] + [
        move_dp(after(weights[k], weights[0]), k, side, 0) for k in range(1, side)
    ]

    grad_sum = lax.psum_scatter(part, "tensor", scatter_dimension=0, tiled=True)

    got = swap_core(send)
    shares = at_place(
        chip_kernel,
        place,
        (keep, got),
        (1,),
        [in_vmem] * 2,
        [fixed(share, 2 * STATE)] * 4,
        [sds((share, 2 * STATE), bf16)] * 4,
    )
    tiles = share * 2 * STATE // (8 * LANES)
    share_tall = -(-tiles * 8 // dp // 16) * 16
    shares = at_place(
        partial(share_kernel, side),
        place,
        [shares[0]] + [move_z(shares[k], k) for k in (1, 2, 3)],
        (1,),
        [in_vmem] * 4,
        [fixed(side, share_tall, LANES)] * side,
        [sds((side, share_tall, LANES), bf16)] * side,
        [pltpu.VMEM((tiles, 8, LANES), f32)],
    )
    shares = [shares[0]] + [move_dp(shares[k], k, side, 0) for k in range(1, side)]

    count = small_rows(dp, channels)
    gains = features // LANES
    plain = 3 * channels
    weights = at_place(
        partial(line_sum_kernel, plain, 2 * (count + gains)),
        place,
        weights + shares,
        (1,),
        [in_vmem] * (2 * side),
        [fixed(tall, lanes)] * side,
        [sds((tall, lanes), bf16)] * side,
    )
    weights = [weights[0]] + [move_dp(weights[k], k, side, 1) for k in range(1, side)]


    vmem = pltpu.CompilerParams(vmem_limit_bytes=SMALL_VMEM)
    weights = pl.pallas_call(
        partial(block_sum_kernel, plain, count, gains),
        in_specs=[in_vmem] * (side + 1),
        out_shape=sds((tall, lanes), bf16),
        compiler_params=vmem,
        cost_estimate=free,
    )(*weights, norm_gain_part)
    sums = lax.all_gather(
        jnp.concatenate([after(grad_sum, weights), out_sum], axis=0), "tensor"
    )
    weights = [weights] + [move_dp(weights, k, side, 1) for k in range(1, side)]
    weights = at_place(
        line_kernel,
        place,
        weights,
        (1,),
        [in_vmem] * side,
        fixed(side, tall, lanes),
        sds((side, tall, lanes), bf16),
    )
    weights = [weights] + [move_dp(weights, k, side, 0) for k in range(1, side)]
    wide = LEN // 2
    wide_rows = by_rows(features, rows=wide)
    sum_rows_at = lambda which: pl.BlockSpec(
        (wide * 8 // LEN, LEN // 8, features), lambda i: (i, which, 0)
    )
    grad_tokens = pl.pallas_call(
        grad_kernel,
        grid=(LEN // wide,),
        in_specs=[sum_rows_at(0), wide_rows, wide_rows, whole(norm_gain)],
        out_specs=wide_rows,
        out_shape=sds((LEN, features), bf16),
        compiler_params=params,
        cost_estimate=free,
    )(sums, tokens, cotangent, norm_gain)
    block_output = pl.pallas_call(
        partial(output_kernel, inner),
        grid=(LEN // wide,),
        in_specs=[sum_rows_at(1), wide_rows, pl.BlockSpec((8, wide), lambda i: (0, i))],
        out_specs=wide_rows,
        out_shape=sds((LEN, features), bf16),
        compiler_params=params,
        cost_estimate=free,
    )(after(sums, grad_tokens), tokens, stats)
    across = features // side // channels

    def unpack(steps_back, *operands):
        count = len(steps_back)
        shapes = [
            sds((features, channels), f32),
            sds((features, channels), f32),
            sds((channels, features), f32),
        ]
        return at_place(
            partial(unpack_kernel, side, steps_back),
            place,
            operands,
            (1,),
            [in_vmem] * count + [anywhere] * (len(operands) - count),
            [anywhere] * 3,
            shapes,
            [
                pltpu.VMEM((count * side, 3, tall, channels), f32),
                pltpu.SemaphoreType.DMA((count * side * (2 + across),)),
            ],
            {1 + count + i: i for i in range(len(operands) - count)},
        )

    unpacked = unpack([0], weights[0])
    others = list(range(2, side))
    unpacked = unpack(others, *[weights[k] for k in others], *unpacked)
    weights[1] = after(weights[1], unpacked[0])

    smalls = [
        (heads, features),
        (1, heads),
        (1, heads),
        (1, heads),
        (CONV, channels),
        (channels,),
        (channels,),
    ]
    share_rows = share + 2 * SHARED
    *smalls, state = at_place(
        partial(small_kernel, heads, side, count, gains, channels),
        place,
        weights,
        (1,),
        [in_vmem] * side,
        [fixed(*shape) for shape in smalls] + [fixed(share_rows, 2 * STATE)],
        [sds(shape, f32) for shape in smalls] + [sds((share_rows, 2 * STATE), bf16)],
        [
            pltpu.VMEM((dp, count, LANES), f32),
            pltpu.VMEM((dp, gains, LANES), f32),
            pltpu.VMEM((tiles, 8, LANES), f32),
        ],
    )
    grad_in_step = smalls[0].T
    (
        grad_step_bias,
        grad_decay_log,
        grad_skip_gain,
        grad_conv_value_kernel,
        grad_conv_value_bias,
        grad_gate_gain,
    ) = (a[0] if a.shape[0] == 1 else a for a in smalls[1:])
    state = [state] + [move_z(state, k) for k in (1, 2, 3)]
    grad_in_value, grad_in_gate, grad_out_weight = unpack(
        [1], after(weights[1], state[0]), *unpacked
    )
    state[0] = after(state[0], grad_in_value, block_output)
    grad_in_state, grad_norm_gain, grad_conv_state_kernel, grad_conv_state_bias = at_place(
        partial(join_kernel, gains),
        place,
        state + [swap_core(piece) for piece in state],
        (1,),
        [in_vmem] * 8,
        [
            fixed(features, 2 * STATE),
            fixed(features),
            fixed(CONV, 2 * STATE),
            fixed(2 * STATE),
        ],
        [
            sds((features, 2 * STATE), f32),
            sds((features,), f32),
            sds((CONV, 2 * STATE), f32),
            sds((2 * STATE,), f32),
        ],
    )
    return (
        block_output,
        grad_tokens,
        grad_norm_gain,
        grad_in_gate,
        grad_in_value,
        grad_in_state,
        grad_in_step,
        grad_step_bias,
        grad_decay_log,
        grad_skip_gain,
        grad_conv_value_kernel,
        grad_conv_value_bias,
        grad_conv_state_kernel,
        grad_conv_state_bias,
        grad_gate_gain,
        grad_out_weight,
    )


def solution(mesh):
    placed = (
        P("dp", None),
        P(),
        P(None, "tensor"),
        P(None, "tensor"),
        P(),
        P(None, "tensor"),
        P("tensor"),
        P("tensor"),
        P("tensor"),
        P(None, "tensor"),
        P("tensor"),
        P(),
        P(),
        P("tensor"),
        P("tensor", None),
        P("dp", None),
    )
    return jax.shard_map(
        on_device,
        mesh=mesh,
        in_specs=placed,
        out_specs=(
            P("dp", None),
            P("dp", None),
            P(),
            P(None, "tensor"),
            P(None, "tensor"),
            P(),
            P(None, "tensor"),
            P("tensor"),
            P("tensor"),
            P("tensor"),
            P(None, "tensor"),
            P("tensor"),
            P(),
            P(),
            P("tensor"),
            P("tensor", None),
        ),
        check_vma=False,
    )
```
